128 devices in a mesh: batch: 4 (over z), seq: 32 (over x, y, core).
Axes of the slice: x: 4, y: 4, z: 4, core: 2. Of those that a mesh axis runs over, the one named last changes fastest.
Arguments:
- tokens: bfloat16 [8, 2048, 2048], P('batch', 'seq'), may hold values from -6 to 6
- time_weights: bfloat16 [5, 2048, 2048], P(None, ('batch', 'seq')), may hold values from -0.125 to 0.125
- channel_key: bfloat16 [2048, 7168], P(('batch', 'seq')), may hold values from -0.125 to 0.125
- channel_value: bfloat16 [2048, 7168], P(('batch', 'seq')), may hold values from -0.0625 to 0.0625
- channel_gate: bfloat16 [2048, 2048], P(('batch', 'seq')), may hold values from -0.125 to 0.125
- vectors: bfloat16 [13, 2048], P(None, ('batch', 'seq')), may hold values from -1 to 1.5
- head_decay: float32 [32], replicated, may hold values from 0.9 to 1
- lengths: int32 [8], P('batch'), may hold values from 512 to 2048, as said below
- cotangent: bfloat16 [8, 2048, 2048], P('batch', 'seq'), may hold values from -6 to 6
Outputs:
- layer_out: bfloat16 [8, 2048, 2048], P('batch', 'seq')
- token_grad: bfloat16 [8, 2048, 2048], P('batch', 'seq')
- time_grads: float32 [5, 2048, 2048], P(None, ('batch', 'seq'))
- key_grad: float32 [2048, 7168], P(('batch', 'seq'))
- value_grad: float32 [2048, 7168], P(('batch', 'seq'))
- gate_grad: float32 [2048, 2048], P(('batch', 'seq'))
- vector_grads: float32 [13, 2048], P(None, ('batch', 'seq'))
The draws below stay inside these ranges and needn't reach their ends.
Inputs may be any that keep to these rules, and one draw needn't show every extreme that they name: `lengths`: in each batch group of 2 sequences one, chosen by the seed, has length 2048.
All inputs are finite; a program needn't handle non-finite values.
Results may differ from the reference program's by a relative error of at most 0.02.
Values may be sent and summed in bfloat16 or wider, within the bound.
A program may use at most 640 MiB of HBM per device.

```python
import jax
import jax.numpy as jnp
from jax import lax

D = 2048
FF = 7168
HEADS = 32
BLOCK_LEN = 64
SEQ_GRP = 2
LEN = 2048
NSEQ = 8


def draw_lengths(key, part):
    key = jax.random.fold_in(key, 11)
    length_key, choose_key = jax.random.split(key)
    group_count = NSEQ // SEQ_GRP
    drawn = jax.random.randint(length_key, (group_count, SEQ_GRP), LEN // 4, LEN + 1)
    chosen = jax.random.randint(choose_key, (group_count, 1), 0, SEQ_GRP)
    full_slot = jnp.arange(SEQ_GRP)[None, :] == chosen
    return jnp.where(full_slot, LEN, drawn).reshape(NSEQ).astype(jnp.int32)


def draw_head_decay(key, part):
    key = jax.random.fold_in(key, 12)
    order_key, quick_key, slow_key = jax.random.split(key, 3)
    ranking = jax.random.permutation(order_key, HEADS)
    quick_count = HEADS // 2
    quick_rate = jax.random.uniform(quick_key, (HEADS,), jnp.float32, 2.0, 4.0) / 40.0
    slow_rate = jax.random.uniform(slow_key, (HEADS,), jnp.float32, 0.2, 1.5) / LEN
    return jnp.exp(-jnp.where(ranking < quick_count, quick_rate, slow_rate))


def draw_vectors(key, part):
    key = jax.random.fold_in(key, 13)
    low_ends = jnp.array([0.5, -0.5, 0.05, 0.05, 0.05, 0.05, -1.0, 0.5, -0.5, 0.5, -0.5, 0.05, 0.05], jnp.float32)
    high_ends = jnp.array([1.5, 0.5, 0.95, 0.95, 0.95, 0.95, 1.0, 1.5, 0.5, 1.5, 0.5, 0.95, 0.95], jnp.float32)
    fraction = jax.random.uniform(key, (13, D), jnp.float32)
    return (low_ends[:, None] + (high_ends - low_ends)[:, None] * fraction).astype(jnp.bfloat16)


def levels(stream_key, extent, cuts, least, largest):
    def one(position, blocks):
        steps = jax.random.uniform(jax.random.fold_in(jax.random.fold_in(stream_key, 6), position), (blocks,), jnp.float32, least / len(cuts), largest / len(cuts))
        return jnp.repeat(jnp.exp(steps), extent[position] // blocks).reshape((-1,) + (1,) * (len(extent) - position - 1))

    loudness = one(*cuts[0])
    for cut in cuts[1:]:
        loudness = loudness * one(*cut)
    return loudness


def noise(stream_key, dims, scale, bound, cuts=(), held_as=jnp.bfloat16):
    level = levels(stream_key, dims, cuts, -0.22, 0.18) if cuts else 1.0
    values = jax.random.normal(stream_key, dims, jnp.float32) * scale * level
    return jnp.minimum(jnp.maximum(values, -bound), bound).astype(held_as)


def setup_inputs(seed: int = 0) -> dict:
    arg_keys = jax.random.split(jax.random.key(seed), 10)
    return {
        "tokens": noise(arg_keys[0], (NSEQ, LEN, D), 1.0, 6.0, ((0, 4), (1, 32))),
        "time_weights": noise(arg_keys[1], (5, D, D), D ** -0.5, 0.125, ((1, 128),)),
        "channel_key": noise(arg_keys[2], (D, FF), D ** -0.5, 0.125, ((0, 128),)),
        "channel_value": noise(arg_keys[3], (D, FF), FF ** -0.5, 0.0625, ((0, 128),)),
        "channel_gate": noise(arg_keys[4], (D, D), D ** -0.5, 0.125, ((0, 128),)),
        "vectors": draw_vectors(jax.random.fold_in(arg_keys[9], 71), 0),
        "head_decay": draw_head_decay(jax.random.fold_in(arg_keys[9], 71), 0),
        "lengths": draw_lengths(jax.random.fold_in(arg_keys[9], 71), 0),
        "cotangent": noise(arg_keys[8], (NSEQ, LEN, D), 1.0, 6.0, ((0, 4), (1, 32))),
    }


epsilon = 1e-05
group_epsilon = 0.00064
highest = lax.Precision.HIGHEST

@jax.custom_vjp
def low(v):
    return lax.optimization_barrier(v.astype(jnp.bfloat16)).astype(jnp.float32)

@jax.custom_vjp
def low_back(v):
    return v

def low_keep(v):
    return (low(v), None)

def low_pass(kept, grad):
    return (grad,)

def back_keep(v):
    return (v, None)

def back_low(kept, grad):
    return (low(grad),)
low.defvjp(low_keep, low_pass)
low_back.defvjp(back_keep, back_low)

def layer_norm(values, gain_row, offset):
    center = values - lax.optimization_barrier(jnp.mean(values, axis=-1, keepdims=True))
    scaled = center * lax.rsqrt(lax.optimization_barrier(jnp.mean(center * center, axis=-1, keepdims=True)) + epsilon)
    return scaled * gain_row + offset

def shift_down(values):
    return jnp.concatenate([jnp.zeros_like(values[:1]), values[:-1]], axis=0)

def mixed_lookup_payload_series(acceptor_entry, lookup_lines, payload_lines, present_reward, fading_exponent):
    length = acceptor_entry.shape[0]
    attention_tally = fading_exponent.shape[0]
    attention_dimension = acceptor_entry.shape[1] // attention_tally
    block_count = length // BLOCK_LEN
    places = jnp.arange(BLOCK_LEN, dtype=jnp.float32)
    below = places[:, None] > places[None, :]
    spread = jnp.where(below, places[:, None] - 1.0 - places[None, :], 0.0)
    mask_table = jnp.where(below[None], jnp.exp(spread[None] * fading_exponent[:, None, None]), 0.0)
    enter_decay = jnp.exp(places[:, None] * fading_exponent[None, :])
    leave_decay = jnp.exp((BLOCK_LEN - 1.0 - places)[:, None] * fading_exponent[None, :])
    block_decay = jnp.exp(BLOCK_LEN * fading_exponent)
    identity_mat = jnp.eye(BLOCK_LEN, dtype=jnp.float32)
    attention_reward = present_reward.reshape(attention_tally, attention_dimension)

    def block_step(state_in, block):
        acceptor_segment, segment_lookup_matrix, value_block = block
        scores = jnp.einsum('ihe,jhe->hij', acceptor_segment, segment_lookup_matrix, precision=highest)
        self_pair_contribution = lax.optimization_barrier(jnp.sum(acceptor_segment * attention_reward * segment_lookup_matrix, axis=-1))
        weights = low(low_back(scores * mask_table + identity_mat[None] * self_pair_contribution.T[:, :, None]))
        intra_out = jnp.einsum('hij,jhe->ihe', weights, value_block, precision=highest)
        carried = jnp.einsum('ihe,hef->ihf', acceptor_segment * enter_decay[:, :, None], state_in, precision=highest)
        state_next = state_in * block_decay[:, None, None] + jnp.einsum('jhe,jhf->hef', segment_lookup_matrix * leave_decay[:, :, None], value_block, precision=highest)
        return (state_next, intra_out + carried)
    block_shape = (block_count, BLOCK_LEN, attention_tally, attention_dimension)
    initial = jnp.zeros((attention_tally, attention_dimension, attention_dimension), jnp.float32)
    _, outputs = lax.scan(jax.checkpoint(block_step), initial, (acceptor_entry.reshape(block_shape), lookup_lines.reshape(block_shape), payload_lines.reshape(block_shape)))
    return outputs.reshape(length, attention_tally * attention_dimension)

def sequence_layer(sequence, time_mats, key_mat, value_mat, gate_mat, vector_rows, fading_exponent):
    length = sequence.shape[0]
    attention_tally = fading_exponent.shape[0]
    first_norm = layer_norm(sequence, vector_rows[0], vector_rows[1])
    first_prev = shift_down(first_norm)
    mix_low = low(first_prev[None] + vector_rows[2:6, None, :] * (first_norm - first_prev)[None])
    projected = jnp.einsum('ptd,pde->pte', mix_low, time_mats[:4], precision=highest)
    acceptor_entry = low(low_back(projected[0]))
    lookup_lines = low(low_back(projected[1]))
    payload_lines = low(low_back(projected[2]))
    gate_act = jax.nn.silu(low_back(projected[3]))
    wkv_out = low_back(mixed_lookup_payload_series(acceptor_entry, lookup_lines, payload_lines, vector_rows[6], fading_exponent))
    grouped = wkv_out.reshape(length, attention_tally, -1)
    center = grouped - lax.optimization_barrier(jnp.mean(grouped, axis=-1, keepdims=True))
    scaled = center * lax.rsqrt(lax.optimization_barrier(jnp.mean(center * center, axis=-1, keepdims=True)) + group_epsilon)
    normed = scaled.reshape(length, -1) * vector_rows[7] + vector_rows[8]
    gated_low = low(normed * gate_act)
    hidden_one = sequence + low_back(jnp.dot(gated_low, time_mats[4], precision=highest))
    second = layer_norm(hidden_one, vector_rows[9], vector_rows[10])
    second_prev = shift_down(second)
    ckey = low(second_prev + vector_rows[11] * (second - second_prev))
    cgate = low(second_prev + vector_rows[12] * (second - second_prev))
    key_pre = low_back(jnp.dot(ckey, key_mat, precision=highest))
    hidden = low(jnp.square(jax.nn.relu(key_pre)))
    value_out = low_back(jnp.dot(hidden, value_mat.T, precision=highest))
    gate_sig = jax.nn.sigmoid(low_back(jnp.dot(cgate, gate_mat, precision=highest)))
    return hidden_one + gate_sig * value_out

def reference(tokens, time_weights, channel_key, channel_value, channel_gate, vectors, head_decay, lengths, cotangent):
    fading_exponent = jnp.log(head_decay.astype(jnp.float32))
    places = jnp.arange(LEN, dtype=jnp.int32)
    valid_mask = (places[None, :] < lengths[:, None]).astype(jnp.float32)
    upstream = cotangent.astype(jnp.float32) * valid_mask[:, :, None]

    def forward(inputs, time_mats, key_mat, value_mat, gate_mat, vector_rows):

        def one_sequence(sequence):
            return sequence_layer(sequence, time_mats, key_mat, value_mat, gate_mat, vector_rows, fading_exponent)
        return lax.map(jax.checkpoint(one_sequence), inputs)
    result, pullback = jax.vjp(forward, tokens.astype(jnp.float32), time_weights.astype(jnp.float32), channel_key.astype(jnp.float32), channel_value.astype(jnp.float32), channel_gate.astype(jnp.float32), vectors.astype(jnp.float32))
    gradients = pullback(upstream)
    return (result.astype(jnp.bfloat16), gradients[0].astype(jnp.bfloat16), gradients[1], gradients[2], gradients[3], gradients[4], gradients[5])
```

```python
import jax
import jax.numpy as jnp
from jax import lax
from jax.experimental import pallas as pl
from jax.experimental.pallas import tpu as pltpu
from jax.sharding import Mesh, PartitionSpec as P

BLOCK_LEN = 64
epsilon = 1e-05
group_epsilon = 0.00064

GROUP = ("y", "core")
ROWS = ("z", "x")
SEQ = ("x", "y", "core")
ALL = ("z", "x", "y", "core")
low = jnp.bfloat16


MESH = pl.DeviceIdType.MESH
HBM = pl.BlockSpec(memory_space=pl.ANY)
VMEM = pl.BlockSpec(memory_space=pltpu.VMEM)


def greet(devices):
    barrier = pltpu.get_barrier_semaphore()
    for device in devices:
        pl.semaphore_signal(barrier, inc=1, device_id=device, device_id_type=MESH)
    pl.semaphore_wait(barrier, len(devices))

def ring_places():
    y, c = lax.axis_index("y"), lax.axis_index("core")
    right, left, far = lax.rem(y + 1, 4), lax.rem(y + 3, 4), lax.rem(y + 2, 4)
    return y, c, right, left, far

def gather_kernel(x_ref, out_ref, send, recv, local):
    y, c, right, left, far = ring_places()
    to_sibling, to_right, to_left = {"core": 1 - c}, {"y": right}, {"y": left}
    greet([to_sibling, to_right, to_left])
    rows = x_ref.shape[0]
    half = rows // 2
    first, last = pl.ds(0, half), pl.ds(half, half)
    def copy(k, src, dst, device):
        return pltpu.make_async_remote_copy(src_ref=src, dst_ref=dst, send_sem=send.at[k], recv_sem=recv.at[k], device_id=device, device_id_type=MESH)
    slot = lambda place: out_ref.at[place * 2 + c]
    own = pltpu.make_async_copy(x_ref, slot(y), local)
    right_1 = copy(0, x_ref.at[first], slot(y).at[first], to_right)
    left_1 = copy(1, x_ref.at[last], slot(y).at[last], to_left)
    right_2 = copy(2, x_ref.at[last], slot(y).at[last], to_right)
    left_2 = copy(3, x_ref.at[first], slot(y).at[first], to_left)
    near = copy(4, x_ref, slot(y), to_sibling)
    for one in (right_1, left_1, right_2, left_2, near):
        one.start()
    own.start()
    right_1.wait_recv()
    far_right = copy(5, slot(left).at[first], slot(left).at[first], to_right)
    far_right.start()
    left_1.wait_recv()
    far_left = copy(6, slot(right).at[last], slot(right).at[last], to_left)
    far_left.start()
    right_2.wait_recv()
    pass_left = copy(7, slot(left), slot(left), to_sibling)
    pass_left.start()
    left_2.wait_recv()
    pass_right = copy(8, slot(right), slot(right), to_sibling)
    pass_right.start()
    far_right.wait_recv()
    pass_first = copy(9, slot(far).at[first], slot(far).at[first], to_sibling)
    pass_first.start()
    far_left.wait_recv()
    pass_last = copy(10, slot(far).at[last], slot(far).at[last], to_sibling)
    pass_last.start()
    for one in (near, pass_left, pass_right, pass_first, pass_last):
        one.wait_recv()
    for one in (right_1, left_1, right_2, left_2, near, far_right, far_left, pass_left, pass_right, pass_first, pass_last):
        one.wait_send()
    own.wait()

def gather(x, cid):
    return pl.pallas_call(
        gather_kernel,
        out_shape=jax.ShapeDtypeStruct((8,) + x.shape, x.dtype),
        in_specs=[HBM], out_specs=HBM,
        scratch_shapes=[pltpu.SemaphoreType.DMA((11,)), pltpu.SemaphoreType.DMA((11,)), pltpu.SemaphoreType.DMA],
        compiler_params=pltpu.CompilerParams(collective_id=cid, has_side_effects=True),
    )(x)

def scatter_kernel(p_ref, out_ref, from_sibling, mid, from_left, from_right, end_left, end_right, send, recv):
    y, c, right, left, far = ring_places()
    to_sibling, to_right, to_left = {"core": 1 - c}, {"y": right}, {"y": left}
    greet([to_sibling, to_right, to_left])
    half = p_ref.shape[1] // 2
    first, last = pl.ds(0, half), pl.ds(half, half)
    def copy(k, src, dst, device):
        return pltpu.make_async_remote_copy(src_ref=src, dst_ref=dst, send_sem=send.at[k], recv_sem=recv.at[k], device_id=device, device_id_type=MESH)
    order = (far, right, left, y)
    near = [copy(k, p_ref.at[order[k] * 2 + 1 - c], from_sibling.at[k], to_sibling) for k in range(4)]
    for one in near:
        one.start()
    def summed(k, rows):
        return p_ref[order[k] * 2 + c, rows].astype(jnp.float32) + from_sibling[k, rows].astype(jnp.float32)
    near[0].wait_recv()
    mid[0] = summed(0, slice(None)).astype(low)
    far_right = copy(4, mid.at[0, first], from_left, to_right)
    far_left = copy(5, mid.at[0, last], from_right, to_left)
    far_right.start(); far_left.start()
    near[1].wait_recv()
    mid[1, last] = summed(1, last).astype(low)
    right_b = copy(6, mid.at[1, last], end_left.at[last], to_right)
    right_b.start()
    near[2].wait_recv()
    mid[2, first] = summed(2, first).astype(low)
    left_b = copy(7, mid.at[2, first], end_right.at[first], to_left)
    left_b.start()
    far_right.wait_recv()
    mid[1, first] = (summed(1, first) + from_left[...].astype(jnp.float32)).astype(low)
    right_a = copy(8, mid.at[1, first], end_left.at[first], to_right)
    right_a.start()
    far_left.wait_recv()
    mid[2, last] = (summed(2, last) + from_right[...].astype(jnp.float32)).astype(low)
    left_a = copy(9, mid.at[2, last], end_right.at[last], to_left)
    left_a.start()
    near[3].wait_recv()
    out_ref[...] = summed(3, slice(None))
    right_b.wait_recv()
    out_ref[last] += end_left[last].astype(jnp.float32)
    left_b.wait_recv()
    out_ref[first] += end_right[first].astype(jnp.float32)
    right_a.wait_recv()
    out_ref[first] += end_left[first].astype(jnp.float32)
    left_a.wait_recv()
    out_ref[last] += end_right[last].astype(jnp.float32)
    for one in near + [far_right, far_left, right_b, left_b, right_a, left_a]:
        one.wait_send()

def scatter(p, cid):
    _, rows, cols = p.shape
    return pl.pallas_call(
        scatter_kernel,
        out_shape=jax.ShapeDtypeStruct((rows, cols), jnp.float32),
        in_specs=[VMEM], out_specs=VMEM,
        scratch_shapes=[pltpu.VMEM((4, rows, cols), low), pltpu.VMEM((3, rows, cols), low), pltpu.VMEM((rows // 2, cols), low), pltpu.VMEM((rows // 2, cols), low),
            pltpu.VMEM((rows, cols), low), pltpu.VMEM((rows, cols), low), pltpu.SemaphoreType.DMA((10,)), pltpu.SemaphoreType.DMA((10,))],
        compiler_params=pltpu.CompilerParams(collective_id=cid, has_side_effects=True, vmem_limit_bytes=40 * 2**20),
    )(p)

def exchange_kernel(x_ref, out_ref, send, recv, local):
    y, c = lax.axis_index("y"), lax.axis_index("core")
    me = y * 2 + c
    places = [lax.rem(me + k, 8) for k in range(1, 8)]
    devices = [{"y": p // 2, "core": lax.rem(p, 2)} for p in places]
    greet(devices)
    copies = [pltpu.make_async_remote_copy(src_ref=x_ref.at[p], dst_ref=out_ref.at[me], send_sem=send.at[k], recv_sem=recv.at[k], device_id=d, device_id_type=MESH)
        for k, (p, d) in enumerate(zip(places, devices))]
    for k in (3, 2, 4, 1, 5, 0, 6):
        copies[k].start()
    own = pltpu.make_async_copy(x_ref.at[me], out_ref.at[me], local)
    own.start()
    for one in copies:
        one.wait()
    own.wait()

def exchange(x, cid):
    return pl.pallas_call(
        exchange_kernel,
        out_shape=jax.ShapeDtypeStruct(x.shape, x.dtype),
        in_specs=[HBM], out_specs=HBM,
        scratch_shapes=[pltpu.SemaphoreType.DMA((7,)), pltpu.SemaphoreType.DMA((7,)), pltpu.SemaphoreType.DMA],
        compiler_params=pltpu.CompilerParams(collective_id=cid, has_side_effects=True),
    )(x)

def line_kernel(x_ref, out_ref, send, recv, local):
    me = lax.axis_index("x")
    devices = [{"x": lax.rem(me + k, 4)} for k in range(1, 4)]
    greet(devices)
    copies = [pltpu.make_async_remote_copy(src_ref=x_ref, dst_ref=out_ref.at[me], send_sem=send.at[k], recv_sem=recv.at[k], device_id=d, device_id_type=MESH)
        for k, d in enumerate(devices)]
    for k in (1, 0, 2):
        copies[k].start()
    own = pltpu.make_async_copy(x_ref, out_ref.at[me], local)
    own.start()
    for one in copies:
        one.wait()
    own.wait()

def line(x, cid):
    return pl.pallas_call(
        line_kernel,
        out_shape=jax.ShapeDtypeStruct((4,) + x.shape, x.dtype),
        in_specs=[HBM], out_specs=HBM,
        scratch_shapes=[pltpu.SemaphoreType.DMA((3,)), pltpu.SemaphoreType.DMA((3,)), pltpu.SemaphoreType.DMA],
        compiler_params=pltpu.CompilerParams(collective_id=cid, has_side_effects=True),
    )(x)

def cube_places():
    z, x, y, c = [lax.axis_index(name) for name in ("z", "x", "y", "core")]
    place, member = z * 4 + x, y * 2 + c
    far = [lax.rem(place + k, 16) for k in range(1, 16)]
    near = [lax.rem(member + k, 8) for k in range(1, 8)]
    return place, member, far, near, [{"z": p // 4, "x": lax.rem(p, 4)} for p in far], [{"y": p // 2, "core": lax.rem(p, 2)} for p in near]

def settings_kernel(x_ref, out_ref, blocks, stripe, send, recv):
    place, member, far, near, far_devices, near_devices = cube_places()
    greet(far_devices + near_devices)
    first = [pltpu.make_async_remote_copy(src_ref=x_ref, dst_ref=blocks.at[k], send_sem=send.at[k], recv_sem=recv.at[k], device_id=d, device_id_type=MESH) for k, d in enumerate(near_devices)]
    for one in first:
        one.start()
    total = x_ref[...].astype(jnp.float32)
    for k, one in enumerate(first):
        one.wait_recv()
        total = total + blocks[k].astype(jnp.float32)
    stripe[...] = total.astype(low)
    second = [pltpu.make_async_remote_copy(src_ref=stripe, dst_ref=out_ref.at[place], send_sem=send.at[7 + k], recv_sem=recv.at[7 + k], device_id=d, device_id_type=MESH) for k, d in enumerate(far_devices)]
    for one in second:
        one.start()
    out_ref[place] = stripe[...]
    for one in second:
        one.wait()
    for one in first:
        one.wait_send()

def gather_settings(x, cid):
    return pl.pallas_call(
        settings_kernel,
        out_shape=jax.ShapeDtypeStruct((16, 16, 128), low),
        in_specs=[VMEM], out_specs=VMEM,
        scratch_shapes=[pltpu.VMEM((7, 16, 128), low), pltpu.VMEM((16, 128), low), pltpu.SemaphoreType.DMA((22,)), pltpu.SemaphoreType.DMA((22,))],
        compiler_params=pltpu.CompilerParams(collective_id=cid, has_side_effects=True),
    )(x)

def total_kernel(x_ref, out_ref, far_blocks, near_blocks, stripe, send, recv):
    place, member, far, near, far_devices, near_devices = cube_places()
    greet(far_devices + near_devices)
    first = [pltpu.make_async_remote_copy(src_ref=x_ref.at[p], dst_ref=far_blocks.at[k], send_sem=send.at[7 + k], recv_sem=recv.at[7 + k], device_id=d, device_id_type=MESH) for k, (p, d) in enumerate(zip(far, far_devices))]
    for one in first:
        one.start()
    total = x_ref[place]
    for k, one in enumerate(first):
        one.wait_recv()
        total = total + far_blocks[k]
    stripe[...] = total
    second = [pltpu.make_async_remote_copy(src_ref=stripe, dst_ref=near_blocks.at[k], send_sem=send.at[k], recv_sem=recv.at[k], device_id=d, device_id_type=MESH) for k, d in enumerate(near_devices)]
    for one in second:
        one.start()
    for k, one in enumerate(second):
        one.wait_recv()
        total = total + near_blocks[k]
    out_ref[...] = total
    for one in first + second:
        one.wait_send()

def total_vectors(x, cid):
    return pl.pallas_call(
        total_kernel,
        out_shape=jax.ShapeDtypeStruct((16, 128), jnp.float32),
        in_specs=[VMEM], out_specs=VMEM,
        scratch_shapes=[pltpu.VMEM((15, 16, 128), jnp.float32), pltpu.VMEM((7, 16, 128), jnp.float32), pltpu.VMEM((16, 128), jnp.float32), pltpu.SemaphoreType.DMA((22,)), pltpu.SemaphoreType.DMA((22,))],
        compiler_params=pltpu.CompilerParams(collective_id=cid, has_side_effects=True),
    )(x)


def shifted(block, axis, distance):
    devices = range(lax.axis_size(axis))
    route = [(i - distance, i) for i in devices if i - distance in devices]
    return lax.ppermute(block, axis, route)


def layer_norm(values, gain_row, offset):
    center = values - jnp.mean(values, axis=-1, keepdims=True)
    inverse = lax.rsqrt(jnp.mean(center * center, axis=-1, keepdims=True) + epsilon)
    scaled = center * inverse
    return (scaled * gain_row + offset, scaled, inverse)


def norm_back(upstream, scaled, inverse, gain_row):
    inner_grad = upstream * gain_row
    return inverse * (
        inner_grad
        - jnp.mean(inner_grad, axis=-1, keepdims=True)
        - scaled * jnp.mean(inner_grad * scaled, axis=-1, keepdims=True)
    )


def dot_to(left, right):
    return jnp.dot(left, right, preferred_element_type=jnp.float32)


def dot_right(left, right):
    return lax.dot_general(left, right, (((1,), (1,)), ((), ())), preferred_element_type=jnp.float32)


def dot_left(left, right):
    return lax.dot_general(left, right, (((0,), (0,)), ((), ())), preferred_element_type=jnp.float32)


def mul(spec, left, right):
    return jnp.einsum(spec, left.astype(low), right.astype(low), preferred_element_type=jnp.float32)


def body(tokens, time_weights, channel_key, channel_value, channel_gate, vectors, head_decay, lengths, cotangent):
    groups, span, width = tokens.shape
    features = channel_key.shape[1]
    local_rows = channel_key.shape[0]
    members = lax.axis_size(GROUP)
    member = lax.axis_index(GROUP)
    x_size, x_place = lax.axis_size("x"), lax.axis_index("x")
    heads = head_decay.shape[0] // members
    head_width = width // head_decay.shape[0]
    own = width // members
    own_features = features // members
    row_count = groups * span
    all_rows = members * row_count
    stripe = members * local_rows

    time_part = jnp.swapaxes(time_weights, 0, 1).reshape(local_rows, 5, members, own)
    time_part = lax.all_to_all(time_part, GROUP, split_axis=2, concat_axis=0, tiled=True)
    time_full = lax.all_gather(time_part.reshape(stripe, 5 * own), ROWS, axis=0, tiled=True)
    channel_part = jnp.concatenate(
        [
            channel_key.reshape(local_rows, members, own_features),
            channel_value.reshape(local_rows, members, own_features),
            channel_gate.reshape(local_rows, members, own),
        ],
        axis=2,
    )
    channel_part = lax.all_to_all(channel_part, GROUP, split_axis=1, concat_axis=0, tiled=True)
    channel_part = channel_part.reshape(stripe, 2 * own_features + own)
    channel_part, time_full = lax.optimization_barrier((channel_part, time_full))
    channel_full = lax.all_gather(channel_part, ROWS, axis=0, tiled=True)
    key_full, value_full = channel_full[:, :own_features], channel_full[:, own_features : 2 * own_features]
    gate_full = channel_full[:, 2 * own_features :]
    out_full = time_full[:, 4 * own :].reshape(members, own, own)
    vector_rows = vectors.shape[0]
    vector_block = lax.dynamic_update_slice(
        jnp.zeros((16, stripe), low), vectors, (0, member * local_rows)
    )
    vector_full = jnp.swapaxes(gather_settings(vector_block, 1), 0, 1).reshape(16, width)[:vector_rows]
    settings = vector_full.astype(jnp.float32)
    own_settings = lax.dynamic_slice_in_dim(settings, member * own, own, axis=1)

    inputs_all = gather(tokens.reshape(row_count, width), 2).reshape(members, groups, span, width)
    first_norm, first_scaled, _ = layer_norm(inputs_all.astype(jnp.float32), settings[0], settings[1])
    edge_norm, _, _ = layer_norm(shifted(inputs_all[-1, :, -1, :], "x", 1).astype(jnp.float32), settings[0], settings[1])
    edge_norm = jnp.where(x_place > 0, edge_norm, 0.0)
    before = jnp.concatenate([edge_norm[None], first_norm[:-1, :, -1, :]], axis=0)
    first_prev = jnp.concatenate([before[:, :, None, :], first_norm[:, :, :-1, :]], axis=2)
    first_delta = (first_norm - first_prev).reshape(all_rows, width)
    first_prev = first_prev.reshape(all_rows, width)
    mix_low = [(first_prev + settings[2 + p] * first_delta).astype(low) for p in range(4)]
    projected = [dot_to(mix_low[p], time_full[:, p * own : (p + 1) * own]) for p in range(4)]
    gate_pre = projected[3]
    gate_act = jax.nn.silu(gate_pre)

    log_decay = jnp.log(lax.dynamic_slice_in_dim(head_decay, member * heads, heads))
    places = jnp.arange(BLOCK_LEN, dtype=jnp.float32)
    below = places[:, None] > places[None, :]
    spread = jnp.where(below, places[:, None] - 1.0 - places[None, :], 0.0)
    mask_table = jnp.where(below[None], jnp.exp(spread[None] * log_decay[:, None, None]), 0.0)
    enter_decay = jnp.exp(places[:, None] * log_decay[None, :])
    leave_decay = jnp.exp((BLOCK_LEN - 1.0 - places)[:, None] * log_decay[None, :])
    block_decay = jnp.exp(BLOCK_LEN * log_decay)[None, :, None, None]

    def power(count):
        return jnp.exp(count * log_decay)[None, :, None, None]

    identity = jnp.eye(BLOCK_LEN, dtype=jnp.float32)
    block_shape = (members, groups, BLOCK_LEN, heads, head_width)
    recv, key, value = [projected[p].astype(low).reshape(block_shape) for p in range(3)]
    bonus = own_settings[6].reshape(heads, head_width)
    recv_wide, key_wide = recv.astype(jnp.float32), key.astype(jnp.float32)
    scores = mul("msihe,msjhe->mshij", recv, key)
    self_pair = jnp.sum(recv_wide * bonus * key_wide, axis=-1)
    weights = (scores * mask_table + identity * jnp.swapaxes(self_pair, 2, 3)[..., None]).astype(low)
    intra = mul("mshij,msjhe->msihe", weights, value)
    key_leave = (key_wide * leave_decay[:, :, None]).astype(low)
    block_states = mul("msjhe,msjhf->mshef", key_leave, value)
    running = jnp.zeros_like(block_states[0])
    prefixes = []
    for m in range(members):
        prefixes.append(running)
        running = running * block_decay + block_states[m]
    every_state = line(running.reshape(-1, 128), 3).reshape((x_size,) + running.shape)
    entering = jnp.zeros_like(running)
    span_decay = power(float(BLOCK_LEN * members))
    for x in range(x_size - 1):
        entering = jnp.where(x < x_place, entering * span_decay + every_state[x], entering)
    incoming = jnp.stack([prefixes[m] + power(float(BLOCK_LEN * m)) * entering for m in range(members)])
    incoming = incoming.astype(low)
    recv_enter = (recv_wide * enter_decay[:, :, None]).astype(low)
    wkv = (intra + mul("msihe,mshef->msihf", recv_enter, incoming)).reshape(all_rows, heads, head_width)
    wkv_center = wkv - jnp.mean(wkv, axis=-1, keepdims=True)
    wkv_inverse = lax.rsqrt(jnp.mean(wkv_center * wkv_center, axis=-1, keepdims=True) + group_epsilon)
    wkv_scaled = wkv_center * wkv_inverse
    normed = wkv_scaled.reshape(all_rows, own) * own_settings[7] + own_settings[8]
    gated_own = (normed * gate_act).astype(low)
    gated_all = gather(gated_own, 5)
    out_own = jnp.einsum("mre,med->rd", gated_all, out_full, preferred_element_type=jnp.float32)
    out = exchange(out_own.astype(low).reshape(members, row_count, own), 6)

    inputs = tokens.astype(jnp.float32)
    hidden_one = inputs.reshape(row_count, width) + jnp.swapaxes(out, 0, 1).reshape(row_count, width).astype(jnp.float32)
    second, second_scaled, second_inverse = layer_norm(
        hidden_one.reshape(groups, span, width), settings[9], settings[10]
    )
    second_all = gather(second.astype(low).reshape(row_count, width), 7).reshape(members, groups, span, width)
    second_edge = shifted(second_all[-1, :, -1, :], "x", 1)
    before = jnp.concatenate([second_edge[None], second_all[:-1, :, -1, :]], axis=0)
    second_prev = jnp.concatenate([before[:, :, None, :], second_all[:, :, :-1, :]], axis=2)
    second_prev = second_prev.reshape(all_rows, width).astype(jnp.float32)
    second_delta = second_all.reshape(all_rows, width).astype(jnp.float32) - second_prev
    ckey = (second_prev + settings[11] * second_delta).astype(low)
    cgate = (second_prev + settings[12] * second_delta).astype(low)
    rectified = jax.nn.relu(dot_to(ckey, key_full))
    hidden = (rectified * rectified).astype(low)
    value_out = scatter(dot_right(hidden, value_full).astype(low).reshape(members, row_count, width), 8)
    gate_pre_own = dot_to(cgate, gate_full).astype(low).reshape(members, row_count, own)
    channel_pre = jnp.swapaxes(exchange(gate_pre_own, 9), 0, 1).reshape(row_count, width)
    gate_sig = jax.nn.sigmoid(channel_pre.astype(jnp.float32))
    layer_out = (hidden_one + gate_sig * value_out).reshape(groups, span, width).astype(low)

    seq_place = lax.axis_index(SEQ)
    offsets = seq_place * span + jnp.arange(span, dtype=jnp.int32)
    valid = (offsets[None, :] < lengths[:, None]).astype(jnp.float32)
    upstream = (cotangent.astype(jnp.float32) * valid[:, :, None]).reshape(row_count, width)
    grad_value = (upstream * gate_sig).astype(low)
    grad_gate = (upstream * value_out * gate_sig * (1.0 - gate_sig)).astype(low)
    grad_value_all = gather(grad_value, 10).reshape(all_rows, width)
    grad_gate_own = exchange(jnp.swapaxes(grad_gate.reshape(row_count, members, own), 0, 1), 11).reshape(all_rows, own)
    grad_key = (2.0 * dot_to(grad_value_all, value_full) * rectified).astype(low)
    grad_ckey = dot_right(grad_key, key_full)
    grad_cgate = dot_right(grad_gate_own, gate_full)
    mix_key_grad = jnp.sum(second_delta * grad_ckey, axis=0)
    mix_gate_grad = jnp.sum(second_delta * grad_cgate, axis=0)
    grad_second = (settings[11] * grad_ckey + settings[12] * grad_cgate).reshape(members, groups, span, width)
    grad_prev = ((1.0 - settings[11]) * grad_ckey + (1.0 - settings[12]) * grad_cgate).reshape(
        members, groups, span, width
    )
    second_back = shifted(grad_prev[0, :, 0, :], "x", -1)
    after = jnp.concatenate([grad_prev[1:, :, 0, :], second_back[None]], axis=0)
    grad_second = grad_second + jnp.concatenate([grad_prev[:, :, 1:, :], after[:, :, None, :]], axis=2)
    grad_second = scatter(grad_second.astype(low).reshape(members, row_count, width), 8).reshape(groups, span, width)
    channel_term = jnp.concatenate(
        [
            dot_left(ckey, grad_key).astype(low),
            dot_left(grad_value_all, hidden).astype(low),
            dot_left(cgate, grad_gate_own).astype(low),
        ],
        axis=1,
    )
    channel_term, grad_second = lax.optimization_barrier((channel_term, grad_second))
    channel_sum = lax.psum_scatter(channel_term, ROWS, scatter_dimension=0, tiled=True)
    channel_sum = lax.all_to_all(
        channel_sum.reshape(members, local_rows, 2 * own_features + own), GROUP, split_axis=0, concat_axis=0, tiled=True
    )
    channel_sum = jnp.swapaxes(channel_sum, 0, 1).astype(jnp.float32)
    key_grad = channel_sum[:, :, :own_features].reshape(local_rows, features)
    value_grad = channel_sum[:, :, own_features : 2 * own_features].reshape(local_rows, features)
    gate_grad = channel_sum[:, :, 2 * own_features :].reshape(local_rows, width)
    second_gain_grad = jnp.sum(grad_second * second_scaled, axis=(0, 1))
    second_bias_grad = jnp.sum(grad_second, axis=(0, 1))
    grad_hidden_one = upstream + norm_back(grad_second, second_scaled, second_inverse, settings[9]).reshape(
        row_count, width
    )
    grad_out = grad_hidden_one.astype(low)
    grad_out_own = exchange(jnp.swapaxes(grad_out.reshape(row_count, members, own), 0, 1), 12).reshape(all_rows, own)
    grad_gated = scatter(
        jnp.einsum("rd,med->mre", grad_out_own, out_full, preferred_element_type=jnp.float32).astype(low), 13
    )
    out_term = jnp.einsum("mre,rd->med", gated_all, grad_out_own, preferred_element_type=jnp.float32).astype(low)
    grad_normed = grad_gated * gate_act
    gate_sigma = jax.nn.sigmoid(gate_pre)
    grad_gate_pre = (grad_gated * normed * gate_sigma * (1.0 + gate_pre * (1.0 - gate_sigma))).astype(low)
    norm_gain_grad = jnp.sum(grad_normed * wkv_scaled.reshape(all_rows, own), axis=0)
    norm_bias_grad = jnp.sum(grad_normed, axis=0)
    grad_wkv = norm_back(
        grad_normed.reshape(all_rows, heads, head_width),
        wkv_scaled,
        wkv_inverse,
        own_settings[7].reshape(heads, head_width),
    )
    grad_wkv = grad_wkv.astype(low).reshape(block_shape)
    grad_weights = mul("msihf,msjhf->mshij", grad_wkv, value).astype(low).astype(jnp.float32)
    masked = (grad_weights * mask_table).astype(low)
    self_back = jnp.swapaxes(jnp.sum(grad_weights * identity, axis=4), 2, 3)[..., None]
    bonus_grad = jnp.sum(self_back * recv_wide * key_wide, axis=(0, 1, 2)).reshape(own)
    grad_incoming = mul("msihe,msihf->mshef", recv_enter, grad_wkv)
    running = jnp.zeros_like(grad_incoming[0])
    suffixes = []
    for m in reversed(range(members)):
        suffixes.append(running)
        running = running * block_decay + grad_incoming[m]
    every_grad = line(running.reshape(-1, 128), 4).reshape((x_size,) + running.shape)
    leaving = jnp.zeros_like(running)
    for x in reversed(range(1, x_size)):
        leaving = jnp.where(x > x_place, leaving * span_decay + every_grad[x], leaving)
    grad_states = jnp.stack(
        [suffixes[members - 1 - m] + power(float(BLOCK_LEN * (members - 1 - m))) * leaving for m in range(members)]
    ).astype(low)
    grad_recv = (
        mul("mshij,msjhe->msihe", masked, key)
        + self_back * bonus * key_wide
        + mul("msihf,mshef->msihe", grad_wkv, incoming) * enter_decay[:, :, None]
    )
    grad_lookup = (
        mul("mshij,msihe->msjhe", masked, recv)
        + self_back * bonus * recv_wide
        + mul("msjhf,mshef->msjhe", value, grad_states) * leave_decay[:, :, None]
    )
    grad_values = mul("mshij,msihf->msjhf", weights, grad_wkv) + mul("msjhe,mshef->msjhf", key_leave, grad_states)
    grad_proj = [
        grad_recv.reshape(all_rows, own).astype(low),
        grad_lookup.reshape(all_rows, own).astype(low),
        grad_values.reshape(all_rows, own).astype(low),
        grad_gate_pre,
    ]
    time_term = jnp.concatenate(
        [dot_left(mix_low[p], grad_proj[p]).astype(low) for p in range(4)] + [out_term.reshape(width, own)], axis=1
    )
    time_sum = lax.psum_scatter(time_term, ROWS, scatter_dimension=0, tiled=True)
    time_sum = lax.all_to_all(
        time_sum.reshape(members, local_rows, 5, own), GROUP, split_axis=0, concat_axis=0, tiled=True
    ).astype(jnp.float32)
    time_grads = jnp.transpose(time_sum, (2, 1, 0, 3)).reshape(5, local_rows, width)
    grad_mix = [dot_right(grad_proj[p], time_full[:, p * own : (p + 1) * own]) for p in range(4)]
    mix_grads = [jnp.sum(first_delta * grad_mix[p], axis=0) for p in range(4)]
    grad_first = sum(settings[2 + p] * grad_mix[p] for p in range(4)).reshape(members, groups, span, width)
    grad_prev = sum((1.0 - settings[2 + p]) * grad_mix[p] for p in range(4)).reshape(members, groups, span, width)
    first_back = shifted(grad_prev[0, :, 0, :], "x", -1)
    after = jnp.concatenate([grad_prev[1:, :, 0, :], first_back[None]], axis=0)
    grad_first = grad_first + jnp.concatenate([grad_prev[:, :, 1:, :], after[:, :, None, :]], axis=2)
    grad_first = scatter(grad_first.astype(low).reshape(members, row_count, width), 8).reshape(groups, span, width)
    own_center = inputs - jnp.mean(inputs, axis=-1, keepdims=True)
    own_inverse = lax.rsqrt(jnp.mean(own_center * own_center, axis=-1, keepdims=True) + epsilon)
    own_scaled = own_center * own_inverse
    first_gain_grad = jnp.sum(grad_first * own_scaled, axis=(0, 1))
    first_bias_grad = jnp.sum(grad_first, axis=(0, 1))
    token_grad = (
        grad_hidden_one.reshape(groups, span, width) + norm_back(grad_first, own_scaled, own_inverse, settings[0])
    ).astype(low)

    def spread_own(row):
        return lax.dynamic_update_slice_in_dim(jnp.zeros((width,), jnp.float32), row, member * own, axis=0)

    vector_term = jnp.stack(
        [
            first_gain_grad,
            first_bias_grad,
            *mix_grads,
            spread_own(bonus_grad),
            spread_own(norm_gain_grad),
            spread_own(norm_bias_grad),
            second_gain_grad,
            second_bias_grad,
            mix_key_grad,
            mix_gate_grad,
        ]
    )
    vector_term = jnp.pad(vector_term, ((0, 16 - vector_rows), (0, 0))).reshape(16, width // stripe, stripe)
    vector_sum = total_vectors(jnp.swapaxes(vector_term, 0, 1), 14)
    vector_sum = lax.dynamic_slice(vector_sum, (0, member * local_rows), (vector_rows, local_rows))
    return layer_out, token_grad, time_grads, key_grad, value_grad, gate_grad, vector_sum


def solution(mesh):
    batch, seq = mesh.devices.shape
    side = 4
    fine = Mesh(mesh.devices.reshape(batch, side, seq // (2 * side), 2), ALL)
    return jax.shard_map(
        body,
        mesh=fine,
        in_specs=(
            P("z", SEQ, None),
            P(None, ALL, None),
            P(ALL, None),
            P(ALL, None),
            P(ALL, None),
            P(None, ALL),
            P(),
            P("z"),
            P("z", SEQ, None),
        ),
        out_specs=(
            P("z", SEQ, None),
            P("z", SEQ, None),
            P(None, ALL, None),
            P(ALL, None),
            P(ALL, None),
            P(ALL, None),
            P(None, ALL),
        ),
        check_vma=False,
    )
```

```python
import jax
import jax.numpy as jnp
from jax import lax
from jax.experimental import pallas as pl
from jax.experimental.pallas import tpu as pltpu
from jax.sharding import Mesh, PartitionSpec as P

BLOCK_LEN = 64
epsilon = 1e-05
group_epsilon = 0.00064

GROUP = ("y", "core")
ROWS = ("z", "x")
SEQ = ("x", "y", "core")
ALL = ("z", "x", "y", "core")
low = jnp.bfloat16


MESH = pl.DeviceIdType.MESH
HBM = pl.BlockSpec(memory_space=pl.ANY)


def cost(microseconds):
    return pl.CostEstimate(flops=0, bytes_accessed=microseconds * 3_000_000, transcendentals=0)


VMEM = pl.BlockSpec(memory_space=pltpu.VMEM)


def greet(devices):
    barrier = pltpu.get_barrier_semaphore()
    for device in devices:
        pl.semaphore_signal(barrier, inc=1, device_id=device, device_id_type=MESH)
    pl.semaphore_wait(barrier, len(devices))

def ring_places():
    y, c = lax.axis_index("y"), lax.axis_index("core")
    right, left, far = lax.rem(y + 1, 4), lax.rem(y + 3, 4), lax.rem(y + 2, 4)
    return y, c, right, left, far

def cube_places():
    z, x, y, c = [lax.axis_index(name) for name in ("z", "x", "y", "core")]
    place, member = z * 4 + x, y * 2 + c
    far = [lax.rem(place + k, 16) for k in range(1, 16)]
    near = [lax.rem(member + k, 8) for k in range(1, 8)]
    return place, member, far, near, [{"z": p // 4, "x": lax.rem(p, 4)} for p in far], [{"y": p // 2, "core": lax.rem(p, 2)} for p in near]

def nn(left, right):
    return jnp.dot(left, right, preferred_element_type=jnp.float32)


def nt(left, right):
    return lax.dot_general(left, right, (((1,), (1,)), ((), ())), preferred_element_type=jnp.float32)


def tn(left, right):
    return lax.dot_general(left, right, (((0,), (0,)), ((), ())), preferred_element_type=jnp.float32)


def head_tables(log_row):
    width = log_row.shape[-1]
    place = lax.broadcasted_iota(jnp.int32, (BLOCK_LEN, width), 0)
    other = lax.rem(lax.broadcasted_iota(jnp.int32, (BLOCK_LEN, width), 1), BLOCK_LEN)
    gap = jnp.maximum(place - 1 - other, 0).astype(jnp.float32)
    mask = jnp.where(other < place, jnp.exp(gap * log_row), 0.0)
    eye = other == place
    enter = jnp.exp(place.astype(jnp.float32) * log_row)
    leave = jnp.exp((BLOCK_LEN - 1 - place).astype(jnp.float32) * log_row)
    tall = lax.broadcasted_iota(jnp.int32, (width, width), 0) // BLOCK_LEN
    wide = lax.broadcasted_iota(jnp.int32, (width, width), 1) // BLOCK_LEN
    return mask, eye, enter, leave, tall == wide


def expand(block, same):
    copies = block.shape[1] // BLOCK_LEN
    return jnp.where(same, jnp.concatenate([block] * copies, axis=0), jnp.zeros((), block.dtype))


def compress(square, same):
    kept = jnp.where(same, square, 0.0)
    return sum(kept[k * BLOCK_LEN : (k + 1) * BLOCK_LEN] for k in range(square.shape[0] // BLOCK_LEN))


def head_sum(values, same, factor=1.0):
    ones = jnp.where(same, factor, 0.0).astype(low)
    high = values.astype(low)
    rest = (values - high.astype(jnp.float32)).astype(low)
    return nn(high, ones) + nn(rest, ones)


def head_mean(values, same):
    return head_sum(values, same, 1.0 / BLOCK_LEN)


def block_rows(m, s):
    return pl.ds(pl.multiple_of(m * 2 * BLOCK_LEN + s * BLOCK_LEN, BLOCK_LEN), BLOCK_LEN)


def start_line(total, slots, send, recv):
    me = lax.axis_index("x")
    devices = [{"x": lax.rem(me + k, 4)} for k in range(1, 4)]
    slots[me] = total[...]
    copies = [
        pltpu.make_async_remote_copy(
            src_ref=total, dst_ref=slots.at[me], send_sem=send.at[k], recv_sem=recv.at[k], device_id=d, device_id_type=MESH
        )
        for k, d in enumerate(devices)
    ]
    for one in copies:
        one.start()
    return copies


def recurrence_kernel(
    r_ref, k_ref, v_ref, g_ref, p_ref, tok_ref, set_ref, time_hbm,
    w_ref, scaled_ref, inverse_ref, in_ref, hidden_ref, second_ref, gated_ref,
    wkv, prefix, total, slots, gated, time, out, out_all, send, recv, local,
):
    x, member, near, near_devices, _, _ = group_and_line()
    y, c, right, left, far = ring_places()
    greet(near_devices + [{"x": lax.rem(x + n, 4)} for n in range(1, 4)])
    copy = Copies(send, recv)
    load = pltpu.make_async_copy(time_hbm.at[4], time, local.at[0])
    load.start()
    log_row, bonus, gain, bias = [p_ref[n : n + 1, :] for n in range(4)]
    mask, eye, enter, leave, same = head_tables(log_row)
    block_decay = jnp.exp(BLOCK_LEN * log_row)

    def first(m, states):
        after = []
        for s in range(2):
            rows = block_rows(m, s)
            r, k, v = r_ref[rows], k_ref[rows], v_ref[rows]
            key = expand(k, same)
            scores = nt(r, key)
            pairs = head_sum(r.astype(jnp.float32) * bonus * k.astype(jnp.float32), same)
            weights = (scores * mask + jnp.where(eye, pairs, 0.0)).astype(low)
            w_ref[rows] = weights
            wkv[rows] = nn(weights, expand(v, same))
            prefix[m * 2 + s] = states[s]
            key_leave = (k.astype(jnp.float32) * leave).astype(low)
            after.append(states[s] * block_decay + compress(tn(key_leave, v), same))
        return tuple(after)

    zero = jnp.zeros(enter.shape, jnp.float32)
    states = lax.fori_loop(0, 8, first, (zero, zero))
    for s in range(2):
        total[s] = states[s]
    for one in start_line(total, slots, send.at[pl.ds(30, 3)], recv.at[pl.ds(30, 3)]):
        one.wait()
    x_place = lax.axis_index("x")
    entering = [zero, zero]
    span_decay = jnp.exp(8.0 * BLOCK_LEN * log_row)
    for x in range(3):
        for s in range(2):
            entering[s] = jnp.where(x < x_place, entering[s] * span_decay + slots[x, s], entering[s])
    for s in range(2):
        total[s] = entering[s]

    def second(m, carry):
        power = jnp.exp((m * BLOCK_LEN).astype(jnp.float32) * log_row)
        for s in range(2):
            rows = block_rows(m, s)
            state = (prefix[m * 2 + s] + power * total[s]).astype(low)
            in_ref[m * 2 + s] = state
            recv_enter = (r_ref[rows].astype(jnp.float32) * enter).astype(low)
            out = wkv[rows] + nn(recv_enter, expand(state, same))
            center = out - head_mean(out, same)
            inverse = lax.rsqrt(head_mean(center * center, same) + group_epsilon)
            scaled = center * inverse
            scaled_ref[rows] = scaled
            inverse_ref[rows] = inverse
            gate = g_ref[rows]
            gated[member, rows] = ((scaled * gain + bias) * gate * jax.nn.sigmoid(gate)).astype(low)
        return carry

    half = gated.shape[1] // 2
    ring = Ring(copy, "y", lambda at, n: gated.at[at * 2 + c, pl.ds(n * half, half)], start=False)
    to_sibling = {"core": 1 - c}
    across = [copy(gated.at[member, pl.ds(n * half, half)], gated.at[member, pl.ds(n * half, half)], to_sibling) for n in range(2)]
    for n in range(2):
        lax.fori_loop(4 * n, 4 * n + 4, second, 0)
        ring.start(n)
        across[n].start()

    def pass_on(at):
        one = copy(gated.at[at * 2 + c], gated.at[at * 2 + c], to_sibling)
        one.start()
        return one

    ring.forward()
    ring.wait_near()
    passed = [pass_on(right), pass_on(left)]
    load.wait()
    ring.wait_far()
    passed.append(pass_on(far))
    for one in across + passed:
        one.wait_recv()
    keep = pltpu.make_async_copy(gated, gated_ref, local.at[1])
    keep.start()

    cols = w_ref.shape[1]
    given = []

    def project(q):
        rows = pl.ds(pl.multiple_of(q * 256, 256), 256)
        value = sum(nn(gated[m, rows], time[m * cols : (m + 1) * cols]) for m in range(8)).astype(low)
        for b in range(2):
            out[q * 2 + b] = value[b * 128 : (b + 1) * 128]

    for at in (far, right, left, y):
        project(at)
        for turn in range(2):
            j = at * 2 + lax.rem(c + turn, 2)
            if at is y and turn == 0:
                continue
            given.append(copy(out.at[j], out_all.at[member], {"y": at, "core": lax.rem(c + turn, 2)}))
            given[-1].start()
    out_all[member] = out[member]
    for one in given:
        one.wait_recv()

    def norm_rows(t, carry):
        rows = pl.ds(pl.multiple_of(t * 16, 16), 16)
        added = jnp.concatenate([out_all[n, rows].astype(jnp.float32) for n in range(8)], axis=1)
        values = tok_ref[rows].astype(jnp.float32) + added
        hidden_ref[rows] = values
        center = values - jnp.mean(values, axis=-1, keepdims=True)
        inverse = lax.rsqrt(jnp.mean(center * center, axis=-1, keepdims=True) + epsilon)
        second_ref[rows] = (center * inverse * set_ref[9:10, :] + set_ref[10:11, :]).astype(low)
        return carry

    lax.fori_loop(0, 8, norm_rows, 0)
    copy.wait_sent()
    keep.wait()


def recurrence(r, k, v, g, params, tokens, settings, time, cid):
    rows, cols = r.shape
    own_rows, width = tokens.shape
    shape = jax.ShapeDtypeStruct
    return pl.pallas_call(
        recurrence_kernel,
        name="recurrence",
        cost_estimate=cost(55),
        out_shape=[
            shape((rows, cols), low),
            shape((rows, cols), jnp.float32),
            shape((rows, cols), jnp.float32),
            shape((16, BLOCK_LEN, cols), low),
            shape((own_rows, width), jnp.float32),
            shape((own_rows, width), low),
            shape((8, rows, cols), low),
        ],
        in_specs=[VMEM] * 7 + [HBM],
        out_specs=[VMEM] * 6 + [HBM],
        scratch_shapes=[
            pltpu.VMEM((rows, cols), jnp.float32),
            pltpu.VMEM((16, BLOCK_LEN, cols), jnp.float32),
            pltpu.VMEM((2, BLOCK_LEN, cols), jnp.float32),
            pltpu.VMEM((4, 2, BLOCK_LEN, cols), jnp.float32),
            pltpu.VMEM((8, rows, cols), low),
            pltpu.VMEM((width, cols), low),
            pltpu.VMEM((8, own_rows, cols), low),
            pltpu.VMEM((8, own_rows, cols), low),
            pltpu.SemaphoreType.DMA((33,)),
            pltpu.SemaphoreType.DMA((33,)),
            pltpu.SemaphoreType.DMA((2,)),
        ],
        compiler_params=pltpu.CompilerParams(collective_id=cid, has_side_effects=True, vmem_limit_bytes=48 * 2**20),
    )(r, k, v, g, params, tokens, settings, time)


class Copies:
    def __init__(self, send, recv):
        self.send, self.recv, self.count, self.all = send, recv, 0, []

    def __call__(self, src, dst, device):
        one = pltpu.make_async_remote_copy(
            src_ref=src,
            dst_ref=dst,
            send_sem=self.send.at[self.count],
            recv_sem=self.recv.at[self.count],
            device_id=device,
            device_id_type=MESH,
        )
        self.count += 1
        self.all.append(one)
        return one

    def wait_sent(self, some=None):
        some = self.all if some is None else some
        for one in some:
            one.wait_send()
        self.all = [one for one in self.all if not any(one is other for other in some)]


class Ring:
    def __init__(self, copy, axis, part, start=True):
        me = lax.axis_index(axis)
        self.copy, self.part = copy, part
        self.right, self.left, self.far = [lax.rem(me + k, 4) for k in (1, 3, 2)]
        self.to_right, self.to_left = {axis: self.right}, {axis: self.left}
        own = [part(me, 0), part(me, 1)]
        self.near = [
            copy(own[0], own[0], self.to_right),
            copy(own[1], own[1], self.to_left),
            copy(own[1], own[1], self.to_right),
            copy(own[0], own[0], self.to_left),
        ]
        if start:
            for one in self.near:
                one.start()

    def start(self, half):
        for n in ((0, 3), (2, 1))[half]:
            self.near[n].start()

    def forward(self):
        self.near[0].wait_recv()
        there = self.part(self.left, 0)
        self.far_right = self.copy(there, there, self.to_right)
        self.far_right.start()
        self.near[1].wait_recv()
        there = self.part(self.right, 1)
        self.far_left = self.copy(there, there, self.to_left)
        self.far_left.start()

    def wait_near(self):
        self.near[2].wait_recv()
        self.near[3].wait_recv()

    def wait_far(self):
        self.far_right.wait_recv()
        self.far_left.wait_recv()


def opening_kernel(
    tok_ref, tw_ref, ck_ref, cv_ref, cg_ref, vec_ref,
    r_ref, k_ref, v_ref, g_ref, set_ref, time_ref, prev_ref, delta_ref, stripe_ref,
    tokens, time, mix, prev, delta, vec_blocks, vec_stripe, vec_all, send, recv, local,
):
    place, member, far, near, far_devices, near_devices = cube_places()
    z, x, y, c = [lax.axis_index(name) for name in ("z", "x", "y", "core")]
    greet(far_devices + near_devices)
    copy = Copies(send, recv)
    own = tw_ref.shape[2] // 8
    wide = ck_ref.shape[1] // 8

    def lanes(p, size):
        return pl.ds(pl.multiple_of(p * size, size), size)

    def tile(p):
        return pl.ds(pl.multiple_of(p * 16, 16), 16)

    vec_near = [copy(vec_ref, vec_blocks.at[n], d) for n, d in enumerate(near_devices)]
    for one in vec_near:
        one.start()
    time_near = [
        copy(tw_ref.at[:, :, lanes(p, own)], time.at[:, z, x, tile(member), :], d) for p, d in zip(near, near_devices)
    ]
    for one in time_near:
        one.start()
    time_own = pltpu.make_async_copy(tw_ref.at[:, :, lanes(member, own)], time.at[:, z, x, tile(member), :], local.at[0])
    time_own.start()
    tokens[member] = tok_ref[...]
    gathered = Tokens(copy, tokens, member)
    to_next = {"x": lax.rem(x + 1, 4)}
    last_rows = [pl.ds(s * BLOCK_LEN + BLOCK_LEN - 16, 16) for s in range(2)]
    edges = [copy(tokens.at[7, rows], tokens.at[8, rows], to_next) for rows in last_rows]

    total = vec_ref[...].astype(jnp.float32)
    for n, one in enumerate(vec_near):
        one.wait_recv()
        total = total + vec_blocks[n].astype(jnp.float32)
    vec_stripe[...] = total.astype(low)
    vec_all[place] = vec_stripe[...]
    vec_far = [copy(vec_stripe, vec_all.at[place], d) for d in far_devices]
    for one in vec_far:
        one.start()

    for one in time_near:
        one.wait_recv()
    time_own.wait()
    one_side, other_side = pl.ds(0, own // 2), pl.ds(own // 2, own // 2)
    rows = time.shape[3] // 2
    z_first = Ring(copy, "z", lambda at, n: time.at[:, at, x, pl.ds(n * rows, rows), one_side])
    x_first = Ring(copy, "x", lambda at, n: time.at[:, z, at, pl.ds(n * rows, rows), other_side])
    gathered.ring.forward()
    z_first.forward()
    x_first.forward()
    z_first.wait_near()
    z_first.wait_far()
    x_last = Ring(copy, "x", lambda at, n: time.at[:, pl.ds(n * 2, 2), at, :, one_side])
    x_first.wait_near()
    x_first.wait_far()
    z_last = Ring(copy, "z", lambda at, n: time.at[:, at, pl.ds(n * 2, 2), :, other_side])
    for one in vec_far:
        one.wait_recv()
    for n in range(16):
        set_ref[:, n * 128 : (n + 1) * 128] = vec_all[n].astype(jnp.float32)
    gathered.wait_next()

    channel = []
    for source, size, start in ((ck_ref, wide, 0), (cv_ref, wide, wide), (cg_ref, own, 2 * wide)):
        for p, d in zip(near, near_devices):
            channel.append(copy(source.at[:, lanes(p, size)], stripe_ref.at[tile(member), pl.ds(start, size)], d))
    for one in channel:
        one.start()
    kept = [
        pltpu.make_async_copy(source.at[:, lanes(member, size)], stripe_ref.at[tile(member), pl.ds(start, size)], local.at[n])
        for n, (source, size, start) in enumerate(((ck_ref, wide, 0), (cv_ref, wide, wide), (cg_ref, own, 2 * wide)))
    ]
    for one in kept:
        one.start()

    width = tok_ref.shape[1]
    step = 512
    row = lax.broadcasted_iota(jnp.int32, (16, step), 0)

    def statistics(values):
        mean = jnp.mean(values, axis=-1, keepdims=True)
        center = values - mean
        return mean, lax.rsqrt(jnp.mean(center * center, axis=-1, keepdims=True) + epsilon)

    def mix_pair(q):
        @pl.when(q == 0)
        def _():
            for one in edges:
                one.wait_recv()

        def mix_block(b, carry):
            j = q * 2 + b
            before_slot = jnp.where(j == 0, 8, j - 1)
            hidden = jnp.logical_and(j == 0, x == 0)
            for s in range(2):
                last = slice(s * BLOCK_LEN + BLOCK_LEN - 16, (s + 1) * BLOCK_LEN)
                found = [statistics(tokens[before_slot, last].astype(jnp.float32))]
                found[0] = (found[0][0][15:16], found[0][1][15:16])
                for t in range(BLOCK_LEN // 16):
                    at = s * BLOCK_LEN + t * 16
                    found.append(statistics(tokens[j, at : at + 16].astype(jnp.float32)))

                def columns(n, carry):
                    cols = pl.ds(pl.multiple_of(n * step, step), step)
                    gain, offset = set_ref[0:1, cols], set_ref[1:2, cols]
                    before = tokens[before_slot, last, cols].astype(jnp.float32)[15:16]
                    before = (before - found[0][0]) * found[0][1] * gain + offset
                    before = jnp.where(hidden, 0.0, before)
                    for t in range(BLOCK_LEN // 16):
                        at = s * BLOCK_LEN + t * 16
                        mean, inverse = found[t + 1]
                        norm = (tokens[j, at : at + 16, cols].astype(jnp.float32) - mean) * inverse * gain + offset
                        moved = jnp.where(row == 0, before, pltpu.roll(norm, 1, 0))
                        before = norm[15:16]
                        gap = norm - moved
                        to = pl.ds(pl.multiple_of(j * 2 * BLOCK_LEN + at, 16), 16)
                        prev[to, cols] = moved.astype(low)
                        delta[to, cols] = gap.astype(low)
                        for p in range(4):
                            mix[p, to, cols] = (moved + set_ref[2 + p : 3 + p, cols] * gap).astype(low)
                    return carry

                lax.fori_loop(0, width // step, columns, 0)
            return carry

        lax.fori_loop(0, 2, mix_block, 0)

    gathered.wait_passed()

    @pl.when(y != 1)
    def _():
        for one in edges:
            one.start()

    mix_pair(gathered.ring.right)
    x_last.forward()
    z_last.forward()
    mix_pair(y)
    gathered.far_pair()

    @pl.when(y == 1)
    def _():
        for one in edges:
            one.start()

    mix_pair(gathered.ring.far)
    mix_pair(gathered.ring.left)
    prev_out = pltpu.make_async_copy(prev, prev_ref, local.at[3])
    prev_out.start()
    delta_out = pltpu.make_async_copy(delta, delta_ref, local.at[4])
    delta_out.start()
    for ring in (x_last, z_last):
        ring.wait_near()
        ring.wait_far()
    time_out = pltpu.make_async_copy(time, time_ref, local.at[5])
    time_out.start()

    def project(n, carry):
        to = pl.ds(pl.multiple_of(n * 256, 256), 256)
        for p, out in enumerate((r_ref, k_ref, v_ref, g_ref)):
            out[to] = nn(mix[p, to], time[p].reshape(16 * 128, own)).astype(out.dtype)
        return carry

    lax.fori_loop(0, 4, project, 0)
    for one in channel:
        one.wait_recv()
    copy.wait_sent()
    for one in kept + [prev_out, delta_out, time_out]:
        one.wait()


def opening(tokens, time_weights, channel_key, channel_value, channel_gate, vector_block, cid):
    rows, width = tokens.shape
    own = width // 8
    stripe = 2 * (channel_key.shape[1] // 8) + own
    shape = jax.ShapeDtypeStruct
    return pl.pallas_call(
        opening_kernel,
        name="opening",
        cost_estimate=cost(60),
        out_shape=[
            shape((8 * rows, own), low),
            shape((8 * rows, own), low),
            shape((8 * rows, own), low),
            shape((8 * rows, own), jnp.float32),
            shape((16, width), jnp.float32),
            shape((5, 4, 4, 128, own), low),
            shape((8 * rows, width), low),
            shape((8 * rows, width), low),
            shape((128, stripe), low),
        ],
        in_specs=[VMEM] * 6,
        out_specs=[VMEM] * 5 + [HBM] * 4,
        scratch_shapes=[
            pltpu.VMEM((9, rows, width), low),
            pltpu.VMEM((5, 4, 4, 128, own), low),
            pltpu.VMEM((4, 8 * rows, width), low),
            pltpu.VMEM((8 * rows, width), low),
            pltpu.VMEM((8 * rows, width), low),
            pltpu.VMEM((7, 16, 128), low),
            pltpu.VMEM((16, 128), low),
            pltpu.VMEM((16, 16, 128), low),
            pltpu.SemaphoreType.DMA((88,)),
            pltpu.SemaphoreType.DMA((88,)),
            pltpu.SemaphoreType.DMA((6,)),
        ],
        compiler_params=pltpu.CompilerParams(collective_id=cid, has_side_effects=True, vmem_limit_bytes=56 * 2**20),
    )(tokens, time_weights, channel_key, channel_value, channel_gate, vector_block)


class Scatter:
    def __init__(self, copy, p, out, from_sibling, mid, from_left, from_right, end_left, end_right):
        y, self.c, right, left, far = ring_places()
        self.order = (far, right, left, y)
        self.copy, self.p, self.out, self.from_sibling, self.mid = copy, p, out, from_sibling, mid
        self.from_left, self.from_right, self.end_left, self.end_right = from_left, from_right, end_left, end_right
        self.to_sibling, self.to_right, self.to_left = {"core": 1 - self.c}, {"y": right}, {"y": left}
        half = p.shape[1] // 2
        self.first, self.last = pl.ds(0, half), pl.ds(half, half)
        self.near = [None] * 4

    def send(self, src, dst, device):
        one = self.copy(src, dst, device)
        one.start()
        return one

    def share(self, k):
        self.near[k] = self.send(self.p.at[self.order[k] * 2 + 1 - self.c], self.from_sibling.at[k], self.to_sibling)

    def summed(self, k, rows):
        own = self.p[self.order[k] * 2 + self.c, rows].astype(jnp.float32)
        return own + self.from_sibling[k, rows].astype(jnp.float32)

    def far_out(self):
        self.near[0].wait_recv()
        self.mid[0] = self.summed(0, slice(None)).astype(low)
        self.far_right = self.send(self.mid.at[0, self.first], self.from_left, self.to_right)
        self.far_left = self.send(self.mid.at[0, self.last], self.from_right, self.to_left)

    def right_b(self):
        self.near[1].wait_recv()
        self.mid[1, self.last] = self.summed(1, self.last).astype(low)
        self.last_right = self.send(self.mid.at[1, self.last], self.end_left.at[self.last], self.to_right)

    def left_b(self):
        self.near[2].wait_recv()
        self.mid[2, self.first] = self.summed(2, self.first).astype(low)
        self.first_left = self.send(self.mid.at[2, self.first], self.end_right.at[self.first], self.to_left)

    def right_a(self):
        self.far_right.wait_recv()
        value = self.summed(1, self.first) + self.from_left[...].astype(jnp.float32)
        self.mid[1, self.first] = value.astype(low)
        self.first_right = self.send(self.mid.at[1, self.first], self.end_left.at[self.first], self.to_right)

    def left_a(self):
        self.far_left.wait_recv()
        value = self.summed(2, self.last) + self.from_right[...].astype(jnp.float32)
        self.mid[2, self.last] = value.astype(low)
        self.last_left = self.send(self.mid.at[2, self.last], self.end_right.at[self.last], self.to_left)

    def finish(self):
        self.near[3].wait_recv()
        self.last_right.wait_recv()
        self.first_left.wait_recv()
        self.first_right.wait_recv()
        self.last_left.wait_recv()
        from_ring = self.end_left[...].astype(jnp.float32) + self.end_right[...].astype(jnp.float32)
        self.out[...] = self.summed(3, slice(None)) + from_ring


def scatter_scratch(rows, cols):
    return [
        pltpu.VMEM((4, rows, cols), low),
        pltpu.VMEM((3, rows, cols), low),
        pltpu.VMEM((rows // 2, cols), low),
        pltpu.VMEM((rows // 2, cols), low),
        pltpu.VMEM((rows, cols), low),
        pltpu.VMEM((rows, cols), low),
    ]


def group_and_line():
    x = lax.axis_index("x")
    place, member, far, near, far_devices, near_devices = cube_places()
    return x, member, near, near_devices, {"x": lax.rem(x + 1, 4)}, {"x": lax.rem(x + 3, 4)}


class Tokens:
    def __init__(self, copy, slots, member):
        c = lax.axis_index("core")
        half = slots.shape[1] // 2
        self.copy, self.c, self.slots, self.to_sibling = copy, c, slots, {"core": 1 - c}
        self.ring = Ring(copy, "y", lambda at, n: slots.at[at * 2 + c, pl.ds(n * half, half)])
        self.near = copy(slots.at[member], slots.at[member], self.to_sibling)
        self.near.start()

    def pass_on(self, at):
        one = self.copy(self.slots.at[at * 2 + self.c], self.slots.at[at * 2 + self.c], self.to_sibling)
        one.start()
        return one

    def wait_next(self):
        self.ring.wait_near()
        self.passed = [self.pass_on(self.ring.right), self.pass_on(self.ring.left)]

    def wait_passed(self):
        self.near.wait_recv()
        for one in self.passed:
            one.wait_recv()

    def next_pairs(self):
        self.ring.forward()
        self.wait_next()
        self.wait_passed()

    def far_pair(self):
        self.ring.wait_far()
        self.passed.append(self.pass_on(self.ring.far))
        self.passed[-1].wait_recv()

    def copies(self):
        return self.ring.near + [self.ring.far_right, self.ring.far_left, self.near] + self.passed


class Blend:
    def __init__(self, copy, terms, coefficients, delta, p, sums, firsts, to_previous):
        self.terms, self.coefficients, self.delta, self.p, self.sums, self.firsts = terms, coefficients, delta, p, sums, firsts
        self.edge = copy(firsts.at[0], firsts.at[4], to_previous)
        self.row = lax.broadcasted_iota(jnp.int32, (16, p.shape[2]), 0)

    def pair(self, q):
        for s in range(2):
            after = jnp.zeros((1, self.p.shape[2]), jnp.float32)
            for b in (1, 0):

                def slab(t, following):
                    at = s * BLOCK_LEN + (BLOCK_LEN // 16 - 1 - t) * 16
                    rows = pl.ds(pl.multiple_of(b * 2 * BLOCK_LEN + at, 16), 16)
                    gap = self.delta[pl.ds(pl.multiple_of(q * 4 * BLOCK_LEN + b * 2 * BLOCK_LEN + at, 16), 16)]
                    gap = gap.astype(jnp.float32)
                    here, whole = 0.0, 0.0
                    for n, coefficient in enumerate(self.coefficients):
                        term = self.terms[n, rows]
                        here = here + coefficient * term
                        whole = whole + term
                        product = gap * term
                        self.sums[n] += product[:8] + product[8:]
                    behind = whole - here
                    moved = jnp.where(self.row == 15, following, pltpu.roll(behind, 15, 0))
                    self.p[q * 2 + b, pl.ds(pl.multiple_of(at, 16), 16)] = (here + moved).astype(low)
                    return behind[0:1]

                after = lax.fori_loop(0, BLOCK_LEN // 16, slab, after)
            self.firsts[q, s, 0:1, :] = after

        @pl.when(q == 0)
        def _():
            self.edge.start()

    def close(self, q):
        @pl.when(q == 3)
        def _():
            self.edge.wait_recv()

        for s in range(2):
            following = self.firsts[q + 1, s, 0:1, :]
            following = jnp.where(jnp.logical_and(q == 3, lax.axis_index("x") == 3), 0.0, following)
            rows = slice(s * BLOCK_LEN + BLOCK_LEN - 16, (s + 1) * BLOCK_LEN)
            value = self.p[q * 2 + 1, rows].astype(jnp.float32)
            self.p[q * 2 + 1, rows] = (value + jnp.where(self.row == 15, following, 0.0)).astype(low)


def channel_kernel(
    own_ref, hidden_ref, up_ref, w_hbm, set_ref,
    out_ref, grad_ref, sums_ref, dw_ref,
    slots, w, ckey, cgate, delta, rect, hidden, gown, pre, gg, gg_own, gkey, terms, p, value, sums, firsts, dw,
    from_sibling, mid, from_left, from_right, end_left, end_right, send, recv, local,
):
    x, member, near, near_devices, to_next, to_previous = group_and_line()
    y, c, right, left, far = ring_places()
    firsts[0:4] = jnp.zeros_like(firsts[0:4])
    sums[...] = jnp.zeros_like(sums)
    greet(near_devices + [to_next, to_previous])
    copy = Copies(send, recv)
    load = pltpu.make_async_copy(w_hbm, w, local.at[0])
    load.start()
    slots[member] = own_ref[...]
    gathered = Tokens(copy, slots, member)
    wide = rect.shape[1]
    cols = gown.shape[2]
    row = lax.broadcasted_iota(jnp.int32, (16, own_ref.shape[1]), 0)
    edges = [
        copy(slots.at[7, pl.ds(s * BLOCK_LEN + BLOCK_LEN - 16, 16)], slots.at[8, pl.ds(s * BLOCK_LEN + BLOCK_LEN - 16, 16)], to_next)
        for s in range(2)
    ]

    def compute(q):
        @pl.when(q == 0)
        def _():
            for one in edges:
                one.wait_recv()

        for b in range(2):
            j = q * 2 + b
            for s in range(2):
                before = slots[jnp.where(j == 0, 8, j - 1), s * BLOCK_LEN + BLOCK_LEN - 16 : (s + 1) * BLOCK_LEN]
                before = before.astype(jnp.float32)[15:16]
                before = jnp.where(jnp.logical_and(j == 0, x == 0), 0.0, before)

                def slab(t, previous):
                    at = s * BLOCK_LEN + t * 16
                    values = slots[j, pl.ds(pl.multiple_of(at, 16), 16)].astype(jnp.float32)
                    moved = jnp.where(row == 0, previous, pltpu.roll(values, 1, 0))
                    gap = values - moved
                    to = pl.ds(pl.multiple_of(j * 2 * BLOCK_LEN + at, 16), 16)
                    delta[to] = gap.astype(low)
                    ckey[to] = (moved + set_ref[11:12, :] * gap).astype(low)
                    cgate[to] = (moved + set_ref[12:13, :] * gap).astype(low)
                    return values[15:16]

                lax.fori_loop(0, BLOCK_LEN // 16, slab, before)
        rows = pl.ds(pl.multiple_of(q * 256, 256), 256)
        kept = jnp.maximum(nn(ckey[rows], w[:, :wide]), 0.0)
        rect[rows] = kept.astype(low)
        hidden[rows] = (kept * kept).astype(low)
        part = nt(hidden[rows], w[:, wide : 2 * wide]).astype(low)
        early = nn(cgate[rows], w[:, 2 * wide :]).astype(low)
        for b in range(2):
            p[q * 2 + b] = part[b * 128 : (b + 1) * 128]
            gown[q * 2 + b] = early[b * 128 : (b + 1) * 128]

    gates = []

    def give_gate(j):
        one = copy(gown.at[j], pre.at[member], {"y": j // 2, "core": lax.rem(j, 2)})
        one.start()
        gates.append(one)

    buffers = (from_sibling, mid, from_left, from_right, end_left, end_right)
    total = Scatter(copy, p, value, *buffers)
    gathered.next_pairs()

    @pl.when(y != 1)
    def _():
        for one in edges:
            one.start()

    load.wait()
    compute(right)
    total.share(1)
    compute(y)
    total.share(3)
    gathered.far_pair()

    @pl.when(y == 1)
    def _():
        for one in edges:
            one.start()

    copy.wait_sent(edges)
    for turn in range(2):
        give_gate(right * 2 + lax.rem(c + turn, 2))
    give_gate(y * 2 + 1 - c)
    compute(far)
    total.share(0)
    total.right_b()
    compute(left)
    copy.wait_sent(gathered.copies())
    total.share(2)
    total.far_out()
    total.left_b()
    for at in (left, far):
        for turn in range(2):
            give_gate(at * 2 + lax.rem(c + turn, 2))
    pre[member] = gown[member]
    total.right_a()
    total.left_a()
    total.finish()
    for one in gates:
        one.wait_recv()
    copy.wait_sent()

    def gate_block(n, carry):
        at = pl.ds(pl.multiple_of(n * cols, cols), cols)
        gate = jax.nn.sigmoid(pre[n].astype(jnp.float32))
        up = up_ref[:, at].astype(jnp.float32)
        out_ref[:, at] = (hidden_ref[:, at] + gate * value[:, at]).astype(low)
        slots[member, :, at] = (up * gate).astype(low)
        gg_own[n] = (up * value[:, at] * gate * (1.0 - gate)).astype(low)
        return carry

    lax.fori_loop(0, 8, gate_block, 0)

    gathered = Tokens(copy, slots, member)
    gates = [copy(gg_own.at[at], gg.at[member], d) for at, d in zip(near, near_devices)]
    for one in gates:
        one.start()
    gg[member] = gg_own[member]
    blend = Blend(copy, terms, [set_ref[11:12, :], set_ref[12:13, :]], delta, p, sums, firsts, to_previous)

    def compute_back(q):
        rows = pl.ds(pl.multiple_of(q * 256, 256), 256)
        pair = pl.ds(q * 2, 2)
        grad_hidden = nn(slots[pair].reshape(256, slots.shape[2]), w[:, wide : 2 * wide])
        gkey[rows] = (2.0 * grad_hidden * rect[rows].astype(jnp.float32)).astype(low)
        terms[0] = nt(gkey[rows], w[:, :wide])
        terms[1] = nt(gg[pair].reshape(256, cols), w[:, 2 * wide :])
        blend.pair(q)

    total = Scatter(copy, p, grad_ref, *buffers)
    gathered.next_pairs()
    for one in gates:
        one.wait_recv()
    compute_back(y)
    compute_back(right)
    blend.close(y)
    total.share(3)
    compute_back(left)
    blend.close(left)
    total.share(2)
    gathered.far_pair()
    total.left_b()
    compute_back(far)
    blend.close(far)
    total.share(0)
    blend.close(right)
    total.share(1)
    total.far_out()
    total.right_b()

    def give(block, slot):
        at = pl.ds(pl.multiple_of(block * 256, 256), 256)
        return pltpu.make_async_copy(dw.at[slot], dw_ref.at[at], local.at[1 + slot])

    def weight_blocks(n, carry):
        for slot in range(2):
            block = n * 2 + slot
            at = pl.ds(pl.multiple_of(block * 256, 256), 256)

            @pl.when(n > 0)
            def _():
                give(block - 2, slot).wait()

            dw[slot, :, :wide] = tn(ckey[:, at], gkey[...]).astype(low)
            dw[slot, :, wide : 2 * wide] = tn(slots[0:8, :, at].reshape(8 * 128, 256), hidden[...]).astype(low)
            dw[slot, :, 2 * wide :] = tn(cgate[:, at], gg[...].reshape(8 * 128, cols)).astype(low)
            give(block, slot).start()
        return carry

    lax.fori_loop(0, 2, weight_blocks, 0)
    total.right_a()
    total.left_a()
    lax.fori_loop(2, 4, weight_blocks, 0)
    for n in range(2):
        sums_ref[n : n + 1, :] = jnp.sum(sums[n], axis=0, keepdims=True)
    sums_ref[2:8, :] = jnp.zeros((6, sums_ref.shape[1]), jnp.float32)
    total.finish()
    copy.wait_sent()
    for slot in range(2):
        give(6 + slot, slot).wait()


def channel(own, hidden_one, upstream, weights, settings, cid):
    rows, width = own.shape
    cols = width // 8
    wide = (weights.shape[1] - cols) // 2
    shape = jax.ShapeDtypeStruct
    big = pltpu.VMEM((8 * rows, width), low)
    mid = pltpu.VMEM((8 * rows, wide), low)
    small = pltpu.VMEM((8, rows, cols), low)
    return pl.pallas_call(
        channel_kernel,
        name="channel",
        cost_estimate=cost(120),
        out_shape=[
            shape((rows, width), low),
            shape((rows, width), jnp.float32),
            shape((8, width), jnp.float32),
            shape(weights.shape, low),
        ],
        in_specs=[VMEM] * 3 + [HBM, VMEM],
        out_specs=[VMEM] * 3 + [HBM],
        scratch_shapes=[
            pltpu.VMEM((9, rows, width), low),
            pltpu.VMEM(weights.shape, low),
            big,
            big,
            big,
            mid,
            mid,
            small,
            small,
            small,
            small,
            mid,
            pltpu.VMEM((2, 256, width), jnp.float32),
            pltpu.VMEM((8, rows, width), low),
            pltpu.VMEM((rows, width), jnp.float32),
            pltpu.VMEM((2, 8, width), jnp.float32),
            pltpu.VMEM((5, 2, 8, width), jnp.float32),
            pltpu.VMEM((2, 256, weights.shape[1]), low),
            *scatter_scratch(rows, width),
            pltpu.SemaphoreType.DMA((70,)),
            pltpu.SemaphoreType.DMA((70,)),
            pltpu.SemaphoreType.DMA((3,)),
        ],
        compiler_params=pltpu.CompilerParams(collective_id=cid, has_side_effects=True, vmem_limit_bytes=59 * 2**20),
    )(own, hidden_one, upstream, weights, settings)


def middle_kernel(
    second_ref, hidden_ref, up_ref, set_ref, column_ref, params_ref,
    g_ref, scaled_ref, inverse_ref, r_ref, k_ref, v_ref, w_ref, in_ref, time_hbm, prev_hbm, delta_hbm, gated_hbm,
    upper_ref, proj_ref, vec_ref, sums_ref, dw_ref,
    time, prev, delta, gated, out, out_all, p, gg, dw, norm_sums, part_k, part_v, suffix, total, slots, sums,
    from_sibling, mid, from_left, from_right, end_left, end_right, send, recv, local,
):
    x, member, near, near_devices, _, _ = group_and_line()
    y, c, right, left, far = ring_places()
    greet(near_devices + [{"x": lax.rem(x + n, 4)} for n in range(1, 4)])
    copy = Copies(send, recv)
    cols = g_ref.shape[1]
    loads = [
        pltpu.make_async_copy(src, dst, local.at[n])
        for n, (src, dst) in enumerate(
            ((time_hbm.at[3:5], time), (gated_hbm, gated), (prev_hbm, prev), (delta_hbm, delta))
        )
    ]
    for one in loads:
        one.start()

    norm_sums[...] = jnp.zeros_like(norm_sums)

    def norm_rows(t, carry):
        rows = pl.ds(pl.multiple_of(t * 16, 16), 16)
        values = hidden_ref[rows]
        center = values - jnp.mean(values, axis=-1, keepdims=True)
        inverse = lax.rsqrt(jnp.mean(center * center, axis=-1, keepdims=True) + epsilon)
        unit = center * inverse
        grad = second_ref[rows]
        product = grad * unit
        norm_sums[0] += product[:8] + product[8:]
        norm_sums[1] += grad[:8] + grad[8:]
        inner = grad * set_ref[9:10, :]
        mean = jnp.mean(inner, axis=-1, keepdims=True)
        along = jnp.mean(inner * unit, axis=-1, keepdims=True)
        upper = up_ref[rows].astype(jnp.float32) + inverse * (inner - mean - unit * along)
        upper_ref[rows] = upper
        for n in range(8):
            out[n, rows] = upper[:, n * cols : (n + 1) * cols].astype(low)
        return carry

    lax.fori_loop(0, 8, norm_rows, 0)
    given = [copy(out.at[at], out_all.at[member], d) for at, d in zip(near, near_devices)]
    for one in given:
        one.start()
    out_all[member] = out[member]
    for n in range(2):
        vec_ref[n : n + 1, :] = jnp.sum(norm_sums[n], axis=0, keepdims=True)
    vec_ref[3:8, :] = jnp.zeros((5, vec_ref.shape[1]), jnp.float32)
    sums[...] = jnp.zeros_like(sums)
    for one in loads:
        one.wait()
    for one in given:
        one.wait_recv()

    def through(q):
        for b in range(2):
            m = q * 2 + b
            rows = pl.ds(pl.multiple_of(m * cols, cols), cols)
            p[m] = nt(out_all[...].reshape(8 * 128, cols), time[1, rows]).astype(low)

    def out_block(m, carry):
        rows = pl.ds(pl.multiple_of(m * cols, cols), cols)
        dw[rows, cols : 2 * cols] = tn(gated[m], out_all[...].reshape(8 * 128, cols)).astype(low)
        return carry

    total_gg = Scatter(copy, p, gg, from_sibling, mid, from_left, from_right, end_left, end_right)
    through(far)
    total_gg.share(0)
    through(right)
    total_gg.share(1)
    through(left)
    total_gg.share(2)
    total_gg.far_out()
    total_gg.right_b()
    total_gg.left_b()
    through(y)
    total_gg.share(3)
    lax.fori_loop(0, 4, out_block, 0)
    total_gg.right_a()
    total_gg.left_a()
    lax.fori_loop(4, 8, out_block, 0)
    total_gg.finish()

    log_row, bonus, gain, bias = [params_ref[n : n + 1, :] for n in range(4)]
    mask, eye, enter, leave, same = head_tables(log_row)
    block_decay = jnp.exp(BLOCK_LEN * log_row)
    ones = jnp.where(same, 1.0, 0.0).astype(low)

    def first(m, carry):
        for s in range(2):
            rows = block_rows(m, s)
            gate, grad, scaled = g_ref[rows], gg[rows], scaled_ref[rows]
            sigma = jax.nn.sigmoid(gate)
            grad_normed = grad * gate * sigma
            proj_ref[3, rows] = (grad * (scaled * gain + bias) * sigma * (1.0 + gate * (1.0 - sigma))).astype(low)
            inner = grad_normed * gain
            wide = inverse_ref[rows] * (inner - head_mean(inner, same) - scaled * head_mean(inner * scaled, same))
            grad_wkv = wide.astype(low)
            r, k, v = r_ref[rows], k_ref[rows], v_ref[rows]
            r_wide, k_wide = r.astype(jnp.float32), k.astype(jnp.float32)
            grad_weights = nt(grad_wkv, expand(v, same)).astype(low).astype(jnp.float32)
            masked = (grad_weights * mask).astype(low)
            own = nn(jnp.where(eye, grad_weights, 0.0).astype(low), ones)
            grad_r = nn(masked, expand(k, same)) + own * bonus * k_wide
            grad_r = grad_r + nt(grad_wkv, expand(in_ref[m * 2 + s], same)) * enter
            proj_ref[0, rows] = grad_r.astype(low)
            part_k[rows] = compress(tn(masked, r), same) + own * bonus * r_wide
            part_v[rows] = compress(tn(w_ref[rows], grad_wkv), same)
            suffix[m * 2 + s] = compress(tn((r_wide * enter).astype(low), grad_wkv), same)
            sums[0] += own * r_wide * k_wide
            sums[1] += grad_normed * scaled
            sums[2] += grad_normed
        return carry

    lax.fori_loop(0, 8, first, 0)

    def chain(n, states):
        m = 7 - n
        after = []
        for s in range(2):
            here = suffix[m * 2 + s]
            suffix[m * 2 + s] = states[s]
            after.append(states[s] * block_decay + here)
        return tuple(after)

    zero = jnp.zeros(enter.shape, jnp.float32)
    states = lax.fori_loop(0, 8, chain, (zero, zero))
    for s in range(2):
        total[s] = states[s]
    line = start_line(total, slots, send.at[pl.ds(40, 3)], recv.at[pl.ds(40, 3)])

    def gate_block(n, carry):
        rows = pl.ds(pl.multiple_of(n * cols, cols), cols)
        by_delta = tn(delta[:, rows], proj_ref[3])
        column = column_ref[rows]
        grads = tn(prev[:, rows], proj_ref[3]) + column[:, 5:6] * by_delta
        dw[rows, :cols] = grads.astype(low)
        product = (time[0, rows].astype(jnp.float32) * by_delta).astype(low)
        vec_ref[2:3, rows] = nt(jnp.ones((8, cols), low), product)[0:1]
        return carry

    lax.fori_loop(0, 8, gate_block, 0)
    give = pltpu.make_async_copy(dw, dw_ref, local.at[4])
    give.start()
    for one in line:
        one.wait()
    x_place = lax.axis_index("x")
    leaving = [zero, zero]
    span_decay = jnp.exp(8.0 * BLOCK_LEN * log_row)
    for x in (3, 2, 1):
        for s in range(2):
            leaving[s] = jnp.where(x > x_place, leaving[s] * span_decay + slots[x, s], leaving[s])
    for s in range(2):
        total[s] = leaving[s]

    def second(m, carry):
        power = jnp.exp(((7 - m) * BLOCK_LEN).astype(jnp.float32) * log_row)
        for s in range(2):
            rows = block_rows(m, s)
            state = expand((suffix[m * 2 + s] + power * total[s]).astype(low), same)
            key_leave = (k_ref[rows].astype(jnp.float32) * leave).astype(low)
            proj_ref[1, rows] = (part_k[rows] + nt(v_ref[rows], state) * leave).astype(low)
            proj_ref[2, rows] = (part_v[rows] + nn(key_leave, state)).astype(low)
        return carry

    lax.fori_loop(0, 8, second, 0)


    for n in range(3):
        sums_ref[n : n + 1, :] = jnp.sum(sums[n], axis=0, keepdims=True)
    sums_ref[3:8, :] = jnp.zeros((5, cols), jnp.float32)
    copy.wait_sent()
    give.wait()


def middle(second, hidden, up, settings, columns, params, g, scaled, inverse, r, k, v, w, states, time, prev, delta, gated, cid):
    rows, width = second.shape
    cols = g.shape[1]
    tall = pltpu.VMEM((8 * rows, cols), jnp.float32)
    shape = jax.ShapeDtypeStruct
    return pl.pallas_call(
        middle_kernel,
        name="middle",
        out_shape=[
            shape((rows, width), jnp.float32),
            shape((4, 8 * rows, cols), low),
            shape((8, width), jnp.float32),
            shape((8, cols), jnp.float32),
            shape((width, 2 * cols), low),
        ],
        in_specs=[VMEM] * 14 + [HBM] * 4,
        out_specs=[VMEM] * 4 + [HBM],
        scratch_shapes=[
            pltpu.VMEM((2, width, cols), low),
            pltpu.VMEM(prev.shape, low),
            pltpu.VMEM(delta.shape, low),
            pltpu.VMEM(gated.shape, low),
            pltpu.VMEM((8, rows, cols), low),
            pltpu.VMEM((8, rows, cols), low),
            pltpu.VMEM((8, 8 * rows, cols), low),
            tall,
            pltpu.VMEM((width, 2 * cols), low),
            pltpu.VMEM((2, 8, width), jnp.float32),
            tall,
            tall,
            pltpu.VMEM((16, BLOCK_LEN, cols), jnp.float32),
            pltpu.VMEM((2, BLOCK_LEN, cols), jnp.float32),
            pltpu.VMEM((4, 2, BLOCK_LEN, cols), jnp.float32),
            pltpu.VMEM((3, BLOCK_LEN, cols), jnp.float32),
            *scatter_scratch(8 * rows, cols),
            pltpu.SemaphoreType.DMA((43,)),
            pltpu.SemaphoreType.DMA((43,)),
            pltpu.SemaphoreType.DMA((5,)),
        ],
        compiler_params=pltpu.CompilerParams(collective_id=cid, has_side_effects=True, vmem_limit_bytes=58 * 2**20),
    )(second, hidden, up, settings, columns, params, g, scaled, inverse, r, k, v, w, states, time, prev, delta, gated)


class RingScatter:
    def __init__(self, copy, axis, part, halves, bufs):
        me = lax.axis_index(axis)
        right, left, self.far = [lax.rem(me + k, 4) for k in (1, 3, 2)]
        self.me, self.right, self.left, self.part, self.halves, self.copy = me, right, left, part, halves, copy
        self.to_right, self.to_left = {axis: right}, {axis: left}
        self.from_left, self.from_right, self.end_left, self.end_right = bufs

    def send(self, src, dst, device):
        one = self.copy(src, dst, device)
        one.start()
        return one

    def far_out(self):
        first, last = self.halves
        self.far_right = self.send(self.part(self.far).at[first], self.from_left, self.to_right)
        self.far_left = self.send(self.part(self.far).at[last], self.from_right, self.to_left)

    def near_out(self):
        first, last = self.halves
        self.last_right = self.send(self.part(self.right).at[last], self.end_left.at[last], self.to_right)
        self.first_left = self.send(self.part(self.left).at[first], self.end_right.at[first], self.to_left)

    def pass_on(self):
        first, last = self.halves
        self.far_right.wait_recv()
        here = self.part(self.right).at[first]
        here[...] = (here[...].astype(jnp.float32) + self.from_left[...].astype(jnp.float32)).astype(low)
        self.first_right = self.send(here, self.end_left.at[first], self.to_right)
        self.far_left.wait_recv()
        here = self.part(self.left).at[last]
        here[...] = (here[...].astype(jnp.float32) + self.from_right[...].astype(jnp.float32)).astype(low)
        self.last_left = self.send(here, self.end_right.at[last], self.to_left)

    def finish(self, out):
        for one in (self.last_right, self.first_left, self.first_right, self.last_left):
            one.wait_recv()
        value = self.part(self.me)[...].astype(jnp.float32) + self.end_left[...].astype(jnp.float32)
        out[...] = (value + self.end_right[...].astype(jnp.float32)).astype(low)


def closing_kernel(
    grad_ref, early_hbm, time_hbm, prev_hbm, delta_hbm, set_ref, column_ref, tok_ref, upper_ref, vec_ref,
    token_ref, weight_ref, total_ref,
    time, scaled, prev, delta, early, terms, p, firsts, one_dw, other_dw, one_sum, other_sum, stripe, gathered, parts,
    one_a, one_b, one_c, one_d, other_a, other_b, other_c, other_d,
    one_e, one_f, one_g, one_h, other_e, other_f, other_g, other_h,
    early_a, early_b, early_c, early_d, early_e, early_f, early_g, early_h,
    early_i, early_j, early_k, early_l, early_m, early_n, early_o, early_p, early_one, early_other, vec_far, vec_near, vec_stripe, first_grad, norm_sums,
    from_sibling, mid, from_left, from_right, end_left, end_right, send, recv, local,
):
    place, member, far_places, near_members, far_devices, near_devices = cube_places()
    x = lax.axis_index("x")
    y, c, right, left, far = ring_places()
    to_previous = {"x": lax.rem(x + 3, 4)}
    firsts[0:4] = jnp.zeros_like(firsts[0:4])
    greet(far_devices + near_devices)
    copy = Copies(send, recv)
    cols = grad_ref.shape[2]
    loads = [
        pltpu.make_async_copy(src, dst, local.at[n])
        for n, (src, dst) in enumerate(
            ((early_hbm, early), (prev_hbm, prev), (delta_hbm, delta), (time_hbm.at[0:4], time))
        )
    ]
    for one in loads:
        one.start()
    slots = (pl.ds(0, 2), pl.ds(2, 2))
    halves = (pl.ds(0, 64), pl.ds(64, 64))
    side = early.shape[3] // 2
    loads[0].wait()
    early_z = RingScatter(copy, "z", lambda at: early.at[at, :, :, 0:side], slots, (early_a, early_b, early_c, early_d))
    early_x = RingScatter(
        copy, "x", lambda at: early.at[:, at, :, side : 2 * side], slots, (early_e, early_f, early_g, early_h)
    )
    for ring in (early_z, early_x):
        ring.far_out()
        ring.near_out()
    for one in loads[1:]:
        one.wait()

    ones = jnp.ones((8, cols), low)

    def weight_block(at):
        def part(h, carry):
            block = at * 2 + h
            rows = pl.ds(pl.multiple_of(block * 256, 256), 256)
            prev_block, delta_block = prev[:, rows].T, delta[:, rows].T
            column = column_ref[rows]
            scaled[3, rows] = (column[:, 5:6] * time[3, rows].astype(jnp.float32)).astype(low)
            grads = []
            for n in range(3):
                by_delta = nn(delta_block, grad_ref[n])
                factor = column[:, 2 + n : 3 + n]
                grads.append((nn(prev_block, grad_ref[n]) + factor * by_delta).astype(low))
                weight = time[n, rows].astype(jnp.float32)
                scaled[n, rows] = (factor * weight).astype(low)
                parts[2 + n : 3 + n, rows] = nt(ones, (weight * by_delta).astype(low))[0:1]
            whole = jnp.concatenate(grads, axis=1)
            half = whole.shape[1] // 2
            for k in range(2):
                one_dw[at, h * 2 + k] = whole[k * 128 : (k + 1) * 128, :half]
                other_dw[at, h * 2 + k] = whole[k * 128 : (k + 1) * 128, half:]
            return carry

        lax.fori_loop(0, 2, part, 0)

    parts[...] = vec_ref[...]
    z_first = RingScatter(copy, "z", lambda at: one_dw.at[at], slots, (one_a, one_b, one_c, one_d))
    x_first = RingScatter(copy, "x", lambda at: other_dw.at[:, at], slots, (other_a, other_b, other_c, other_d))

    row = lax.broadcasted_iota(jnp.int32, (16, p.shape[2]), 0)
    edge = copy(firsts.at[0], firsts.at[4], to_previous)

    def compute(q):
        rows = pl.ds(pl.multiple_of(q * 256, 256), 256)
        whole, here = 0.0, 0.0
        for n in range(4):
            whole = whole + nt(grad_ref[n, rows], time[n])
            here = here + nt(grad_ref[n, rows], scaled[n])
        terms[0] = here
        terms[1] = whole - here
        for s in range(2):
            after = jnp.zeros((1, p.shape[2]), jnp.float32)
            for b in (1, 0):

                def slab(t, following):
                    at = s * BLOCK_LEN + (BLOCK_LEN // 16 - 1 - t) * 16
                    rows = pl.ds(pl.multiple_of(b * 2 * BLOCK_LEN + at, 16), 16)
                    behind = terms[1, rows]
                    moved = jnp.where(row == 15, following, pltpu.roll(behind, 15, 0))
                    p[q * 2 + b, pl.ds(pl.multiple_of(at, 16), 16)] = (terms[0, rows] + moved).astype(low)
                    return behind[0:1]

                after = lax.fori_loop(0, BLOCK_LEN // 16, slab, after)
            firsts[q, s, 0:1, :] = after

        @pl.when(q == 0)
        def _():
            edge.start()

    def close(q):
        @pl.when(q == 3)
        def _():
            edge.wait_recv()

        for s in range(2):
            following = firsts[q + 1, s, 0:1, :]
            following = jnp.where(jnp.logical_and(q == 3, x == 3), 0.0, following)
            rows = slice(s * BLOCK_LEN + BLOCK_LEN - 16, (s + 1) * BLOCK_LEN)
            value = p[q * 2 + 1, rows].astype(jnp.float32)
            p[q * 2 + 1, rows] = (value + jnp.where(row == 15, following, 0.0)).astype(low)

    total = Scatter(copy, p, first_grad, from_sibling, mid, from_left, from_right, end_left, end_right)
    weight_block(z_first.far)
    z_first.far_out()
    early_z.pass_on()
    early_x.pass_on()
    weight_block(z_first.right)
    weight_block(z_first.left)
    z_first.near_out()
    weight_block(z_first.me)
    x_first.far_out()
    x_first.near_out()
    compute(left)
    z_first.pass_on()
    early_z.finish(early_one)
    early_x.finish(early_other)
    early_last_x = RingScatter(copy, "x", lambda at: early_one.at[at], halves, (early_i, early_j, early_k, early_l))
    early_last_z = RingScatter(copy, "z", lambda at: early_other.at[at], halves, (early_m, early_n, early_o, early_p))
    for ring in (early_last_x, early_last_z):
        ring.far_out()
        ring.near_out()
    compute(far)
    close(far)
    total.share(0)
    x_first.pass_on()
    compute(right)
    total.far_out()
    close(right)
    total.share(1)
    total.right_b()
    early_last_x.pass_on()
    early_last_z.pass_on()
    z_first.finish(one_sum)
    x_last = RingScatter(copy, "x", lambda at: one_sum.at[at], halves, (one_e, one_f, one_g, one_h))
    x_last.far_out()
    x_last.near_out()
    compute(y)
    close(left)
    total.share(2)
    close(y)
    total.share(3)
    total.left_b()
    total.right_a()
    total.left_a()
    x_first.finish(other_sum)
    z_last = RingScatter(copy, "z", lambda at: other_sum.at[at], halves, (other_e, other_f, other_g, other_h))
    z_last.far_out()
    z_last.near_out()
    x_last.pass_on()
    z_last.pass_on()
    early_last_x.finish(stripe.at[:, 3 * cols : 3 * cols + side])
    early_last_z.finish(stripe.at[:, 3 * cols + side : 3 * cols + 2 * side])
    half = one_sum.shape[2]
    x_last.finish(stripe.at[:, 0:half])
    z_last.finish(stripe.at[:, half : 2 * half])
    given = [
        copy(stripe.at[pl.ds(pl.multiple_of(at * 16, 16), 16)], gathered.at[member], d)
        for at, d in zip(near_members, near_devices)
    ]
    for one in given:
        one.start()
    gathered[member] = stripe[pl.ds(pl.multiple_of(member * 16, 16), 16)]
    total.finish()

    norm_sums[...] = jnp.zeros_like(norm_sums)

    def norm_rows(t, carry):
        rows = pl.ds(pl.multiple_of(t * 16, 16), 16)
        values = tok_ref[rows].astype(jnp.float32)
        center = values - jnp.mean(values, axis=-1, keepdims=True)
        inverse = lax.rsqrt(jnp.mean(center * center, axis=-1, keepdims=True) + epsilon)
        unit = center * inverse
        grad = first_grad[rows]
        product = grad * unit
        norm_sums[0] += product[:8] + product[8:]
        norm_sums[1] += grad[:8] + grad[8:]
        inner = grad * set_ref[0:1, :]
        mean = jnp.mean(inner, axis=-1, keepdims=True)
        along = jnp.mean(inner * unit, axis=-1, keepdims=True)
        token_ref[rows] = (upper_ref[rows] + inverse * (inner - mean - unit * along)).astype(low)
        return carry

    lax.fori_loop(0, 8, norm_rows, 0)
    for n in range(2):
        parts[n : n + 1, :] = jnp.sum(norm_sums[n], axis=0, keepdims=True)
    vec_first = [
        copy(parts.at[:, pl.ds(pl.multiple_of(at * 128, 128), 128)], vec_far.at[n], d)
        for n, (at, d) in enumerate(zip(far_places, far_devices))
    ]
    for one in vec_first:
        one.start()
    sum_all = parts[:, pl.ds(pl.multiple_of(place * 128, 128), 128)]
    for n, one in enumerate(vec_first):
        one.wait_recv()
        sum_all = sum_all + vec_far[n]
    vec_stripe[...] = sum_all
    vec_last = [copy(vec_stripe, vec_near.at[n], d) for n, d in enumerate(near_devices)]
    for one in vec_last:
        one.start()
    for one in given:
        one.wait_recv()
    for m in range(8):
        for n in range(5):
            weight_ref[n, :, m * cols : (m + 1) * cols] = gathered[m, :, n * cols : (n + 1) * cols].astype(jnp.float32)
    for n, one in enumerate(vec_last):
        one.wait_recv()
        sum_all = sum_all + vec_near[n]
    total_ref[...] = sum_all
    copy.wait_sent()


def closing(grads, early, time, prev, delta, settings, columns, tokens, upper, vec, cid):
    _, width, cols = time.shape
    rows = delta.shape[0] // 8
    half, side = 3 * cols // 2, cols
    early = early.reshape(4, 4, 128, 2 * cols)
    shape = jax.ShapeDtypeStruct
    wide = [pltpu.VMEM((2, 128, half), low)] * 2 + [pltpu.VMEM((4, 128, half), low)] * 2
    thin = [pltpu.VMEM((64, half), low)] * 2 + [pltpu.VMEM((128, half), low)] * 2
    early_wide = [pltpu.VMEM((2, 128, side), low)] * 2 + [pltpu.VMEM((4, 128, side), low)] * 2
    early_thin = [pltpu.VMEM((64, side), low)] * 2 + [pltpu.VMEM((128, side), low)] * 2
    early_sum = pltpu.VMEM((4, 128, side), low)
    return pl.pallas_call(
        closing_kernel,
        name="closing",
        out_shape=[
            shape((rows, width), low),
            shape((5, 16, width), jnp.float32),
            shape((16, 128), jnp.float32),
        ],
        in_specs=[VMEM, HBM, HBM, HBM, HBM, VMEM, VMEM, VMEM, VMEM, VMEM],
        out_specs=[VMEM] * 3,
        scratch_shapes=[
            pltpu.VMEM((4, width, cols), low),
            pltpu.VMEM((4, width, cols), low),
            pltpu.VMEM(delta.shape, low),
            pltpu.VMEM(delta.shape, low),
            pltpu.VMEM(early.shape, low),
            pltpu.VMEM((2, 256, width), jnp.float32),
            pltpu.VMEM((8, rows, width), low),
            pltpu.VMEM((5, 2, 8, width), jnp.float32),
            pltpu.VMEM((4, 4, 128, half), low),
            pltpu.VMEM((4, 4, 128, half), low),
            pltpu.VMEM((4, 128, half), low),
            pltpu.VMEM((4, 128, half), low),
            pltpu.VMEM((128, 5 * cols), low),
            pltpu.VMEM((8, 16, 5 * cols), low),
            pltpu.VMEM((16, width), jnp.float32),
            *wide,
            *wide,
            *thin,
            *thin,
            *early_wide,
            *early_wide,
            *early_thin,
            *early_thin,
            early_sum,
            early_sum,
            pltpu.VMEM((15, 16, 128), jnp.float32),
            pltpu.VMEM((7, 16, 128), jnp.float32),
            pltpu.VMEM((16, 128), jnp.float32),
            pltpu.VMEM((rows, width), jnp.float32),
            pltpu.VMEM((2, 8, width), jnp.float32),
            *scatter_scratch(rows, width),
            pltpu.SemaphoreType.DMA((104,)),
            pltpu.SemaphoreType.DMA((104,)),
            pltpu.SemaphoreType.DMA((4,)),
        ],
        compiler_params=pltpu.CompilerParams(collective_id=cid, has_side_effects=True, vmem_limit_bytes=59 * 2**20),
    )(grads, early, time, prev, delta, settings, columns, tokens, upper, vec)


def body(tokens, time_weights, channel_key, channel_value, channel_gate, vectors, head_decay, lengths, cotangent):
    groups, span, width = tokens.shape
    features = channel_key.shape[1]
    local_rows = channel_key.shape[0]
    members = lax.axis_size(GROUP)
    member = lax.axis_index(GROUP)
    x_size, x_place = lax.axis_size("x"), lax.axis_index("x")
    heads = head_decay.shape[0] // members
    head_width = width // head_decay.shape[0]
    own = width // members
    own_features = features // members
    row_count = groups * span
    all_rows = members * row_count
    stripe = members * local_rows

    vector_rows = vectors.shape[0]
    vector_block = lax.dynamic_update_slice(jnp.zeros((16, stripe), low), vectors, (0, member * local_rows))
    recv, key, value, gate_pre, settings, time_full, first_prev, first_delta, channel_part = opening(
        tokens.reshape(row_count, width), time_weights, channel_key, channel_value, channel_gate, vector_block, 1
    )
    time_full = time_full.reshape(5, width, own)
    channel_full = lax.all_gather(channel_part, ROWS, axis=0, tiled=True)
    own_settings = lax.dynamic_slice_in_dim(settings, member * own, own, axis=1)

    log_decay = jnp.log(lax.dynamic_slice_in_dim(head_decay, member * heads, heads))
    params = jnp.concatenate(
        [jnp.repeat(log_decay, head_width)[None], own_settings[6:9], jnp.zeros((4, own), jnp.float32)]
    )
    weights, wkv_scaled, wkv_inverse, incoming, hidden_one, second, gated_all = recurrence(
        recv, key, value, gate_pre, params, tokens.reshape(row_count, width), settings, time_full, 3
    )

    offsets = lax.axis_index(SEQ) * span + jnp.arange(span, dtype=jnp.int32)
    upstream = jnp.where((offsets[None, :] < lengths[:, None])[:, :, None], cotangent, jnp.zeros((), low))
    upstream = upstream.reshape(row_count, width)
    layer_out, grad_second, channel_sums, channel_term = channel(
        second, hidden_one, upstream, channel_full, settings, 7
    )
    layer_out = layer_out.reshape(groups, span, width)
    mix_key_grad, mix_gate_grad = channel_sums[0], channel_sums[1]
    channel_sum = lax.psum_scatter(channel_term, ROWS, scatter_dimension=0, tiled=True)
    upper, grad_proj, middle_sums, own_sums, early_term = middle(
        grad_second,
        hidden_one,
        upstream,
        settings,
        settings.T,
        params,
        gate_pre,
        wkv_scaled,
        wkv_inverse,
        recv,
        key,
        value,
        weights,
        incoming,
        time_full,
        first_prev,
        first_delta,
        gated_all,
        4,
    )
    bonus_grad, norm_gain_grad, norm_bias_grad = own_sums[0], own_sums[1], own_sums[2]
    second_gain_grad, second_bias_grad = middle_sums[0], middle_sums[1]
    def spread_own(row):
        return lax.dynamic_update_slice_in_dim(jnp.zeros((width,), jnp.float32), row, member * own, axis=0)

    nothing = jnp.zeros((width,), jnp.float32)
    vector_term = jnp.stack(
        [nothing] * 5
        + [middle_sums[2]]
        + [
            spread_own(bonus_grad),
            spread_own(norm_gain_grad),
            spread_own(norm_bias_grad),
            second_gain_grad,
            second_bias_grad,
            mix_key_grad,
            mix_gate_grad,
        ]
        + [nothing] * 3
    )
    token_grad, time_grads, vector_sum = closing(
        grad_proj,
        early_term,
        time_full,
        first_prev,
        first_delta,
        settings,
        settings.T,
        tokens.reshape(row_count, width),
        upper,
        vector_term,
        9,
    )
    token_grad = token_grad.reshape(groups, span, width)
    channel_sum, vector_sum = lax.optimization_barrier((channel_sum, vector_sum))
    channel_sum = lax.all_to_all(
        channel_sum.reshape(members, local_rows, 2 * own_features + own), GROUP, split_axis=0, concat_axis=0, tiled=True
    )
    channel_sum = jnp.swapaxes(channel_sum, 0, 1).astype(jnp.float32)
    key_grad = channel_sum[:, :, :own_features].reshape(local_rows, features)
    value_grad = channel_sum[:, :, own_features : 2 * own_features].reshape(local_rows, features)
    gate_grad = channel_sum[:, :, 2 * own_features :].reshape(local_rows, width)
    vector_sum = lax.dynamic_slice(vector_sum, (0, member * local_rows), (vector_rows, local_rows))
    return layer_out, token_grad, time_grads, key_grad, value_grad, gate_grad, vector_sum


def solution(mesh):
    batch, seq = mesh.devices.shape
    side = 4
    fine = Mesh(mesh.devices.reshape(batch, side, seq // (2 * side), 2), ALL)
    return jax.shard_map(
        body,
        mesh=fine,
        in_specs=(
            P("z", SEQ, None),
            P(None, ALL, None),
            P(ALL, None),
            P(ALL, None),
            P(ALL, None),
            P(None, ALL),
            P(),
            P("z"),
            P("z", SEQ, None),
        ),
        out_specs=(
            P("z", SEQ, None),
            P("z", SEQ, None),
            P(None, ALL, None),
            P(ALL, None),
            P(ALL, None),
            P(ALL, None),
            P(None, ALL),
        ),
        check_vma=False,
    )
```

```python
import jax
import jax.numpy as jnp
from jax import lax
from jax.experimental import pallas as pl
from jax.experimental.pallas import tpu as pltpu
from jax.sharding import Mesh, PartitionSpec as P

BLOCK_LEN = 64
epsilon = 1e-05
group_epsilon = 0.00064

GROUP = ("y", "core")
ROWS = ("z", "x")
SEQ = ("x", "y", "core")
ALL = ("z", "x", "y", "core")
low = jnp.bfloat16


MESH = pl.DeviceIdType.MESH
HBM = pl.BlockSpec(memory_space=pl.ANY)


def cost(microseconds):
    return pl.CostEstimate(flops=0, bytes_accessed=microseconds * 3_000_000, transcendentals=0)


VMEM = pl.BlockSpec(memory_space=pltpu.VMEM)


def greet(devices):
    barrier = pltpu.get_barrier_semaphore()
    for device in devices:
        pl.semaphore_signal(barrier, inc=1, device_id=device, device_id_type=MESH)
    pl.semaphore_wait(barrier, len(devices))

def ring_places():
    y, c = lax.axis_index("y"), lax.axis_index("core")
    right, left, far = lax.rem(y + 1, 4), lax.rem(y + 3, 4), lax.rem(y + 2, 4)
    return y, c, right, left, far

def cube_places():
    z, x, y, c = [lax.axis_index(name) for name in ("z", "x", "y", "core")]
    place, member = z * 4 + x, y * 2 + c
    far = [lax.rem(place + k, 16) for k in range(1, 16)]
    near = [lax.rem(member + k, 8) for k in range(1, 8)]
    return place, member, far, near, [{"z": p // 4, "x": lax.rem(p, 4)} for p in far], [{"y": p // 2, "core": lax.rem(p, 2)} for p in near]

def nn(left, right):
    return jnp.dot(left, right, preferred_element_type=jnp.float32)


def nt(left, right):
    return lax.dot_general(left, right, (((1,), (1,)), ((), ())), preferred_element_type=jnp.float32)


def tn(left, right):
    return lax.dot_general(left, right, (((0,), (0,)), ((), ())), preferred_element_type=jnp.float32)


def head_tables(log_row):
    width = log_row.shape[-1]
    place = lax.broadcasted_iota(jnp.int32, (BLOCK_LEN, width), 0)
    other = lax.rem(lax.broadcasted_iota(jnp.int32, (BLOCK_LEN, width), 1), BLOCK_LEN)
    gap = jnp.maximum(place - 1 - other, 0).astype(jnp.float32)
    mask = jnp.where(other < place, jnp.exp(gap * log_row), 0.0)
    eye = other == place
    enter = jnp.exp(place.astype(jnp.float32) * log_row)
    leave = jnp.exp((BLOCK_LEN - 1 - place).astype(jnp.float32) * log_row)
    tall = lax.broadcasted_iota(jnp.int32, (width, width), 0) // BLOCK_LEN
    wide = lax.broadcasted_iota(jnp.int32, (width, width), 1) // BLOCK_LEN
    return mask, eye, enter, leave, tall == wide


def expand(block, same):
    copies = block.shape[1] // BLOCK_LEN
    return jnp.where(same, jnp.concatenate([block] * copies, axis=0), jnp.zeros((), block.dtype))


def compress(square, same):
    kept = jnp.where(same, square, 0.0)
    return sum(kept[k * BLOCK_LEN : (k + 1) * BLOCK_LEN] for k in range(square.shape[0] // BLOCK_LEN))


def head_sum(values, same, factor=1.0):
    ones = jnp.where(same, factor, 0.0).astype(low)
    high = values.astype(low)
    rest = (values - high.astype(jnp.float32)).astype(low)
    return nn(high, ones) + nn(rest, ones)


def head_mean(values, same):
    return head_sum(values, same, 1.0 / BLOCK_LEN)


def block_rows(m, s):
    return pl.ds(pl.multiple_of(m * 2 * BLOCK_LEN + s * BLOCK_LEN, BLOCK_LEN), BLOCK_LEN)


def start_line(total, slots, send, recv):
    me = lax.axis_index("x")
    devices = [{"x": lax.rem(me + k, 4)} for k in range(1, 4)]
    slots[me] = total[...]
    copies = [
        pltpu.make_async_remote_copy(
            src_ref=total, dst_ref=slots.at[me], send_sem=send.at[k], recv_sem=recv.at[k], device_id=d, device_id_type=MESH
        )
        for k, d in enumerate(devices)
    ]
    for one in copies:
        one.start()
    return copies


def recurrence_kernel(
    r_hbm, k_hbm, v_hbm, g_hbm, p_ref, tok_hbm, set_hbm, time_hbm, stripe_hbm,
    second_ref, w_out, scaled_out, inverse_out, in_out, hidden_out, gated_ref, full_ref,
    r_ref, k_ref, v_ref, g_ref, tok_ref, set_ref, stripe_ref, w_ref, scaled_ref, inverse_ref, in_ref, hidden_ref, wkv, prefix, total, slots, gated, time, out, out_all, send, recv, local,
):
    loads = [
        pltpu.make_async_copy(source, target, local.at[8 + n])
        for n, (source, target) in enumerate(
            ((k_hbm, k_ref), (r_hbm, r_ref), (v_hbm, v_ref), (g_hbm, g_ref), (tok_hbm, tok_ref), (set_hbm, set_ref), (stripe_hbm, stripe_ref))
        )
    ]
    for one in loads:
        one.start()
    x, member, near, near_devices, _, _ = group_and_line()
    y, c, right, left, far = ring_places()
    z = lax.axis_index("z")
    greet(near_devices + [{"x": lax.rem(x + n, 4)} for n in range(1, 4)] + [{"z": lax.rem(z + n, 4)} for n in (1, 3)])
    copy = Copies(send, recv)
    loads.pop().wait()
    place = pltpu.make_async_copy(stripe_ref, full_ref.at[z, x], local.at[2])
    place.start()
    place.wait()
    side = stripe_hbm.shape[1] // 2
    one_side, other_side = pl.ds(0, side), pl.ds(side, side)
    z_first = Ring(copy, "z", lambda at, n: full_ref.at[at, x, pl.ds(n * 64, 64), one_side])
    x_first = Ring(copy, "x", lambda at, n: full_ref.at[z, at, pl.ds(n * 64, 64), other_side])
    load = pltpu.make_async_copy(time_hbm.at[4], time, local.at[0])
    load.start()
    for one in loads:
        one.wait()
    log_row, bonus, gain, bias = [p_ref[n : n + 1, :] for n in range(4)]
    mask, eye, enter, leave, same = head_tables(log_row)
    block_decay = jnp.exp(BLOCK_LEN * log_row)

    def first(m, states):
        after = []
        for s in range(2):
            rows = block_rows(m, s)
            r, k, v = r_ref[rows], k_ref[rows], v_ref[rows]
            key = expand(k, same)
            scores = nt(r, key)
            pairs = head_sum(r.astype(jnp.float32) * bonus * k.astype(jnp.float32), same)
            weights = (scores * mask + jnp.where(eye, pairs, 0.0)).astype(low)
            w_ref[rows] = weights
            wkv[rows] = nn(weights, expand(v, same))
            prefix[m * 2 + s] = states[s]
            key_leave = (k.astype(jnp.float32) * leave).astype(low)
            after.append(states[s] * block_decay + compress(tn(key_leave, v), same))
        return tuple(after)

    zero = jnp.zeros(enter.shape, jnp.float32)
    states = lax.fori_loop(0, 8, first, (zero, zero))
    z_first.forward()
    x_first.forward()
    for s in range(2):
        total[s] = states[s]
    line = start_line(total, slots, send.at[pl.ds(50, 3)], recv.at[pl.ds(50, 3)])
    for ring in (z_first, x_first):
        ring.wait_near()
        ring.wait_far()
    for one in line:
        one.wait()
    x_last = Ring(copy, "x", lambda at, n: full_ref.at[pl.ds(n * 2, 2), at, :, one_side])
    z_last = Ring(copy, "z", lambda at, n: full_ref.at[at, pl.ds(n * 2, 2), :, other_side])
    x_place = lax.axis_index("x")
    entering = [zero, zero]
    span_decay = jnp.exp(8.0 * BLOCK_LEN * log_row)
    for x in range(3):
        for s in range(2):
            entering[s] = jnp.where(x < x_place, entering[s] * span_decay + slots[x, s], entering[s])
    for s in range(2):
        total[s] = entering[s]

    def second(m, carry):
        power = jnp.exp((m * BLOCK_LEN).astype(jnp.float32) * log_row)
        for s in range(2):
            rows = block_rows(m, s)
            state = (prefix[m * 2 + s] + power * total[s]).astype(low)
            in_ref[m * 2 + s] = state
            recv_enter = (r_ref[rows].astype(jnp.float32) * enter).astype(low)
            out = wkv[rows] + nn(recv_enter, expand(state, same))
            center = out - head_mean(out, same)
            inverse = lax.rsqrt(head_mean(center * center, same) + group_epsilon)
            scaled = center * inverse
            scaled_ref[rows] = scaled
            inverse_ref[rows] = inverse
            gate = g_ref[rows]
            gated[member, rows] = ((scaled * gain + bias) * gate * jax.nn.sigmoid(gate)).astype(low)
        return carry

    half = gated.shape[1] // 2
    ring = Ring(copy, "y", lambda at, n: gated.at[at * 2 + c, pl.ds(n * half, half)], start=False)
    to_sibling = {"core": 1 - c}
    across = [copy(gated.at[member, pl.ds(n * half, half)], gated.at[member, pl.ds(n * half, half)], to_sibling) for n in range(2)]
    for n in range(2):
        lax.fori_loop(4 * n, 4 * n + 4, second, 0)
        ring.start(n)
        across[n].start()

    def pass_on(at):
        one = copy(gated.at[at * 2 + c], gated.at[at * 2 + c], to_sibling)
        one.start()
        return one

    outs = [
        pltpu.make_async_copy(source, target, local.at[3 + n])
        for n, (source, target) in enumerate(
            ((w_ref, w_out), (scaled_ref, scaled_out), (inverse_ref, inverse_out), (in_ref, in_out))
        )
    ]
    for one in outs:
        one.start()
    x_last.forward()
    z_last.forward()
    ring.forward()
    ring.wait_near()
    passed = [pass_on(right), pass_on(left)]
    load.wait()
    ring.wait_far()
    passed.append(pass_on(far))
    for one in across + passed:
        one.wait_recv()
    keep = pltpu.make_async_copy(gated, gated_ref, local.at[1])
    keep.start()

    cols = w_ref.shape[1]
    given = []

    def project(q):
        rows = pl.ds(pl.multiple_of(q * 256, 256), 256)
        value = sum(nn(gated[m, rows], time[m * cols : (m + 1) * cols]) for m in range(8)).astype(low)
        for b in range(2):
            out[q * 2 + b] = value[b * 128 : (b + 1) * 128]

    for at in (far, right, left, y):
        project(at)
        for turn in range(2):
            j = at * 2 + lax.rem(c + turn, 2)
            if at is y and turn == 0:
                continue
            given.append(copy(out.at[j], out_all.at[member], {"y": at, "core": lax.rem(c + turn, 2)}))
            given[-1].start()
    out_all[member] = out[member]
    for one in given:
        one.wait_recv()

    def norm_rows(t, carry):
        rows = pl.ds(pl.multiple_of(t * 16, 16), 16)
        added = jnp.concatenate([out_all[n, rows].astype(jnp.float32) for n in range(8)], axis=1)
        values = tok_ref[rows].astype(jnp.float32) + added
        hidden_ref[rows] = values
        center = values - jnp.mean(values, axis=-1, keepdims=True)
        inverse = lax.rsqrt(jnp.mean(center * center, axis=-1, keepdims=True) + epsilon)
        second_ref[rows] = (center * inverse * set_ref[9:10, :] + set_ref[10:11, :]).astype(low)
        return carry

    lax.fori_loop(0, 8, norm_rows, 0)
    outs.append(pltpu.make_async_copy(hidden_ref, hidden_out, local.at[7]))
    outs[-1].start()
    for last in (x_last, z_last):
        last.wait_near()
        last.wait_far()
    copy.wait_sent()
    keep.wait()
    for one in outs:
        one.wait()


def recurrence(r, k, v, g, params, tokens, settings, time, stripe, cid):
    rows, cols = r.shape
    own_rows, width = tokens.shape
    shape = jax.ShapeDtypeStruct
    return pl.pallas_call(
        recurrence_kernel,
        name="recurrence",
        cost_estimate=cost(55),
        out_shape=[
            shape((own_rows, width), low),
            shape((rows, cols), low),
            shape((rows, cols), jnp.float32),
            shape((rows, cols), jnp.float32),
            shape((16, BLOCK_LEN, cols), low),
            shape((own_rows, width), jnp.float32),
            shape((8, rows, cols), low),
            shape((4, 4) + stripe.shape, low),
        ],
        in_specs=[HBM] * 4 + [VMEM] + [HBM] * 4,
        out_specs=[VMEM] + [HBM] * 7,
        scratch_shapes=[
            pltpu.VMEM((rows, cols), low),
            pltpu.VMEM((rows, cols), low),
            pltpu.VMEM((rows, cols), low),
            pltpu.VMEM((rows, cols), jnp.float32),
            pltpu.VMEM((own_rows, width), low),
            pltpu.VMEM(settings.shape, jnp.float32),
            pltpu.VMEM(stripe.shape, low),
            pltpu.VMEM((rows, cols), low),
            pltpu.VMEM((rows, cols), jnp.float32),
            pltpu.VMEM((rows, cols), jnp.float32),
            pltpu.VMEM((16, BLOCK_LEN, cols), low),
            pltpu.VMEM((own_rows, width), jnp.float32),
            pltpu.VMEM((rows, cols), jnp.float32),
            pltpu.VMEM((16, BLOCK_LEN, cols), jnp.float32),
            pltpu.VMEM((2, BLOCK_LEN, cols), jnp.float32),
            pltpu.VMEM((4, 2, BLOCK_LEN, cols), jnp.float32),
            pltpu.VMEM((8, rows, cols), low),
            pltpu.VMEM((width, cols), low),
            pltpu.VMEM((8, own_rows, cols), low),
            pltpu.VMEM((8, own_rows, cols), low),
            pltpu.SemaphoreType.DMA((53,)),
            pltpu.SemaphoreType.DMA((53,)),
            pltpu.SemaphoreType.DMA((15,)),
        ],
        compiler_params=pltpu.CompilerParams(collective_id=cid, has_side_effects=True, vmem_limit_bytes=59 * 2**20),
    )(r, k, v, g, params, tokens, settings, time, stripe)


class Copies:
    def __init__(self, send, recv):
        self.send, self.recv, self.count, self.all = send, recv, 0, []

    def __call__(self, src, dst, device):
        one = pltpu.make_async_remote_copy(
            src_ref=src,
            dst_ref=dst,
            send_sem=self.send.at[self.count],
            recv_sem=self.recv.at[self.count],
            device_id=device,
            device_id_type=MESH,
        )
        self.count += 1
        self.all.append(one)
        return one

    def wait_sent(self, some=None):
        some = self.all if some is None else some
        for one in some:
            one.wait_send()
        self.all = [one for one in self.all if not any(one is other for other in some)]


class Ring:
    def __init__(self, copy, axis, part, start=True):
        me = lax.axis_index(axis)
        self.copy, self.part = copy, part
        self.right, self.left, self.far = [lax.rem(me + k, 4) for k in (1, 3, 2)]
        self.to_right, self.to_left = {axis: self.right}, {axis: self.left}
        own = [part(me, 0), part(me, 1)]
        self.near = [
            copy(own[0], own[0], self.to_right),
            copy(own[1], own[1], self.to_left),
            copy(own[1], own[1], self.to_right),
            copy(own[0], own[0], self.to_left),
        ]
        if start:
            for one in self.near:
                one.start()

    def start(self, half):
        for n in ((0, 3), (2, 1))[half]:
            self.near[n].start()

    def forward(self):
        self.near[0].wait_recv()
        there = self.part(self.left, 0)
        self.far_right = self.copy(there, there, self.to_right)
        self.far_right.start()
        self.near[1].wait_recv()
        there = self.part(self.right, 1)
        self.far_left = self.copy(there, there, self.to_left)
        self.far_left.start()

    def wait_near(self):
        self.near[2].wait_recv()
        self.near[3].wait_recv()

    def wait_far(self):
        self.far_right.wait_recv()
        self.far_left.wait_recv()


def opening_kernel(
    tok_ref, tw_ref, ck_ref, cv_ref, cg_ref, vec_ref,
    r_out, k_out, v_out, g_out, set_out, time_ref, prev_ref, delta_ref, unit_ref, stripe_ref,
    r_ref, k_ref, v_ref, g_ref, set_ref, tokens, time, mix, prev, delta, unit, vec_blocks, vec_stripe, vec_all, send, recv, local,
):
    place, member, far, near, far_devices, near_devices = cube_places()
    z, x, y, c = [lax.axis_index(name) for name in ("z", "x", "y", "core")]
    greet(far_devices + near_devices)
    copy = Copies(send, recv)
    own = tw_ref.shape[2] // 8
    wide = ck_ref.shape[1] // 8

    def lanes(p, size):
        return pl.ds(pl.multiple_of(p * size, size), size)

    def tile(p):
        return pl.ds(pl.multiple_of(p * 16, 16), 16)

    vec_near = [copy(vec_ref, vec_blocks.at[n], d) for n, d in enumerate(near_devices)]
    for one in vec_near:
        one.start()
    time_near = [
        copy(tw_ref.at[:, :, lanes(p, own)], time.at[:, z, x, tile(member), :], d) for p, d in zip(near, near_devices)
    ]
    for one in time_near:
        one.start()
    time_own = pltpu.make_async_copy(tw_ref.at[:, :, lanes(member, own)], time.at[:, z, x, tile(member), :], local.at[0])
    time_own.start()
    tokens[member] = tok_ref[...]
    gathered = Tokens(copy, tokens, member)
    to_next = {"x": lax.rem(x + 1, 4)}
    last_rows = [pl.ds(s * BLOCK_LEN + BLOCK_LEN - 16, 16) for s in range(2)]
    edges = [copy(tokens.at[7, rows], tokens.at[8, rows], to_next) for rows in last_rows]

    total = vec_ref[...].astype(jnp.float32)
    for n, one in enumerate(vec_near):
        one.wait_recv()
        total = total + vec_blocks[n].astype(jnp.float32)
    vec_stripe[...] = total.astype(low)
    vec_all[place] = vec_stripe[...]
    vec_far = [copy(vec_stripe, vec_all.at[place], d) for d in far_devices]
    for one in vec_far:
        one.start()

    for one in time_near:
        one.wait_recv()
    time_own.wait()
    one_side, other_side = pl.ds(0, own // 2), pl.ds(own // 2, own // 2)
    rows = time.shape[3] // 2
    z_first = Ring(copy, "z", lambda at, n: time.at[:, at, x, pl.ds(n * rows, rows), one_side])
    x_first = Ring(copy, "x", lambda at, n: time.at[:, z, at, pl.ds(n * rows, rows), other_side])
    gathered.ring.forward()
    z_first.forward()
    x_first.forward()
    z_first.wait_near()
    z_first.wait_far()
    x_last = Ring(copy, "x", lambda at, n: time.at[:, pl.ds(n * 2, 2), at, :, one_side])
    x_first.wait_near()
    x_first.wait_far()
    z_last = Ring(copy, "z", lambda at, n: time.at[:, at, pl.ds(n * 2, 2), :, other_side])
    for one in vec_far:
        one.wait_recv()
    for n in range(16):
        set_ref[:, n * 128 : (n + 1) * 128] = vec_all[n].astype(jnp.float32)
    gathered.wait_next()

    channel = []
    for source, size, start in ((ck_ref, wide, 0), (cv_ref, wide, wide), (cg_ref, own, 2 * wide)):
        for p, d in zip(near, near_devices):
            channel.append(copy(source.at[:, lanes(p, size)], stripe_ref.at[tile(member), pl.ds(start, size)], d))
    for one in channel:
        one.start()
    kept = [
        pltpu.make_async_copy(source.at[:, lanes(member, size)], stripe_ref.at[tile(member), pl.ds(start, size)], local.at[n])
        for n, (source, size, start) in enumerate(((ck_ref, wide, 0), (cv_ref, wide, wide), (cg_ref, own, 2 * wide)))
    ]
    for one in kept:
        one.start()

    width = tok_ref.shape[1]
    step = 512
    row = lax.broadcasted_iota(jnp.int32, (16, step), 0)

    def statistics(values):
        mean = jnp.mean(values, axis=-1, keepdims=True)
        center = values - mean
        return mean, lax.rsqrt(jnp.mean(center * center, axis=-1, keepdims=True) + epsilon)

    def mix_pair(q):
        @pl.when(q == 0)
        def _():
            for one in edges:
                one.wait_recv()

        def mix_block(b, carry):
            j = q * 2 + b
            before_slot = jnp.where(j == 0, 8, j - 1)
            hidden = jnp.logical_and(j == 0, x == 0)
            for s in range(2):
                last = slice(s * BLOCK_LEN + BLOCK_LEN - 16, (s + 1) * BLOCK_LEN)
                found = [statistics(tokens[before_slot, last].astype(jnp.float32))]
                found[0] = (found[0][0][15:16], found[0][1][15:16])
                for t in range(BLOCK_LEN // 16):
                    at = s * BLOCK_LEN + t * 16
                    found.append(statistics(tokens[j, at : at + 16].astype(jnp.float32)))

                def columns(n, carry):
                    cols = pl.ds(pl.multiple_of(n * step, step), step)
                    gain, offset = set_ref[0:1, cols], set_ref[1:2, cols]
                    before = tokens[before_slot, last, cols].astype(jnp.float32)[15:16]
                    before = (before - found[0][0]) * found[0][1] * gain + offset
                    before = jnp.where(hidden, 0.0, before)
                    for t in range(BLOCK_LEN // 16):
                        at = s * BLOCK_LEN + t * 16
                        mean, inverse = found[t + 1]
                        scaled = (tokens[j, at : at + 16, cols].astype(jnp.float32) - mean) * inverse
                        norm = scaled * gain + offset
                        moved = jnp.where(row == 0, before, pltpu.roll(norm, 1, 0))
                        before = norm[15:16]
                        gap = norm - moved
                        to = pl.ds(pl.multiple_of(j * 2 * BLOCK_LEN + at, 16), 16)
                        unit[to, cols] = scaled.astype(low)
                        prev[to, cols] = moved.astype(low)
                        delta[to, cols] = gap.astype(low)
                        for p in range(4):
                            mix[p, to, cols] = (moved + set_ref[2 + p : 3 + p, cols] * gap).astype(low)
                    return carry

                lax.fori_loop(0, width // step, columns, 0)
            return carry

        lax.fori_loop(0, 2, mix_block, 0)

    gathered.wait_passed()

    @pl.when(y != 1)
    def _():
        for one in edges:
            one.start()

    mix_pair(gathered.ring.right)
    x_last.forward()
    z_last.forward()
    mix_pair(y)
    gathered.far_pair()

    @pl.when(y == 1)
    def _():
        for one in edges:
            one.start()

    mix_pair(gathered.ring.far)
    mix_pair(gathered.ring.left)
    prev_out = pltpu.make_async_copy(prev, prev_ref, local.at[3])
    prev_out.start()
    delta_out = pltpu.make_async_copy(delta, delta_ref, local.at[4])
    delta_out.start()
    unit_out = pltpu.make_async_copy(unit, unit_ref, local.at[6])
    unit_out.start()
    for ring in (x_last, z_last):
        ring.wait_near()
        ring.wait_far()
    time_out = pltpu.make_async_copy(time, time_ref, local.at[5])
    time_out.start()

    def project(n, carry):
        to = pl.ds(pl.multiple_of(n * 256, 256), 256)
        for p, out in enumerate((r_ref, k_ref, v_ref, g_ref)):
            out[to] = nn(mix[p, to], time[p].reshape(16 * 128, own)).astype(out.dtype)
        return carry

    lax.fori_loop(0, 4, project, 0)
    results = [
        pltpu.make_async_copy(source, target, local.at[7 + n])
        for n, (source, target) in enumerate(
            ((r_ref, r_out), (k_ref, k_out), (v_ref, v_out), (g_ref, g_out), (set_ref, set_out))
        )
    ]
    for one in results:
        one.start()
    for one in channel:
        one.wait_recv()
    copy.wait_sent()
    for one in kept + results + [prev_out, delta_out, unit_out, time_out]:
        one.wait()


def opening(tokens, time_weights, channel_key, channel_value, channel_gate, vector_block, cid):
    rows, width = tokens.shape
    own = width // 8
    stripe = 2 * (channel_key.shape[1] // 8) + own
    shape = jax.ShapeDtypeStruct
    return pl.pallas_call(
        opening_kernel,
        name="opening",
        cost_estimate=cost(60),
        out_shape=[
            shape((8 * rows, own), low),
            shape((8 * rows, own), low),
            shape((8 * rows, own), low),
            shape((8 * rows, own), jnp.float32),
            shape((16, width), jnp.float32),
            shape((5, 4, 4, 128, own), low),
            shape((8 * rows, width), low),
            shape((8 * rows, width), low),
            shape((8 * rows, width), low),
            shape((128, stripe), low),
        ],
        in_specs=[VMEM] * 6,
        out_specs=[HBM] * 10,
        scratch_shapes=[
            pltpu.VMEM((8 * rows, own), low),
            pltpu.VMEM((8 * rows, own), low),
            pltpu.VMEM((8 * rows, own), low),
            pltpu.VMEM((8 * rows, own), jnp.float32),
            pltpu.VMEM((16, width), jnp.float32),
            pltpu.VMEM((9, rows, width), low),
            pltpu.VMEM((5, 4, 4, 128, own), low),
            pltpu.VMEM((4, 8 * rows, width), low),
            pltpu.VMEM((8 * rows, width), low),
            pltpu.VMEM((8 * rows, width), low),
            pltpu.VMEM((8 * rows, width), low),
            pltpu.VMEM((7, 16, 128), low),
            pltpu.VMEM((16, 128), low),
            pltpu.VMEM((16, 16, 128), low),
            pltpu.SemaphoreType.DMA((88,)),
            pltpu.SemaphoreType.DMA((88,)),
            pltpu.SemaphoreType.DMA((12,)),
        ],
        compiler_params=pltpu.CompilerParams(collective_id=cid, has_side_effects=True, vmem_limit_bytes=56 * 2**20),
    )(tokens, time_weights, channel_key, channel_value, channel_gate, vector_block)


class Scatter:
    def __init__(self, copy, p, out, from_sibling, mid, from_left, from_right, end_left, end_right):
        y, self.c, right, left, far = ring_places()
        self.order = (far, right, left, y)
        self.copy, self.p, self.out, self.from_sibling, self.mid = copy, p, out, from_sibling, mid
        self.from_left, self.from_right, self.end_left, self.end_right = from_left, from_right, end_left, end_right
        self.to_sibling, self.to_right, self.to_left = {"core": 1 - self.c}, {"y": right}, {"y": left}
        half = p.shape[1] // 2
        self.first, self.last = pl.ds(0, half), pl.ds(half, half)
        self.near = [None] * 4

    def send(self, src, dst, device):
        one = self.copy(src, dst, device)
        one.start()
        return one

    def share(self, k):
        self.near[k] = self.send(self.p.at[self.order[k] * 2 + 1 - self.c], self.from_sibling.at[k], self.to_sibling)

    def summed(self, k, rows):
        own = self.p[self.order[k] * 2 + self.c, rows].astype(jnp.float32)
        return own + self.from_sibling[k, rows].astype(jnp.float32)

    def far_out(self):
        self.near[0].wait_recv()
        self.mid[0] = self.summed(0, slice(None)).astype(low)
        self.far_right = self.send(self.mid.at[0, self.first], self.from_left, self.to_right)
        self.far_left = self.send(self.mid.at[0, self.last], self.from_right, self.to_left)

    def right_b(self):
        self.near[1].wait_recv()
        self.mid[1, self.last] = self.summed(1, self.last).astype(low)
        self.last_right = self.send(self.mid.at[1, self.last], self.end_left.at[self.last], self.to_right)

    def left_b(self):
        self.near[2].wait_recv()
        self.mid[2, self.first] = self.summed(2, self.first).astype(low)
        self.first_left = self.send(self.mid.at[2, self.first], self.end_right.at[self.first], self.to_left)

    def right_a(self):
        self.far_right.wait_recv()
        value = self.summed(1, self.first) + self.from_left[...].astype(jnp.float32)
        self.mid[1, self.first] = value.astype(low)
        self.first_right = self.send(self.mid.at[1, self.first], self.end_left.at[self.first], self.to_right)

    def left_a(self):
        self.far_left.wait_recv()
        value = self.summed(2, self.last) + self.from_right[...].astype(jnp.float32)
        self.mid[2, self.last] = value.astype(low)
        self.last_left = self.send(self.mid.at[2, self.last], self.end_right.at[self.last], self.to_left)

    def finish(self):
        self.near[3].wait_recv()
        self.last_right.wait_recv()
        self.first_left.wait_recv()
        self.first_right.wait_recv()
        self.last_left.wait_recv()
        from_ring = self.end_left[...].astype(jnp.float32) + self.end_right[...].astype(jnp.float32)
        self.out[...] = self.summed(3, slice(None)) + from_ring


def scatter_scratch(rows, cols):
    return [
        pltpu.VMEM((4, rows, cols), low),
        pltpu.VMEM((3, rows, cols), low),
        pltpu.VMEM((rows // 2, cols), low),
        pltpu.VMEM((rows // 2, cols), low),
        pltpu.VMEM((rows, cols), low),
        pltpu.VMEM((rows, cols), low),
    ]


def group_and_line():
    x = lax.axis_index("x")
    place, member, far, near, far_devices, near_devices = cube_places()
    return x, member, near, near_devices, {"x": lax.rem(x + 1, 4)}, {"x": lax.rem(x + 3, 4)}


class Tokens:
    def __init__(self, copy, slots, member):
        c = lax.axis_index("core")
        half = slots.shape[1] // 2
        self.copy, self.c, self.slots, self.to_sibling = copy, c, slots, {"core": 1 - c}
        self.ring = Ring(copy, "y", lambda at, n: slots.at[at * 2 + c, pl.ds(n * half, half)])
        self.near = copy(slots.at[member], slots.at[member], self.to_sibling)
        self.near.start()

    def pass_on(self, at):
        one = self.copy(self.slots.at[at * 2 + self.c], self.slots.at[at * 2 + self.c], self.to_sibling)
        one.start()
        return one

    def wait_next(self):
        self.ring.wait_near()
        self.passed = [self.pass_on(self.ring.right), self.pass_on(self.ring.left)]

    def wait_passed(self, near=True):
        if near:
            self.near.wait_recv()
        for one in self.passed:
            one.wait_recv()

    def next_pairs(self, near=True):
        self.ring.forward()
        self.wait_next()
        self.wait_passed(near)

    def far_pair(self):
        self.ring.wait_far()
        self.passed.append(self.pass_on(self.ring.far))
        self.passed[-1].wait_recv()

    def copies(self):
        return self.ring.near + [self.ring.far_right, self.ring.far_left, self.near] + self.passed


class Blend:
    def __init__(self, copy, terms, coefficients, delta, p, sums, firsts, to_previous):
        self.terms, self.coefficients, self.delta, self.p, self.sums, self.firsts = terms, coefficients, delta, p, sums, firsts
        self.edge = copy(firsts.at[0], firsts.at[4], to_previous)

    def pair(self, q):
        step = 512
        row = lax.broadcasted_iota(jnp.int32, (16, step), 0)
        for s in range(2):

            def columns(k, carry):
                lanes = pl.ds(pl.multiple_of(k * step, step), step)
                factors = [ref[n : n + 1, lanes] for ref, n in self.coefficients]
                added = [0.0] * len(factors)
                following = jnp.zeros((1, step), jnp.float32)
                for b in (1, 0):
                    for t in reversed(range(BLOCK_LEN // 16)):
                        at = s * BLOCK_LEN + t * 16
                        rows = slice(b * 2 * BLOCK_LEN + at, b * 2 * BLOCK_LEN + at + 16)
                        gap = self.delta[pl.ds(pl.multiple_of(q * 4 * BLOCK_LEN + b * 2 * BLOCK_LEN + at, 16), 16), lanes]
                        gap = gap.astype(jnp.float32)
                        here, whole = 0.0, 0.0
                        for n, factor in enumerate(factors):
                            term = self.terms[n, rows, lanes]
                            here = here + factor * term
                            whole = whole + term
                            product = gap * term
                            added[n] = added[n] + product[:8] + product[8:]
                        behind = whole - here
                        moved = jnp.where(row == 15, following, pltpu.roll(behind, 15, 0))
                        self.p[q * 2 + b, at : at + 16, lanes] = (here + moved).astype(low)
                        following = behind[0:1]
                for n, value in enumerate(added):
                    self.sums[n, :, lanes] += value
                self.firsts[q, s, 0:1, lanes] = following
                return carry

            lax.fori_loop(0, self.p.shape[2] // step, columns, 0)

        @pl.when(q == 0)
        def _():
            self.edge.start()

    def close(self, q):
        @pl.when(q == 3)
        def _():
            self.edge.wait_recv()

        row = lax.broadcasted_iota(jnp.int32, (16, self.p.shape[2]), 0)
        for s in range(2):
            following = self.firsts[q + 1, s, 0:1, :]
            following = jnp.where(jnp.logical_and(q == 3, lax.axis_index("x") == 3), 0.0, following)
            rows = slice(s * BLOCK_LEN + BLOCK_LEN - 16, (s + 1) * BLOCK_LEN)
            value = self.p[q * 2 + 1, rows].astype(jnp.float32)
            self.p[q * 2 + 1, rows] = (value + jnp.where(row == 15, following, 0.0)).astype(low)


def channel_kernel(
    own_hbm, hidden_hbm, cot_hbm, mask_ref, w_hbm, set_hbm,
    out_ref, up_ref, grad_ref, sums_ref, dw_ref,
    hidden_ref, cot_ref, set_ref, slots, w, ckey, cgate, delta, rect, hidden, gown, pre, gg, gg_own, gkey, terms, p, value, sums, firsts, dw,
    from_sibling, mid, from_left, from_right, end_left, end_right, send, recv, local,
):
    x, member, near, near_devices, to_next, to_previous = group_and_line()
    loads = [
        pltpu.make_async_copy(source, target, local.at[3 + n])
        for n, (source, target) in enumerate(
            ((own_hbm, slots.at[member]), (set_hbm, set_ref), (hidden_hbm, hidden_ref), (cot_hbm, cot_ref))
        )
    ]
    for one in loads:
        one.start()
    y, c, right, left, far = ring_places()
    firsts[0:4] = jnp.zeros_like(firsts[0:4])
    sums[...] = jnp.zeros_like(sums)
    greet(near_devices + [to_next, to_previous])
    copy = Copies(send, recv)
    load = pltpu.make_async_copy(w_hbm, w, local.at[0])
    load.start()
    for one in loads:
        one.wait()
    gathered = Tokens(copy, slots, member)
    wide = rect.shape[1]
    cols = gown.shape[2]
    step = 512
    row = lax.broadcasted_iota(jnp.int32, (16, step), 0)
    edges = [
        copy(slots.at[7, pl.ds(s * BLOCK_LEN + BLOCK_LEN - 16, 16)], slots.at[8, pl.ds(s * BLOCK_LEN + BLOCK_LEN - 16, 16)], to_next)
        for s in range(2)
    ]

    def compute(q):
        @pl.when(q == 0)
        def _():
            for one in edges:
                one.wait_recv()

        for b in range(2):
            j = q * 2 + b
            for s in range(2):
                before_slot = jnp.where(j == 0, 8, j - 1)
                last = slice(s * BLOCK_LEN + BLOCK_LEN - 16, (s + 1) * BLOCK_LEN)

                def columns(n, carry):
                    lanes = pl.ds(pl.multiple_of(n * step, step), step)
                    before = slots[before_slot, last, lanes].astype(jnp.float32)[15:16]
                    before = jnp.where(jnp.logical_and(j == 0, x == 0), 0.0, before)
                    for t in range(BLOCK_LEN // 16):
                        at = s * BLOCK_LEN + t * 16
                        values = slots[j, at : at + 16, lanes].astype(jnp.float32)
                        moved = jnp.where(row == 0, before, pltpu.roll(values, 1, 0))
                        before = values[15:16]
                        gap = values - moved
                        to = pl.ds(pl.multiple_of(j * 2 * BLOCK_LEN + at, 16), 16)
                        delta[to, lanes] = gap.astype(low)
                        ckey[to, lanes] = (moved + set_ref[11:12, lanes] * gap).astype(low)
                        cgate[to, lanes] = (moved + set_ref[12:13, lanes] * gap).astype(low)
                    return carry

                lax.fori_loop(0, w_hbm.shape[0] // step, columns, 0)
        rows = pl.ds(pl.multiple_of(q * 256, 256), 256)
        kept = jnp.maximum(nn(ckey[rows], w[:, :wide]), 0.0)
        rect[rows] = kept.astype(low)
        hidden[rows] = (kept * kept).astype(low)
        part = nt(hidden[rows], w[:, wide : 2 * wide]).astype(low)
        early = nn(cgate[rows], w[:, 2 * wide :]).astype(low)
        for b in range(2):
            p[q * 2 + b] = part[b * 128 : (b + 1) * 128]
            gown[q * 2 + b] = early[b * 128 : (b + 1) * 128]

    gates = []

    def give_gate(j):
        one = copy(gown.at[j], pre.at[member], {"y": j // 2, "core": lax.rem(j, 2)})
        one.start()
        gates.append(one)

    buffers = (from_sibling, mid, from_left, from_right, end_left, end_right)
    total = Scatter(copy, p, value, *buffers)
    gathered.next_pairs()

    @pl.when(y != 1)
    def _():
        for one in edges:
            one.start()

    load.wait()
    compute(right)
    total.share(1)
    compute(y)
    total.share(3)
    gathered.far_pair()

    @pl.when(y == 1)
    def _():
        for one in edges:
            one.start()

    copy.wait_sent(edges)
    for turn in range(2):
        give_gate(right * 2 + lax.rem(c + turn, 2))
    give_gate(y * 2 + 1 - c)
    compute(far)
    total.share(0)
    total.right_b()
    compute(left)
    copy.wait_sent(gathered.copies())
    total.share(2)
    total.far_out()
    total.left_b()
    for at in (left, far):
        for turn in range(2):
            give_gate(at * 2 + lax.rem(c + turn, 2))
    pre[member] = gown[member]
    total.right_a()
    total.left_a()
    total.finish()
    for one in gates:
        one.wait_recv()
    copy.wait_sent()

    def gate_block(n, carry):
        at = pl.ds(pl.multiple_of(n * cols, cols), cols)
        gate = jax.nn.sigmoid(pre[n].astype(jnp.float32))
        up = cot_ref[:, at].astype(jnp.float32) * mask_ref[...]
        up_ref[:, at] = up
        out_ref[:, at] = (hidden_ref[:, at] + gate * value[:, at]).astype(low)
        slots[member, :, at] = (up * gate).astype(low)
        gg_own[n] = (up * value[:, at] * gate * (1.0 - gate)).astype(low)
        return carry

    lax.fori_loop(0, 8, gate_block, 0)

    gates = [copy(gg_own.at[at], gg.at[member], d) for at, d in zip(near, near_devices)]
    for one in gates:
        one.start()
    gathered = Tokens(copy, slots, member)
    gg[member] = gg_own[member]
    blend = Blend(copy, terms, [(set_ref, 11), (set_ref, 12)], delta, p, sums, firsts, to_previous)

    def compute_back(q):
        rows = pl.ds(pl.multiple_of(q * 256, 256), 256)
        pair = pl.ds(q * 2, 2)
        grad_hidden = nn(slots[pair].reshape(256, slots.shape[2]), w[:, wide : 2 * wide])
        gkey[rows] = (2.0 * grad_hidden * rect[rows].astype(jnp.float32)).astype(low)
        terms[0] = nt(gkey[rows], w[:, :wide])
        terms[1] = nt(gg[pair].reshape(256, cols), w[:, 2 * wide :])
        blend.pair(q)

    total = Scatter(copy, p, grad_ref, *buffers)
    gathered.near.wait_recv()
    for one in gates:
        one.wait_recv()
    compute_back(y)
    gathered.next_pairs(False)
    compute_back(right)
    blend.close(y)
    total.share(3)
    compute_back(left)
    blend.close(left)
    total.share(2)
    gathered.far_pair()
    total.left_b()
    compute_back(far)
    blend.close(far)
    total.share(0)
    blend.close(right)
    total.share(1)
    total.far_out()
    total.right_b()

    def give(block, slot):
        at = pl.ds(pl.multiple_of(block * 256, 256), 256)
        return pltpu.make_async_copy(dw.at[slot], dw_ref.at[at], local.at[1 + slot])

    def weight_blocks(n, carry):
        for slot in range(2):
            block = n * 2 + slot
            at = pl.ds(pl.multiple_of(block * 256, 256), 256)

            @pl.when(n > 0)
            def _():
                give(block - 2, slot).wait()

            dw[slot, :, :wide] = tn(ckey[:, at], gkey[...]).astype(low)
            dw[slot, :, wide : 2 * wide] = tn(slots[0:8, :, at].reshape(8 * 128, 256), hidden[...]).astype(low)
            dw[slot, :, 2 * wide :] = tn(cgate[:, at], gg[...].reshape(8 * 128, cols)).astype(low)
            give(block, slot).start()
        return carry

    lax.fori_loop(0, 2, weight_blocks, 0)
    total.right_a()
    total.left_a()
    lax.fori_loop(2, 4, weight_blocks, 0)
    for n in range(2):
        sums_ref[n : n + 1, :] = jnp.sum(sums[n], axis=0, keepdims=True)
    sums_ref[2:8, :] = jnp.zeros((6, sums_ref.shape[1]), jnp.float32)
    total.finish()
    copy.wait_sent()
    for slot in range(2):
        give(6 + slot, slot).wait()


def channel(own, hidden_one, cotangent, mask, weights, settings, cid):
    rows, width = own.shape
    cols = width // 8
    wide = (weights.shape[1] - cols) // 2
    shape = jax.ShapeDtypeStruct
    big = pltpu.VMEM((8 * rows, width), low)
    mid = pltpu.VMEM((8 * rows, wide), low)
    small = pltpu.VMEM((8, rows, cols), low)
    return pl.pallas_call(
        channel_kernel,
        name="channel",
        cost_estimate=cost(120),
        out_shape=[
            shape((rows, width), low),
            shape((rows, width), jnp.float32),
            shape((rows, width), jnp.float32),
            shape((8, width), jnp.float32),
            shape(weights.shape, low),
        ],
        in_specs=[HBM] * 3 + [VMEM] + [HBM] * 2,
        out_specs=[VMEM] * 4 + [HBM],
        scratch_shapes=[
            pltpu.VMEM((rows, width), jnp.float32),
            pltpu.VMEM((rows, width), low),
            pltpu.VMEM(settings.shape, jnp.float32),
            pltpu.VMEM((9, rows, width), low),
            pltpu.VMEM(weights.shape, low),
            big,
            big,
            big,
            mid,
            mid,
            small,
            small,
            small,
            small,
            mid,
            pltpu.VMEM((2, 256, width), jnp.float32),
            pltpu.VMEM((8, rows, width), low),
            pltpu.VMEM((rows, width), jnp.float32),
            pltpu.VMEM((2, 8, width), jnp.float32),
            pltpu.VMEM((5, 2, 8, width), jnp.float32),
            pltpu.VMEM((2, 256, weights.shape[1]), low),
            *scatter_scratch(rows, width),
            pltpu.SemaphoreType.DMA((70,)),
            pltpu.SemaphoreType.DMA((70,)),
            pltpu.SemaphoreType.DMA((7,)),
        ],
        compiler_params=pltpu.CompilerParams(collective_id=cid, has_side_effects=True, vmem_limit_bytes=59 * 2**20),
    )(own, hidden_one, cotangent, mask, weights, settings)


def middle_kernel(
    second_ref, hidden_ref, up_ref, set_ref, column_ref, params_ref,
    g_ref, scaled_ref, inverse_ref, r_ref, k_ref, v_ref, w_ref, in_ref, time_hbm, prev_hbm, delta_hbm, gated_hbm,
    upper_ref, proj_ref, vec_ref, sums_ref, dw_ref,
    time, prev, delta, gated, out, out_all, p, gg, dw, norm_sums, part_k, part_v, suffix, total, slots, sums,
    from_sibling, mid, from_left, from_right, end_left, end_right, send, recv, local,
):
    x, member, near, near_devices, _, _ = group_and_line()
    y, c, right, left, far = ring_places()
    greet(near_devices + [{"x": lax.rem(x + n, 4)} for n in range(1, 4)])
    copy = Copies(send, recv)
    cols = g_ref.shape[1]
    loads = [
        pltpu.make_async_copy(src, dst, local.at[n])
        for n, (src, dst) in enumerate(
            ((time_hbm.at[3:5], time.at[1:3]), (time_hbm.at[0:1], time.at[0:1]), (gated_hbm, gated), (prev_hbm, prev), (delta_hbm, delta))
        )
    ]
    for one in loads:
        one.start()

    norm_sums[...] = jnp.zeros_like(norm_sums)

    def norm_rows(t, carry):
        rows = pl.ds(pl.multiple_of(t * 16, 16), 16)
        values = hidden_ref[rows]
        center = values - jnp.mean(values, axis=-1, keepdims=True)
        inverse = lax.rsqrt(jnp.mean(center * center, axis=-1, keepdims=True) + epsilon)
        unit = center * inverse
        grad = second_ref[rows]
        product = grad * unit
        norm_sums[0] += product[:8] + product[8:]
        norm_sums[1] += grad[:8] + grad[8:]
        inner = grad * set_ref[9:10, :]
        mean = jnp.mean(inner, axis=-1, keepdims=True)
        along = jnp.mean(inner * unit, axis=-1, keepdims=True)
        upper = up_ref[rows] + inverse * (inner - mean - unit * along)
        upper_ref[rows] = upper
        for n in range(8):
            out[n, rows] = upper[:, n * cols : (n + 1) * cols].astype(low)
        return carry

    lax.fori_loop(0, 8, norm_rows, 0)
    given = [copy(out.at[at], out_all.at[member], d) for at, d in zip(near, near_devices)]
    for one in given:
        one.start()
    out_all[member] = out[member]
    for n in range(2):
        vec_ref[n : n + 1, :] = jnp.sum(norm_sums[n], axis=0, keepdims=True)
    vec_ref[4:8, :] = jnp.zeros((4, vec_ref.shape[1]), jnp.float32)
    sums[...] = jnp.zeros_like(sums)
    for one in loads:
        one.wait()
    for one in given:
        one.wait_recv()

    def through(q):
        for b in range(2):
            m = q * 2 + b
            rows = pl.ds(pl.multiple_of(m * cols, cols), cols)
            p[m] = nt(out_all[...].reshape(8 * 128, cols), time[2, rows]).astype(low)

    def out_block(m, carry):
        rows = pl.ds(pl.multiple_of(m * cols, cols), cols)
        dw[rows, 2 * cols : 3 * cols] = tn(gated[m], out_all[...].reshape(8 * 128, cols)).astype(low)
        return carry

    total_gg = Scatter(copy, p, gg, from_sibling, mid, from_left, from_right, end_left, end_right)
    through(far)
    total_gg.share(0)
    through(right)
    total_gg.share(1)
    through(left)
    total_gg.share(2)
    total_gg.far_out()
    total_gg.right_b()
    total_gg.left_b()
    through(y)
    total_gg.share(3)
    lax.fori_loop(0, 4, out_block, 0)
    total_gg.right_a()
    total_gg.left_a()
    lax.fori_loop(4, 8, out_block, 0)
    total_gg.finish()

    log_row, bonus, gain, bias = [params_ref[n : n + 1, :] for n in range(4)]
    mask, eye, enter, leave, same = head_tables(log_row)
    block_decay = jnp.exp(BLOCK_LEN * log_row)
    ones = jnp.where(same, 1.0, 0.0).astype(low)

    def first(m, carry):
        for s in range(2):
            rows = block_rows(m, s)
            gate, grad, scaled = g_ref[rows], gg[rows], scaled_ref[rows]
            sigma = jax.nn.sigmoid(gate)
            grad_normed = grad * gate * sigma
            proj_ref[3, rows] = (grad * (scaled * gain + bias) * sigma * (1.0 + gate * (1.0 - sigma))).astype(low)
            inner = grad_normed * gain
            wide = inverse_ref[rows] * (inner - head_mean(inner, same) - scaled * head_mean(inner * scaled, same))
            grad_wkv = wide.astype(low)
            r, k, v = r_ref[rows], k_ref[rows], v_ref[rows]
            r_wide, k_wide = r.astype(jnp.float32), k.astype(jnp.float32)
            grad_weights = nt(grad_wkv, expand(v, same)).astype(low).astype(jnp.float32)
            masked = (grad_weights * mask).astype(low)
            own = nn(jnp.where(eye, grad_weights, 0.0).astype(low), ones)
            grad_r = nn(masked, expand(k, same)) + own * bonus * k_wide
            grad_r = grad_r + nt(grad_wkv, expand(in_ref[m * 2 + s], same)) * enter
            proj_ref[0, rows] = grad_r.astype(low)
            part_k[rows] = compress(tn(masked, r), same) + own * bonus * r_wide
            part_v[rows] = compress(tn(w_ref[rows], grad_wkv), same)
            suffix[m * 2 + s] = compress(tn((r_wide * enter).astype(low), grad_wkv), same)
            sums[0] += own * r_wide * k_wide
            sums[1] += grad_normed * scaled
            sums[2] += grad_normed
        return carry

    lax.fori_loop(0, 8, first, 0)

    def chain(n, states):
        m = 7 - n
        after = []
        for s in range(2):
            here = suffix[m * 2 + s]
            suffix[m * 2 + s] = states[s]
            after.append(states[s] * block_decay + here)
        return tuple(after)

    zero = jnp.zeros(enter.shape, jnp.float32)
    states = lax.fori_loop(0, 8, chain, (zero, zero))
    for s in range(2):
        total[s] = states[s]
    line = start_line(total, slots, send.at[pl.ds(40, 3)], recv.at[pl.ds(40, 3)])

    def gate_block(n, carry):
        rows = pl.ds(pl.multiple_of(n * cols, cols), cols)
        prev_block, delta_block = prev[:, rows].T, delta[:, rows].T
        column = column_ref[rows]
        for n, source in enumerate((0, 3)):
            by_delta = nn(delta_block, proj_ref[source])
            grads = nn(prev_block, proj_ref[source]) + column[:, 2 + source : 3 + source] * by_delta
            dw[rows, n * cols : (n + 1) * cols] = grads.astype(low)
            product = (time[n, rows].astype(jnp.float32) * by_delta).astype(low)
            vec_ref[2 + n : 3 + n, rows] = nt(jnp.ones((8, cols), low), product)[0:1]
        return carry

    lax.fori_loop(0, 8, gate_block, 0)
    give = pltpu.make_async_copy(dw, dw_ref, local.at[5])
    give.start()
    for one in line:
        one.wait()
    x_place = lax.axis_index("x")
    leaving = [zero, zero]
    span_decay = jnp.exp(8.0 * BLOCK_LEN * log_row)
    for x in (3, 2, 1):
        for s in range(2):
            leaving[s] = jnp.where(x > x_place, leaving[s] * span_decay + slots[x, s], leaving[s])
    for s in range(2):
        total[s] = leaving[s]

    def second(m, carry):
        power = jnp.exp(((7 - m) * BLOCK_LEN).astype(jnp.float32) * log_row)
        for s in range(2):
            rows = block_rows(m, s)
            state = expand((suffix[m * 2 + s] + power * total[s]).astype(low), same)
            key_leave = (k_ref[rows].astype(jnp.float32) * leave).astype(low)
            proj_ref[1, rows] = (part_k[rows] + nt(v_ref[rows], state) * leave).astype(low)
            proj_ref[2, rows] = (part_v[rows] + nn(key_leave, state)).astype(low)
        return carry

    lax.fori_loop(0, 8, second, 0)


    for n in range(3):
        sums_ref[n : n + 1, :] = jnp.sum(sums[n], axis=0, keepdims=True)
    sums_ref[3:8, :] = jnp.zeros((5, cols), jnp.float32)
    copy.wait_sent()
    give.wait()


def middle(second, hidden, up, settings, columns, params, g, scaled, inverse, r, k, v, w, states, time, prev, delta, gated, cid):
    rows, width = second.shape
    cols = g.shape[1]
    tall = pltpu.VMEM((8 * rows, cols), jnp.float32)
    shape = jax.ShapeDtypeStruct
    return pl.pallas_call(
        middle_kernel,
        name="middle",
        out_shape=[
            shape((rows, width), jnp.float32),
            shape((4, 8 * rows, cols), low),
            shape((8, width), jnp.float32),
            shape((8, cols), jnp.float32),
            shape((width, 3 * cols), low),
        ],
        in_specs=[VMEM] * 14 + [HBM] * 4,
        out_specs=[VMEM] * 4 + [HBM],
        scratch_shapes=[
            pltpu.VMEM((3, width, cols), low),
            pltpu.VMEM(prev.shape, low),
            pltpu.VMEM(delta.shape, low),
            pltpu.VMEM(gated.shape, low),
            pltpu.VMEM((8, rows, cols), low),
            pltpu.VMEM((8, rows, cols), low),
            pltpu.VMEM((8, 8 * rows, cols), low),
            tall,
            pltpu.VMEM((width, 3 * cols), low),
            pltpu.VMEM((2, 8, width), jnp.float32),
            tall,
            tall,
            pltpu.VMEM((16, BLOCK_LEN, cols), jnp.float32),
            pltpu.VMEM((2, BLOCK_LEN, cols), jnp.float32),
            pltpu.VMEM((4, 2, BLOCK_LEN, cols), jnp.float32),
            pltpu.VMEM((3, BLOCK_LEN, cols), jnp.float32),
            *scatter_scratch(8 * rows, cols),
            pltpu.SemaphoreType.DMA((43,)),
            pltpu.SemaphoreType.DMA((43,)),
            pltpu.SemaphoreType.DMA((6,)),
        ],
        compiler_params=pltpu.CompilerParams(collective_id=cid, has_side_effects=True, vmem_limit_bytes=58 * 2**20),
    )(second, hidden, up, settings, columns, params, g, scaled, inverse, r, k, v, w, states, time, prev, delta, gated)


class RingScatter:
    def __init__(self, copy, axis, part, halves, bufs):
        me = lax.axis_index(axis)
        right, left, self.far = [lax.rem(me + k, 4) for k in (1, 3, 2)]
        self.me, self.right, self.left, self.part, self.halves, self.copy = me, right, left, part, halves, copy
        self.to_right, self.to_left = {axis: right}, {axis: left}
        self.from_left, self.from_right, self.end_left, self.end_right = bufs

    def send(self, src, dst, device):
        one = self.copy(src, dst, device)
        one.start()
        return one

    def far_out(self):
        first, last = self.halves
        self.far_right = self.send(self.part(self.far).at[first], self.from_left, self.to_right)
        self.far_left = self.send(self.part(self.far).at[last], self.from_right, self.to_left)

    def near_out(self):
        first, last = self.halves
        self.last_right = self.send(self.part(self.right).at[last], self.end_left.at[last], self.to_right)
        self.first_left = self.send(self.part(self.left).at[first], self.end_right.at[first], self.to_left)

    def pass_on(self):
        first, last = self.halves
        self.far_right.wait_recv()
        here = self.part(self.right).at[first]
        here[...] = (here[...].astype(jnp.float32) + self.from_left[...].astype(jnp.float32)).astype(low)
        self.first_right = self.send(here, self.end_left.at[first], self.to_right)
        self.far_left.wait_recv()
        here = self.part(self.left).at[last]
        here[...] = (here[...].astype(jnp.float32) + self.from_right[...].astype(jnp.float32)).astype(low)
        self.last_left = self.send(here, self.end_right.at[last], self.to_left)

    def finish(self, out):
        for one in (self.last_right, self.first_left, self.first_right, self.last_left):
            one.wait_recv()
        value = self.part(self.me)[...].astype(jnp.float32) + self.end_left[...].astype(jnp.float32)
        out[...] = (value + self.end_right[...].astype(jnp.float32)).astype(low)


def closing_kernel(
    grad_ref, early_hbm, time_hbm, prev_hbm, delta_hbm, unit_hbm, set_ref, column_ref, tok_hbm, upper_hbm, own_ref, middle_ref, channel_ref,
    token_ref, weight_ref, total_ref,
    time, scaled, prev, delta, unit, early, terms, p, firsts, one_dw, other_dw, one_sum, other_sum, stripe, gathered, parts,
    one_a, one_b, one_c, one_d, other_a, other_b, other_c, other_d,
    one_e, one_f, one_g, one_h, other_e, other_f, other_g, other_h,
    early_a, early_b, early_c, early_d, early_e, early_f, early_g, early_h,
    early_i, early_j, early_k, early_l, early_m, early_n, early_o, early_p, early_one, early_other, vec_far, vec_near, vec_stripe, norm_sums,
    from_sibling, mid, from_left, from_right, end_left, end_right, send, recv, local,
):
    place, member, far_places, near_members, far_devices, near_devices = cube_places()
    x = lax.axis_index("x")
    y, c, right, left, far = ring_places()
    to_previous = {"x": lax.rem(x + 3, 4)}
    firsts[0:4] = jnp.zeros_like(firsts[0:4])
    greet(far_devices + near_devices)
    copy = Copies(send, recv)
    cols = grad_ref.shape[2]
    loads = [
        pltpu.make_async_copy(src, dst, local.at[n])
        for n, (src, dst) in enumerate(
            ((time_hbm.at[0:4], time), (early_hbm, early), (unit_hbm, unit), (prev_hbm, prev), (delta_hbm, delta))
        )
    ]
    for one in loads:
        one.start()
    slots = (pl.ds(0, 2), pl.ds(2, 2))
    halves = (pl.ds(0, 64), pl.ds(64, 64))
    side = early.shape[3] // 2
    parts[...] = jnp.zeros_like(parts)
    parts[2:3, :] = middle_ref[2:3, :]
    parts[5:6, :] = middle_ref[3:4, :]
    parts[6:9, pl.ds(pl.multiple_of(member * cols, cols), cols)] = own_ref[0:3, :]
    parts[9:11, :] = middle_ref[0:2, :]
    parts[11:13, :] = channel_ref[0:2, :]
    norm_sums[...] = jnp.zeros_like(norm_sums)
    loads[0].wait()
    loads[1].wait()
    early_z = RingScatter(copy, "z", lambda at: early.at[at, :, :, 0:side], slots, (early_a, early_b, early_c, early_d))
    early_x = RingScatter(
        copy, "x", lambda at: early.at[:, at, :, side : 2 * side], slots, (early_e, early_f, early_g, early_h)
    )
    for ring in (early_z, early_x):
        ring.far_out()
        ring.near_out()

    def scale_block(n, carry):
        rows = pl.ds(pl.multiple_of(n * 256, 256), 256)
        column = column_ref[rows]
        for k in range(4):
            scaled[k, rows] = (column[:, 2 + k : 3 + k] * time[k, rows].astype(jnp.float32)).astype(low)
        return carry

    lax.fori_loop(0, 8, scale_block, 0)
    for one in loads[2:]:
        one.wait()

    ones = jnp.ones((8, cols), low)

    def weight_block(at):
        def part(h, carry):
            block = at * 2 + h
            rows = pl.ds(pl.multiple_of(block * 256, 256), 256)
            prev_block, delta_block = prev[:, rows].T, delta[:, rows].T
            column = column_ref[rows]
            grads = []
            for n in (1, 2):
                by_delta = nn(delta_block, grad_ref[n])
                factor = column[:, 2 + n : 3 + n]
                grads.append((nn(prev_block, grad_ref[n]) + factor * by_delta).astype(low))
                weight = time[n, rows].astype(jnp.float32)
                parts[2 + n : 3 + n, rows] = nt(ones, (weight * by_delta).astype(low))[0:1]
            whole = jnp.concatenate(grads, axis=1)
            half = whole.shape[1] // 2
            for k in range(2):
                one_dw[at, h * 2 + k] = whole[k * 128 : (k + 1) * 128, :half]
                other_dw[at, h * 2 + k] = whole[k * 128 : (k + 1) * 128, half:]
            return carry

        lax.fori_loop(0, 2, part, 0)

    z_first = RingScatter(copy, "z", lambda at: one_dw.at[at], slots, (one_a, one_b, one_c, one_d))
    x_first = RingScatter(copy, "x", lambda at: other_dw.at[:, at], slots, (other_a, other_b, other_c, other_d))

    step = 512
    edge = copy(firsts.at[0], firsts.at[4], to_previous)

    def compute(q):
        rows = pl.ds(pl.multiple_of(q * 256, 256), 256)
        whole, here = 0.0, 0.0
        for n in range(4):
            whole = whole + nt(grad_ref[n, rows], time[n])
            here = here + nt(grad_ref[n, rows], scaled[n])
        terms[0] = here
        terms[1] = whole - here
        row = lax.broadcasted_iota(jnp.int32, (16, step), 0)
        for s in range(2):

            def columns(k, carry):
                lanes = pl.ds(pl.multiple_of(k * step, step), step)
                following = jnp.zeros((1, step), jnp.float32)
                added = [0.0, 0.0]
                for b in (1, 0):
                    for t in reversed(range(BLOCK_LEN // 16)):
                        at = s * BLOCK_LEN + t * 16
                        rows = slice(b * 2 * BLOCK_LEN + at, b * 2 * BLOCK_LEN + at + 16)
                        behind = terms[1, rows, lanes]
                        value = terms[0, rows, lanes] + jnp.where(row == 15, following, pltpu.roll(behind, 15, 0))
                        following = behind[0:1]
                        p[q * 2 + b, at : at + 16, lanes] = value.astype(low)
                        product = value * unit[
                            pl.ds(pl.multiple_of(q * 4 * BLOCK_LEN + b * 2 * BLOCK_LEN + at, 16), 16), lanes
                        ].astype(jnp.float32)
                        added = [added[0] + product[:8] + product[8:], added[1] + value[:8] + value[8:]]
                for n in range(2):
                    norm_sums[n, :, lanes] += added[n]
                firsts[q, s, 0:1, lanes] = following
                return carry

            lax.fori_loop(0, p.shape[2] // step, columns, 0)

        @pl.when(q == 0)
        def _():
            edge.start()

    def close(q):
        @pl.when(q == 3)
        def _():
            edge.wait_recv()

        row = lax.broadcasted_iota(jnp.int32, (16, p.shape[2]), 0)
        for s in range(2):
            following = firsts[q + 1, s, 0:1, :]
            following = jnp.where(jnp.logical_and(q == 3, x == 3), 0.0, following)
            rows = slice(s * BLOCK_LEN + BLOCK_LEN - 16, (s + 1) * BLOCK_LEN)
            value = p[q * 2 + 1, rows].astype(jnp.float32)
            p[q * 2 + 1, rows] = (value + jnp.where(row == 15, following, 0.0)).astype(low)
            last = pl.ds(pl.multiple_of(q * 4 * BLOCK_LEN + 2 * BLOCK_LEN + s * BLOCK_LEN + BLOCK_LEN - 16, 16), 16)
            norm_sums[0, 0:1, :] += following * unit[last].astype(jnp.float32)[15:16]
            norm_sums[1, 0:1, :] += following

    total = Scatter(copy, p, terms.at[1, pl.ds(0, p.shape[1])], from_sibling, mid, from_left, from_right, end_left, end_right)
    compute(left)
    compute(far)
    close(far)
    total.share(0)
    early_z.pass_on()
    early_x.pass_on()
    weight_block(z_first.far)
    z_first.far_out()
    total.far_out()
    weight_block(z_first.right)
    weight_block(z_first.left)
    z_first.near_out()
    weight_block(z_first.me)
    x_first.far_out()
    x_first.near_out()
    early_z.finish(early_one)
    early_x.finish(early_other)
    early_last_x = RingScatter(copy, "x", lambda at: early_one.at[at], halves, (early_i, early_j, early_k, early_l))
    early_last_z = RingScatter(copy, "z", lambda at: early_other.at[at], halves, (early_m, early_n, early_o, early_p))
    for ring in (early_last_x, early_last_z):
        ring.far_out()
        ring.near_out()
    compute(right)
    close(right)
    total.share(1)
    z_first.pass_on()
    x_first.pass_on()
    total.right_b()
    compute(y)
    rest = [
        pltpu.make_async_copy(upper_hbm, terms.at[0, pl.ds(0, p.shape[1])], local.at[5]),
        pltpu.make_async_copy(tok_hbm, delta.at[pl.ds(0, p.shape[1])], local.at[6]),
    ]
    for one in rest:
        one.start()
    close(left)
    total.share(2)
    close(y)
    total.share(3)
    total.left_b()
    total.right_a()
    total.left_a()
    early_last_x.pass_on()
    early_last_z.pass_on()
    for n in range(2):
        parts[n : n + 1, :] = jnp.sum(norm_sums[n], axis=0, keepdims=True)
    vec_first = [
        copy(parts.at[:, pl.ds(pl.multiple_of(at * 128, 128), 128)], vec_far.at[n], d)
        for n, (at, d) in enumerate(zip(far_places, far_devices))
    ]
    for one in vec_first:
        one.start()
    z_first.finish(one_sum)
    x_last = RingScatter(copy, "x", lambda at: one_sum.at[at], halves, (one_e, one_f, one_g, one_h))
    x_last.far_out()
    x_last.near_out()
    x_first.finish(other_sum)
    z_last = RingScatter(copy, "z", lambda at: other_sum.at[at], halves, (other_e, other_f, other_g, other_h))
    z_last.far_out()
    z_last.near_out()
    early_last_x.finish(stripe.at[:, 2 * cols : 2 * cols + side])
    early_last_z.finish(stripe.at[:, 2 * cols + side : 2 * cols + 2 * side])
    x_last.pass_on()
    z_last.pass_on()
    half = one_sum.shape[2]
    x_last.finish(stripe.at[:, 0:half])
    z_last.finish(stripe.at[:, half : 2 * half])
    given = [
        copy(stripe.at[pl.ds(pl.multiple_of(at * 16, 16), 16)], gathered.at[member], d)
        for at, d in zip(near_members, near_devices)
    ]
    for one in given:
        one.start()
    gathered[member] = stripe[pl.ds(pl.multiple_of(member * 16, 16), 16)]
    sum_all = parts[:, pl.ds(pl.multiple_of(place * 128, 128), 128)]
    for n, one in enumerate(vec_first):
        one.wait_recv()
        sum_all = sum_all + vec_far[n]
    vec_stripe[...] = sum_all
    vec_last = [copy(vec_stripe, vec_near.at[n], d) for n, d in enumerate(near_devices)]
    for one in vec_last:
        one.start()
    total.finish()

    def norm_rows(t, carry):
        rows = pl.ds(pl.multiple_of(t * 16, 16), 16)
        values = delta[rows].astype(jnp.float32)
        center = values - jnp.mean(values, axis=-1, keepdims=True)
        inverse = lax.rsqrt(jnp.mean(center * center, axis=-1, keepdims=True) + epsilon)
        scaled_row = center * inverse
        inner = terms[1, rows] * set_ref[0:1, :]
        mean = jnp.mean(inner, axis=-1, keepdims=True)
        along = jnp.mean(inner * scaled_row, axis=-1, keepdims=True)
        token_ref[rows] = (terms[0, rows] + inverse * (inner - mean - scaled_row * along)).astype(low)
        return carry

    for one in rest:
        one.wait()
    lax.fori_loop(0, 8, norm_rows, 0)
    for one in given:
        one.wait_recv()
    for m in range(8):
        for n, source in enumerate((2, 0, 1, 3, 4)):
            block = gathered[m, :, source * cols : (source + 1) * cols]
            weight_ref[n, :, m * cols : (m + 1) * cols] = block.astype(jnp.float32)
    for n, one in enumerate(vec_last):
        one.wait_recv()
        sum_all = sum_all + vec_near[n]
    total_ref[...] = sum_all
    copy.wait_sent()


def closing(grads, early, time, prev, delta, unit, settings, columns, tokens, upper, own_sums, middle_sums, channel_sums, cid):
    _, width, cols = time.shape
    rows = delta.shape[0] // 8
    half, side = cols, 3 * cols // 2
    early = early.reshape(4, 4, 128, 3 * cols)
    shape = jax.ShapeDtypeStruct
    wide = [pltpu.VMEM((2, 128, half), low)] * 2 + [pltpu.VMEM((4, 128, half), low)] * 2
    thin = [pltpu.VMEM((64, half), low)] * 2 + [pltpu.VMEM((128, half), low)] * 2
    early_wide = [pltpu.VMEM((2, 128, side), low)] * 2 + [pltpu.VMEM((4, 128, side), low)] * 2
    early_thin = [pltpu.VMEM((64, side), low)] * 2 + [pltpu.VMEM((128, side), low)] * 2
    early_sum = pltpu.VMEM((4, 128, side), low)
    return pl.pallas_call(
        closing_kernel,
        name="closing",
        out_shape=[
            shape((rows, width), low),
            shape((5, 16, width), jnp.float32),
            shape((16, 128), jnp.float32),
        ],
        in_specs=[VMEM] + [HBM] * 5 + [VMEM] * 2 + [HBM] * 2 + [VMEM] * 3,
        out_specs=[VMEM] * 3,
        scratch_shapes=[
            pltpu.VMEM((4, width, cols), low),
            pltpu.VMEM((4, width, cols), low),
            pltpu.VMEM(delta.shape, low),
            pltpu.VMEM(delta.shape, low),
            pltpu.VMEM(delta.shape, low),
            pltpu.VMEM(early.shape, low),
            pltpu.VMEM((2, 256, width), jnp.float32),
            pltpu.VMEM((8, rows, width), low),
            pltpu.VMEM((5, 2, 8, width), jnp.float32),
            pltpu.VMEM((4, 4, 128, half), low),
            pltpu.VMEM((4, 4, 128, half), low),
            pltpu.VMEM((4, 128, half), low),
            pltpu.VMEM((4, 128, half), low),
            pltpu.VMEM((128, 5 * cols), low),
            pltpu.VMEM((8, 16, 5 * cols), low),
            pltpu.VMEM((16, width), jnp.float32),
            *wide,
            *wide,
            *thin,
            *thin,
            *early_wide,
            *early_wide,
            *early_thin,
            *early_thin,
            early_sum,
            early_sum,
            pltpu.VMEM((15, 16, 128), jnp.float32),
            pltpu.VMEM((7, 16, 128), jnp.float32),
            pltpu.VMEM((16, 128), jnp.float32),
            pltpu.VMEM((2, 8, width), jnp.float32),
            *scatter_scratch(rows, width),
            pltpu.SemaphoreType.DMA((104,)),
            pltpu.SemaphoreType.DMA((104,)),
            pltpu.SemaphoreType.DMA((7,)),
        ],
        compiler_params=pltpu.CompilerParams(collective_id=cid, has_side_effects=True, vmem_limit_bytes=60 * 2**20),
    )(grads, early, time, prev, delta, unit, settings, columns, tokens, upper, own_sums, middle_sums, channel_sums)


def ending_kernel(x_ref, key_ref, value_ref, gate_ref, blocks, send, recv):
    _, member, near, near_devices, _, _ = group_and_line()
    greet(near_devices)
    copy = Copies(send, recv)
    given = [
        copy(x_ref.at[pl.ds(pl.multiple_of(at * 16, 16), 16)], blocks.at[member], d) for at, d in zip(near, near_devices)
    ]
    for one in given:
        one.start()
    blocks[member] = x_ref[pl.ds(pl.multiple_of(member * 16, 16), 16)]
    for one in given:
        one.wait_recv()
    wide, cols = key_ref.shape[1] // 8, gate_ref.shape[1] // 8
    for m in range(8):
        key_ref[:, m * wide : (m + 1) * wide] = blocks[m, :, :wide].astype(jnp.float32)
        value_ref[:, m * wide : (m + 1) * wide] = blocks[m, :, wide : 2 * wide].astype(jnp.float32)
        gate_ref[:, m * cols : (m + 1) * cols] = blocks[m, :, 2 * wide :].astype(jnp.float32)
    copy.wait_sent()


def ending(stripe, features, width, cid):
    rows = stripe.shape[0] // 8
    shape = jax.ShapeDtypeStruct
    return pl.pallas_call(
        ending_kernel,
        name="ending",
        out_shape=[shape((rows, n), jnp.float32) for n in (features, features, width)],
        in_specs=[VMEM],
        out_specs=[VMEM] * 3,
        scratch_shapes=[
            pltpu.VMEM((8, rows, stripe.shape[1]), low),
            pltpu.SemaphoreType.DMA((7,)),
            pltpu.SemaphoreType.DMA((7,)),
        ],
        compiler_params=pltpu.CompilerParams(collective_id=cid, has_side_effects=True, vmem_limit_bytes=32 * 2**20),
    )(stripe)


def body(tokens, time_weights, channel_key, channel_value, channel_gate, vectors, head_decay, lengths, cotangent):
    groups, span, width = tokens.shape
    features = channel_key.shape[1]
    local_rows = channel_key.shape[0]
    members = lax.axis_size(GROUP)
    member = lax.axis_index(GROUP)
    x_size, x_place = lax.axis_size("x"), lax.axis_index("x")
    heads = head_decay.shape[0] // members
    head_width = width // head_decay.shape[0]
    own = width // members
    own_features = features // members
    row_count = groups * span
    all_rows = members * row_count
    stripe = members * local_rows

    vector_rows = vectors.shape[0]
    vector_block = lax.dynamic_update_slice(jnp.zeros((16, stripe), low), vectors, (0, member * local_rows))
    recv, key, value, gate_pre, settings, time_full, first_prev, first_delta, first_unit, channel_part = opening(
        tokens.reshape(row_count, width), time_weights, channel_key, channel_value, channel_gate, vector_block, 1
    )
    time_full = time_full.reshape(5, width, own)
    own_settings = lax.dynamic_slice_in_dim(settings, member * own, own, axis=1)

    log_decay = jnp.log(lax.dynamic_slice_in_dim(head_decay, member * heads, heads))
    params = jnp.concatenate(
        [jnp.repeat(log_decay, head_width)[None], own_settings[6:9], jnp.zeros((4, own), jnp.float32)]
    )
    second, weights, wkv_scaled, wkv_inverse, incoming, hidden_one, gated_all, channel_full = recurrence(
        recv, key, value, gate_pre, params, tokens.reshape(row_count, width), settings, time_full, channel_part, 3
    )
    channel_full = channel_full.reshape(width, channel_part.shape[1])

    offsets = lax.axis_index(SEQ) * span + jnp.arange(span, dtype=jnp.int32)
    mask = (offsets[None, :] < lengths[:, None]).astype(jnp.float32).reshape(row_count, 1)
    layer_out, upstream, grad_second, channel_sums, channel_term = channel(
        second, hidden_one, cotangent.reshape(row_count, width), mask, channel_full, settings, 7
    )
    layer_out = layer_out.reshape(groups, span, width)
    channel_sum = lax.psum_scatter(channel_term, ROWS, scatter_dimension=0, tiled=True)
    upper, grad_proj, middle_sums, own_sums, early_term = middle(
        grad_second,
        hidden_one,
        upstream,
        settings,
        settings.T,
        params,
        gate_pre,
        wkv_scaled,
        wkv_inverse,
        recv,
        key,
        value,
        weights,
        incoming,
        time_full,
        first_prev,
        first_delta,
        gated_all,
        4,
    )
    token_grad, time_grads, vector_sum = closing(
        grad_proj,
        early_term,
        time_full,
        first_prev,
        first_delta,
        first_unit,
        settings,
        settings.T,
        tokens.reshape(row_count, width),
        upper,
        own_sums,
        middle_sums,
        channel_sums,
        9,
    )
    token_grad = token_grad.reshape(groups, span, width)
    channel_sum, vector_sum = lax.optimization_barrier((channel_sum, vector_sum))
    key_grad, value_grad, gate_grad = ending(channel_sum, features, width, 6)
    vector_sum = lax.dynamic_slice(vector_sum, (0, member * local_rows), (vector_rows, local_rows))
    return layer_out, token_grad, time_grads, key_grad, value_grad, gate_grad, vector_sum


def solution(mesh):
    batch, seq = mesh.devices.shape
    side = 4
    fine = Mesh(mesh.devices.reshape(batch, side, seq // (2 * side), 2), ALL)
    return jax.shard_map(
        body,
        mesh=fine,
        in_specs=(
            P("z", SEQ, None),
            P(None, ALL, None),
            P(ALL, None),
            P(ALL, None),
            P(ALL, None),
            P(None, ALL),
            P(),
            P("z"),
            P("z", SEQ, None),
        ),
        out_specs=(
            P("z", SEQ, None),
            P("z", SEQ, None),
            P(None, ALL, None),
            P(ALL, None),
            P(ALL, None),
            P(ALL, None),
            P(None, ALL),
        ),
        check_vma=False,
    )
```

```python
import jax
import jax.numpy as jnp
from jax import lax
from jax.experimental import pallas as pl
from jax.experimental.pallas import tpu as pltpu
from jax.sharding import Mesh, PartitionSpec as P

BLOCK_LEN = 64
epsilon = 1e-05
group_epsilon = 0.00064

GROUP = ("y", "core")
ROWS = ("z", "x")
SEQ = ("x", "y", "core")
ALL = ("z", "x", "y", "core")
low = jnp.bfloat16


MESH = pl.DeviceIdType.MESH
HBM = pl.BlockSpec(memory_space=pl.ANY)


def cost(microseconds):
    return pl.CostEstimate(flops=0, bytes_accessed=microseconds * 3_000_000, transcendentals=0)


VMEM = pl.BlockSpec(memory_space=pltpu.VMEM)


def greet(devices):
    barrier = pltpu.get_barrier_semaphore()
    for device in devices:
        pl.semaphore_signal(barrier, inc=1, device_id=device, device_id_type=MESH)
    pl.semaphore_wait(barrier, len(devices))

def ring_places():
    y, c = lax.axis_index("y"), lax.axis_index("core")
    right, left, far = lax.rem(y + 1, 4), lax.rem(y + 3, 4), lax.rem(y + 2, 4)
    return y, c, right, left, far

def cube_places():
    z, x, y, c = [lax.axis_index(name) for name in ("z", "x", "y", "core")]
    place, member = z * 4 + x, y * 2 + c
    far = [lax.rem(place + k, 16) for k in range(1, 16)]
    near = [lax.rem(member + k, 8) for k in range(1, 8)]
    return place, member, far, near, [{"z": p // 4, "x": lax.rem(p, 4)} for p in far], [{"y": p // 2, "core": lax.rem(p, 2)} for p in near]

def nn(left, right):
    return jnp.dot(left, right, preferred_element_type=jnp.float32)


def nt(left, right):
    return lax.dot_general(left, right, (((1,), (1,)), ((), ())), preferred_element_type=jnp.float32)


def tn(left, right):
    return lax.dot_general(left, right, (((0,), (0,)), ((), ())), preferred_element_type=jnp.float32)


def head_tables(log_row):
    width = log_row.shape[-1]
    place = lax.broadcasted_iota(jnp.int32, (BLOCK_LEN, width), 0)
    other = lax.rem(lax.broadcasted_iota(jnp.int32, (BLOCK_LEN, width), 1), BLOCK_LEN)
    gap = jnp.maximum(place - 1 - other, 0).astype(jnp.float32)
    mask = jnp.where(other < place, jnp.exp(gap * log_row), 0.0)
    eye = other == place
    enter = jnp.exp(place.astype(jnp.float32) * log_row)
    leave = jnp.exp((BLOCK_LEN - 1 - place).astype(jnp.float32) * log_row)
    tall = lax.broadcasted_iota(jnp.int32, (width, width), 0) // BLOCK_LEN
    wide = lax.broadcasted_iota(jnp.int32, (width, width), 1) // BLOCK_LEN
    return mask, eye, enter, leave, tall == wide


def expand(block, same):
    copies = block.shape[1] // BLOCK_LEN
    return jnp.where(same, jnp.concatenate([block] * copies, axis=0), jnp.zeros((), block.dtype))


def compress(square, same):
    kept = jnp.where(same, square, 0.0)
    return sum(kept[k * BLOCK_LEN : (k + 1) * BLOCK_LEN] for k in range(square.shape[0] // BLOCK_LEN))


def head_sum(values, same, factor=1.0):
    ones = jnp.where(same, factor, 0.0).astype(low)
    high = values.astype(low)
    rest = (values - high.astype(jnp.float32)).astype(low)
    return nn(high, ones) + nn(rest, ones)


def head_mean(values, same):
    return head_sum(values, same, 1.0 / BLOCK_LEN)


def block_rows(m, s):
    return pl.ds(pl.multiple_of(m * 2 * BLOCK_LEN + s * BLOCK_LEN, BLOCK_LEN), BLOCK_LEN)


def start_line(total, slots, send, recv):
    me = lax.axis_index("x")
    devices = [{"x": lax.rem(me + k, 4)} for k in range(1, 4)]
    slots[me] = total[...]
    copies = [
        pltpu.make_async_remote_copy(
            src_ref=total, dst_ref=slots.at[me], send_sem=send.at[k], recv_sem=recv.at[k], device_id=d, device_id_type=MESH
        )
        for k, d in enumerate(devices)
    ]
    for one in copies:
        one.start()
    return copies


def recurrence_kernel(
    r_hbm, k_hbm, v_hbm, g_hbm, p_ref, tok_hbm, set_hbm, time_hbm, stripe_hbm,
    second_ref, w_out, scaled_out, inverse_out, in_out, hidden_out, gated_ref, full_ref,
    r_ref, k_ref, v_ref, g_ref, tok_ref, set_ref, stripe_ref, w_ref, scaled_ref, inverse_ref, in_ref, hidden_ref, wkv, prefix, total, slots, gated, time, out, out_all, send, recv, local,
):
    loads = [
        pltpu.make_async_copy(source, target, local.at[8 + n])
        for n, (source, target) in enumerate(
            ((k_hbm, k_ref), (r_hbm, r_ref), (v_hbm, v_ref), (g_hbm, g_ref), (tok_hbm, tok_ref), (set_hbm, set_ref), (stripe_hbm, stripe_ref))
        )
    ]
    for one in loads:
        one.start()
    x, member, near, near_devices, _, _ = group_and_line()
    y, c, right, left, far = ring_places()
    z = lax.axis_index("z")
    greet(near_devices + [{"x": lax.rem(x + n, 4)} for n in range(1, 4)] + [{"z": lax.rem(z + n, 4)} for n in (1, 3)])
    copy = Copies(send, recv)
    loads.pop().wait()
    place = pltpu.make_async_copy(stripe_ref, full_ref.at[z, x], local.at[2])
    place.start()
    place.wait()
    side = stripe_hbm.shape[1] // 2
    one_side, other_side = pl.ds(0, side), pl.ds(side, side)
    z_first = Ring(copy, "z", lambda at, n: full_ref.at[at, x, pl.ds(n * 64, 64), one_side])
    x_first = Ring(copy, "x", lambda at, n: full_ref.at[z, at, pl.ds(n * 64, 64), other_side])
    load = pltpu.make_async_copy(time_hbm.at[4], time, local.at[0])
    load.start()
    for one in loads:
        one.wait()
    log_row, bonus, gain, bias = [p_ref[n : n + 1, :] for n in range(4)]
    mask, eye, enter, leave, same = head_tables(log_row)
    block_decay = jnp.exp(BLOCK_LEN * log_row)

    def first(m, states):
        after = []
        for s in range(2):
            rows = block_rows(m, s)
            r, k, v = r_ref[rows], k_ref[rows], v_ref[rows]
            key = expand(k, same)
            scores = nt(r, key)
            pairs = head_sum(r.astype(jnp.float32) * bonus * k.astype(jnp.float32), same)
            weights = (scores * mask + jnp.where(eye, pairs, 0.0)).astype(low)
            w_ref[rows] = weights
            wkv[rows] = nn(weights, expand(v, same))
            prefix[m * 2 + s] = states[s]
            key_leave = (k.astype(jnp.float32) * leave).astype(low)
            after.append(states[s] * block_decay + compress(tn(key_leave, v), same))
        return tuple(after)

    zero = jnp.zeros(enter.shape, jnp.float32)
    states = lax.fori_loop(0, 8, first, (zero, zero))
    z_first.forward()
    x_first.forward()
    for s in range(2):
        total[s] = states[s]
    line = start_line(total, slots, send.at[pl.ds(50, 3)], recv.at[pl.ds(50, 3)])
    for ring in (z_first, x_first):
        ring.wait_near()
        ring.wait_far()
    for one in line:
        one.wait()
    x_last = Ring(copy, "x", lambda at, n: full_ref.at[pl.ds(n * 2, 2), at, :, one_side])
    z_last = Ring(copy, "z", lambda at, n: full_ref.at[at, pl.ds(n * 2, 2), :, other_side])
    x_place = lax.axis_index("x")
    entering = [zero, zero]
    span_decay = jnp.exp(8.0 * BLOCK_LEN * log_row)
    for x in range(3):
        for s in range(2):
            entering[s] = jnp.where(x < x_place, entering[s] * span_decay + slots[x, s], entering[s])
    for s in range(2):
        total[s] = entering[s]

    def second(m, carry):
        power = jnp.exp((m * BLOCK_LEN).astype(jnp.float32) * log_row)
        for s in range(2):
            rows = block_rows(m, s)
            state = (prefix[m * 2 + s] + power * total[s]).astype(low)
            in_ref[m * 2 + s] = state
            recv_enter = (r_ref[rows].astype(jnp.float32) * enter).astype(low)
            out = wkv[rows] + nn(recv_enter, expand(state, same))
            center = out - head_mean(out, same)
            inverse = lax.rsqrt(head_mean(center * center, same) + group_epsilon)
            scaled = center * inverse
            scaled_ref[rows] = scaled
            inverse_ref[rows] = inverse
            gate = g_ref[rows]
            gated[member, rows] = ((scaled * gain + bias) * gate * jax.nn.sigmoid(gate)).astype(low)
        return carry

    half = gated.shape[1] // 2
    ring = Ring(copy, "y", lambda at, n: gated.at[at * 2 + c, pl.ds(n * half, half)], start=False)
    to_sibling = {"core": 1 - c}
    across = [copy(gated.at[member, pl.ds(n * half, half)], gated.at[member, pl.ds(n * half, half)], to_sibling) for n in range(2)]
    for n in range(2):
        lax.fori_loop(4 * n, 4 * n + 4, second, 0)
        ring.start(n)
        across[n].start()

    def pass_on(at):
        one = copy(gated.at[at * 2 + c], gated.at[at * 2 + c], to_sibling)
        one.start()
        return one

    outs = [
        pltpu.make_async_copy(source, target, local.at[3 + n])
        for n, (source, target) in enumerate(
            ((w_ref, w_out), (scaled_ref, scaled_out), (inverse_ref, inverse_out), (in_ref, in_out))
        )
    ]
    for one in outs:
        one.start()
    x_last.forward()
    z_last.forward()
    ring.forward()
    ring.wait_near()
    passed = [pass_on(right), pass_on(left)]
    load.wait()
    ring.wait_far()
    passed.append(pass_on(far))
    for one in across + passed:
        one.wait_recv()
    keep = pltpu.make_async_copy(gated, gated_ref, local.at[1])
    keep.start()

    cols = w_ref.shape[1]
    given = []

    def project(q):
        rows = pl.ds(pl.multiple_of(q * 256, 256), 256)
        value = sum(nn(gated[m, rows], time[m * cols : (m + 1) * cols]) for m in range(8)).astype(low)
        for b in range(2):
            out[q * 2 + b] = value[b * 128 : (b + 1) * 128]

    for at in (far, right, left, y):
        project(at)
        for turn in range(2):
            j = at * 2 + lax.rem(c + turn, 2)
            if at is y and turn == 0:
                continue
            given.append(copy(out.at[j], out_all.at[member], {"y": at, "core": lax.rem(c + turn, 2)}))
            given[-1].start()
    out_all[member] = out[member]
    for one in given:
        one.wait_recv()

    def norm_rows(t, carry):
        rows = pl.ds(pl.multiple_of(t * 16, 16), 16)
        added = jnp.concatenate([out_all[n, rows].astype(jnp.float32) for n in range(8)], axis=1)
        values = tok_ref[rows].astype(jnp.float32) + added
        hidden_ref[rows] = values
        center = values - jnp.mean(values, axis=-1, keepdims=True)
        inverse = lax.rsqrt(jnp.mean(center * center, axis=-1, keepdims=True) + epsilon)
        second_ref[rows] = (center * inverse * set_ref[9:10, :] + set_ref[10:11, :]).astype(low)
        return carry

    lax.fori_loop(0, 8, norm_rows, 0)
    outs.append(pltpu.make_async_copy(hidden_ref, hidden_out, local.at[7]))
    outs[-1].start()
    for last in (x_last, z_last):
        last.wait_near()
        last.wait_far()
    copy.wait_sent()
    keep.wait()
    for one in outs:
        one.wait()


def recurrence(r, k, v, g, params, tokens, settings, time, stripe, cid):
    rows, cols = r.shape
    own_rows, width = tokens.shape
    shape = jax.ShapeDtypeStruct
    return pl.pallas_call(
        recurrence_kernel,
        name="recurrence",
        cost_estimate=cost(55),
        out_shape=[
            shape((own_rows, width), low),
            shape((rows, cols), low),
            shape((rows, cols), jnp.float32),
            shape((rows, cols), jnp.float32),
            shape((16, BLOCK_LEN, cols), low),
            shape((own_rows, width), jnp.float32),
            shape((8, rows, cols), low),
            shape((4, 4) + stripe.shape, low),
        ],
        in_specs=[HBM] * 4 + [VMEM] + [HBM] * 4,
        out_specs=[VMEM] + [HBM] * 7,
        scratch_shapes=[
            pltpu.VMEM((rows, cols), low),
            pltpu.VMEM((rows, cols), low),
            pltpu.VMEM((rows, cols), low),
            pltpu.VMEM((rows, cols), jnp.float32),
            pltpu.VMEM((own_rows, width), low),
            pltpu.VMEM(settings.shape, jnp.float32),
            pltpu.VMEM(stripe.shape, low),
            pltpu.VMEM((rows, cols), low),
            pltpu.VMEM((rows, cols), jnp.float32),
            pltpu.VMEM((rows, cols), jnp.float32),
            pltpu.VMEM((16, BLOCK_LEN, cols), low),
            pltpu.VMEM((own_rows, width), jnp.float32),
            pltpu.VMEM((rows, cols), jnp.float32),
            pltpu.VMEM((16, BLOCK_LEN, cols), jnp.float32),
            pltpu.VMEM((2, BLOCK_LEN, cols), jnp.float32),
            pltpu.VMEM((4, 2, BLOCK_LEN, cols), jnp.float32),
            pltpu.VMEM((8, rows, cols), low),
            pltpu.VMEM((width, cols), low),
            pltpu.VMEM((8, own_rows, cols), low),
            pltpu.VMEM((8, own_rows, cols), low),
            pltpu.SemaphoreType.DMA((53,)),
            pltpu.SemaphoreType.DMA((53,)),
            pltpu.SemaphoreType.DMA((15,)),
        ],
        compiler_params=pltpu.CompilerParams(collective_id=cid, has_side_effects=True, vmem_limit_bytes=59 * 2**20),
    )(r, k, v, g, params, tokens, settings, time, stripe)


class Copies:
    def __init__(self, send, recv):
        self.send, self.recv, self.count, self.all = send, recv, 0, []

    def __call__(self, src, dst, device):
        one = pltpu.make_async_remote_copy(
            src_ref=src,
            dst_ref=dst,
            send_sem=self.send.at[self.count],
            recv_sem=self.recv.at[self.count],
            device_id=device,
            device_id_type=MESH,
        )
        self.count += 1
        self.all.append(one)
        return one

    def wait_sent(self, some=None):
        some = self.all if some is None else some
        for one in some:
            one.wait_send()
        self.all = [one for one in self.all if not any(one is other for other in some)]


class Ring:
    def __init__(self, copy, axis, part, start=True):
        me = lax.axis_index(axis)
        self.copy, self.part = copy, part
        self.right, self.left, self.far = [lax.rem(me + k, 4) for k in (1, 3, 2)]
        self.to_right, self.to_left = {axis: self.right}, {axis: self.left}
        own = [part(me, 0), part(me, 1)]
        self.near = [
            copy(own[0], own[0], self.to_right),
            copy(own[1], own[1], self.to_left),
            copy(own[1], own[1], self.to_right),
            copy(own[0], own[0], self.to_left),
        ]
        if start:
            for one in self.near:
                one.start()

    def start(self, half):
        for n in ((0, 3), (2, 1))[half]:
            self.near[n].start()

    def forward(self):
        self.near[0].wait_recv()
        there = self.part(self.left, 0)
        self.far_right = self.copy(there, there, self.to_right)
        self.far_right.start()
        self.near[1].wait_recv()
        there = self.part(self.right, 1)
        self.far_left = self.copy(there, there, self.to_left)
        self.far_left.start()

    def wait_near(self):
        self.near[2].wait_recv()
        self.near[3].wait_recv()

    def wait_far(self):
        self.far_right.wait_recv()
        self.far_left.wait_recv()


def opening_kernel(
    tok_ref, tw_ref, ck_ref, cv_ref, cg_ref, vec_ref,
    r_out, k_out, v_out, g_out, set_out, time_ref, prev_ref, delta_ref, unit_ref, stripe_ref,
    r_ref, k_ref, v_ref, g_ref, set_ref, tokens, time, mix, prev, delta, unit, vec_blocks, vec_stripe, vec_all, send, recv, local,
):
    place, member, far, near, far_devices, near_devices = cube_places()
    z, x, y, c = [lax.axis_index(name) for name in ("z", "x", "y", "core")]
    greet(far_devices + near_devices)
    copy = Copies(send, recv)
    own = tw_ref.shape[2] // 8
    wide = ck_ref.shape[1] // 8

    def lanes(p, size):
        return pl.ds(pl.multiple_of(p * size, size), size)

    def tile(p):
        return pl.ds(pl.multiple_of(p * 16, 16), 16)

    vec_near = [copy(vec_ref, vec_blocks.at[n], d) for n, d in enumerate(near_devices)]
    for one in vec_near:
        one.start()
    time_near = [
        copy(tw_ref.at[:, :, lanes(p, own)], time.at[:, z, x, tile(member), :], d) for p, d in zip(near, near_devices)
    ]
    for one in time_near:
        one.start()
    time_own = pltpu.make_async_copy(tw_ref.at[:, :, lanes(member, own)], time.at[:, z, x, tile(member), :], local.at[0])
    time_own.start()
    tokens[member] = tok_ref[...]
    gathered = Tokens(copy, tokens, member)
    to_next = {"x": lax.rem(x + 1, 4)}
    last_rows = [pl.ds(s * BLOCK_LEN + BLOCK_LEN - 16, 16) for s in range(2)]
    edges = [copy(tokens.at[7, rows], tokens.at[8, rows], to_next) for rows in last_rows]

    total = vec_ref[...].astype(jnp.float32)
    for n, one in enumerate(vec_near):
        one.wait_recv()
        total = total + vec_blocks[n].astype(jnp.float32)
    vec_stripe[...] = total.astype(low)
    vec_all[place] = vec_stripe[...]
    vec_far = [copy(vec_stripe, vec_all.at[place], d) for d in far_devices]
    for one in vec_far:
        one.start()

    for one in time_near:
        one.wait_recv()
    time_own.wait()
    one_side, other_side = pl.ds(0, own // 2), pl.ds(own // 2, own // 2)
    rows = time.shape[3] // 2
    z_first = Ring(copy, "z", lambda at, n: time.at[:, at, x, pl.ds(n * rows, rows), one_side])
    x_first = Ring(copy, "x", lambda at, n: time.at[:, z, at, pl.ds(n * rows, rows), other_side])
    gathered.ring.forward()
    z_first.forward()
    x_first.forward()
    z_first.wait_near()
    z_first.wait_far()
    x_last = Ring(copy, "x", lambda at, n: time.at[:, pl.ds(n * 2, 2), at, :, one_side])
    x_first.wait_near()
    x_first.wait_far()
    z_last = Ring(copy, "z", lambda at, n: time.at[:, at, pl.ds(n * 2, 2), :, other_side])
    for one in vec_far:
        one.wait_recv()
    for n in range(16):
        set_ref[:, n * 128 : (n + 1) * 128] = vec_all[n].astype(jnp.float32)
    gathered.wait_next()

    channel = []
    for source, size, start in ((ck_ref, wide, 0), (cv_ref, wide, wide), (cg_ref, own, 2 * wide)):
        for p, d in zip(near, near_devices):
            channel.append(copy(source.at[:, lanes(p, size)], stripe_ref.at[tile(member), pl.ds(start, size)], d))
    for one in channel:
        one.start()
    kept = [
        pltpu.make_async_copy(source.at[:, lanes(member, size)], stripe_ref.at[tile(member), pl.ds(start, size)], local.at[n])
        for n, (source, size, start) in enumerate(((ck_ref, wide, 0), (cv_ref, wide, wide), (cg_ref, own, 2 * wide)))
    ]
    for one in kept:
        one.start()

    width = tok_ref.shape[1]
    step = 512
    row = lax.broadcasted_iota(jnp.int32, (16, step), 0)

    def statistics(values):
        mean = jnp.mean(values, axis=-1, keepdims=True)
        center = values - mean
        return mean, lax.rsqrt(jnp.mean(center * center, axis=-1, keepdims=True) + epsilon)

    def mix_pair(q):
        @pl.when(q == 0)
        def _():
            for one in edges:
                one.wait_recv()

        def mix_block(b, carry):
            j = q * 2 + b
            before_slot = jnp.where(j == 0, 8, j - 1)
            hidden = jnp.logical_and(j == 0, x == 0)
            for s in range(2):
                last = slice(s * BLOCK_LEN + BLOCK_LEN - 16, (s + 1) * BLOCK_LEN)
                found = [statistics(tokens[before_slot, last].astype(jnp.float32))]
                found[0] = (found[0][0][15:16], found[0][1][15:16])
                for t in range(BLOCK_LEN // 16):
                    at = s * BLOCK_LEN + t * 16
                    found.append(statistics(tokens[j, at : at + 16].astype(jnp.float32)))

                def columns(n, carry):
                    cols = pl.ds(pl.multiple_of(n * step, step), step)
                    gain, offset = set_ref[0:1, cols], set_ref[1:2, cols]
                    before = tokens[before_slot, last, cols].astype(jnp.float32)[15:16]
                    before = (before - found[0][0]) * found[0][1] * gain + offset
                    before = jnp.where(hidden, 0.0, before)
                    for t in range(BLOCK_LEN // 16):
                        at = s * BLOCK_LEN + t * 16
                        mean, inverse = found[t + 1]
                        scaled = (tokens[j, at : at + 16, cols].astype(jnp.float32) - mean) * inverse
                        norm = scaled * gain + offset
                        moved = jnp.where(row == 0, before, pltpu.roll(norm, 1, 0))
                        before = norm[15:16]
                        gap = norm - moved
                        to = pl.ds(pl.multiple_of(j * 2 * BLOCK_LEN + at, 16), 16)
                        unit[to, cols] = scaled.astype(low)
                        prev[to, cols] = moved.astype(low)
                        delta[to, cols] = gap.astype(low)
                        for p in range(4):
                            mix[p, to, cols] = (moved + set_ref[2 + p : 3 + p, cols] * gap).astype(low)
                    return carry

                lax.fori_loop(0, width // step, columns, 0)
            return carry

        lax.fori_loop(0, 2, mix_block, 0)

    gathered.wait_passed()

    @pl.when(y != 1)
    def _():
        for one in edges:
            one.start()

    mix_pair(gathered.ring.right)
    x_last.forward()
    z_last.forward()
    mix_pair(y)
    gathered.far_pair()

    @pl.when(y == 1)
    def _():
        for one in edges:
            one.start()

    mix_pair(gathered.ring.far)
    mix_pair(gathered.ring.left)
    prev_out = pltpu.make_async_copy(prev, prev_ref, local.at[3])
    prev_out.start()
    delta_out = pltpu.make_async_copy(delta, delta_ref, local.at[4])
    delta_out.start()
    unit_out = pltpu.make_async_copy(unit, unit_ref, local.at[6])
    unit_out.start()
    for ring in (x_last, z_last):
        ring.wait_near()
        ring.wait_far()
    time_out = pltpu.make_async_copy(time, time_ref, local.at[5])
    time_out.start()

    def project(n, carry):
        to = pl.ds(pl.multiple_of(n * 256, 256), 256)
        for p, out in enumerate((r_ref, k_ref, v_ref, g_ref)):
            out[to] = nn(mix[p, to], time[p].reshape(16 * 128, own)).astype(out.dtype)
        return carry

    lax.fori_loop(0, 4, project, 0)
    results = [
        pltpu.make_async_copy(source, target, local.at[7 + n])
        for n, (source, target) in enumerate(
            ((r_ref, r_out), (k_ref, k_out), (v_ref, v_out), (g_ref, g_out), (set_ref, set_out))
        )
    ]
    for one in results:
        one.start()
    for one in channel:
        one.wait_recv()
    copy.wait_sent()
    for one in kept + results + [prev_out, delta_out, unit_out, time_out]:
        one.wait()


def opening(tokens, time_weights, channel_key, channel_value, channel_gate, vector_block, cid):
    rows, width = tokens.shape
    own = width // 8
    stripe = 2 * (channel_key.shape[1] // 8) + own
    shape = jax.ShapeDtypeStruct
    return pl.pallas_call(
        opening_kernel,
        name="opening",
        cost_estimate=cost(60),
        out_shape=[
            shape((8 * rows, own), low),
            shape((8 * rows, own), low),
            shape((8 * rows, own), low),
            shape((8 * rows, own), jnp.float32),
            shape((16, width), jnp.float32),
            shape((5, 4, 4, 128, own), low),
            shape((8 * rows, width), low),
            shape((8 * rows, width), low),
            shape((8 * rows, width), low),
            shape((128, stripe), low),
        ],
        in_specs=[VMEM] * 6,
        out_specs=[HBM] * 10,
        scratch_shapes=[
            pltpu.VMEM((8 * rows, own), low),
            pltpu.VMEM((8 * rows, own), low),
            pltpu.VMEM((8 * rows, own), low),
            pltpu.VMEM((8 * rows, own), jnp.float32),
            pltpu.VMEM((16, width), jnp.float32),
            pltpu.VMEM((9, rows, width), low),
            pltpu.VMEM((5, 4, 4, 128, own), low),
            pltpu.VMEM((4, 8 * rows, width), low),
            pltpu.VMEM((8 * rows, width), low),
            pltpu.VMEM((8 * rows, width), low),
            pltpu.VMEM((8 * rows, width), low),
            pltpu.VMEM((7, 16, 128), low),
            pltpu.VMEM((16, 128), low),
            pltpu.VMEM((16, 16, 128), low),
            pltpu.SemaphoreType.DMA((88,)),
            pltpu.SemaphoreType.DMA((88,)),
            pltpu.SemaphoreType.DMA((12,)),
        ],
        compiler_params=pltpu.CompilerParams(collective_id=cid, has_side_effects=True, vmem_limit_bytes=56 * 2**20),
    )(tokens, time_weights, channel_key, channel_value, channel_gate, vector_block)


class Scatter:
    def __init__(self, copy, p, out, from_sibling, mid, from_left, from_right, end_left, end_right):
        y, self.c, right, left, far = ring_places()
        self.order = (far, right, left, y)
        self.copy, self.p, self.out, self.from_sibling, self.mid = copy, p, out, from_sibling, mid
        self.from_left, self.from_right, self.end_left, self.end_right = from_left, from_right, end_left, end_right
        self.to_sibling, self.to_right, self.to_left = {"core": 1 - self.c}, {"y": right}, {"y": left}
        half = p.shape[1] // 2
        self.first, self.last = pl.ds(0, half), pl.ds(half, half)
        self.near = [None] * 4

    def send(self, src, dst, device):
        one = self.copy(src, dst, device)
        one.start()
        return one

    def share(self, k):
        self.near[k] = self.send(self.p.at[self.order[k] * 2 + 1 - self.c], self.from_sibling.at[k], self.to_sibling)

    def summed(self, k, rows):
        own = self.p[self.order[k] * 2 + self.c, rows].astype(jnp.float32)
        return own + self.from_sibling[k, rows].astype(jnp.float32)

    def far_out(self):
        self.near[0].wait_recv()
        self.mid[0] = self.summed(0, slice(None)).astype(low)
        self.far_right = self.send(self.mid.at[0, self.first], self.from_left, self.to_right)
        self.far_left = self.send(self.mid.at[0, self.last], self.from_right, self.to_left)

    def right_b(self):
        self.near[1].wait_recv()
        self.mid[1, self.last] = self.summed(1, self.last).astype(low)
        self.last_right = self.send(self.mid.at[1, self.last], self.end_left.at[self.last], self.to_right)

    def left_b(self):
        self.near[2].wait_recv()
        self.mid[2, self.first] = self.summed(2, self.first).astype(low)
        self.first_left = self.send(self.mid.at[2, self.first], self.end_right.at[self.first], self.to_left)

    def right_a(self):
        self.far_right.wait_recv()
        value = self.summed(1, self.first) + self.from_left[...].astype(jnp.float32)
        self.mid[1, self.first] = value.astype(low)
        self.first_right = self.send(self.mid.at[1, self.first], self.end_left.at[self.first], self.to_right)

    def left_a(self):
        self.far_left.wait_recv()
        value = self.summed(2, self.last) + self.from_right[...].astype(jnp.float32)
        self.mid[2, self.last] = value.astype(low)
        self.last_left = self.send(self.mid.at[2, self.last], self.end_right.at[self.last], self.to_left)

    def finish(self):
        self.near[3].wait_recv()
        self.last_right.wait_recv()
        self.first_left.wait_recv()
        self.first_right.wait_recv()
        self.last_left.wait_recv()
        from_ring = self.end_left[...].astype(jnp.float32) + self.end_right[...].astype(jnp.float32)
        self.out[...] = self.summed(3, slice(None)) + from_ring


def scatter_scratch(rows, cols):
    return [
        pltpu.VMEM((4, rows, cols), low),
        pltpu.VMEM((3, rows, cols), low),
        pltpu.VMEM((rows // 2, cols), low),
        pltpu.VMEM((rows // 2, cols), low),
        pltpu.VMEM((rows, cols), low),
        pltpu.VMEM((rows, cols), low),
    ]


def group_and_line():
    x = lax.axis_index("x")
    place, member, far, near, far_devices, near_devices = cube_places()
    return x, member, near, near_devices, {"x": lax.rem(x + 1, 4)}, {"x": lax.rem(x + 3, 4)}


class Tokens:
    def __init__(self, copy, slots, member):
        c = lax.axis_index("core")
        half = slots.shape[1] // 2
        self.copy, self.c, self.slots, self.to_sibling = copy, c, slots, {"core": 1 - c}
        self.ring = Ring(copy, "y", lambda at, n: slots.at[at * 2 + c, pl.ds(n * half, half)])
        self.near = copy(slots.at[member], slots.at[member], self.to_sibling)
        self.near.start()

    def pass_on(self, at):
        one = self.copy(self.slots.at[at * 2 + self.c], self.slots.at[at * 2 + self.c], self.to_sibling)
        one.start()
        return one

    def wait_next(self):
        self.ring.wait_near()
        self.passed = [self.pass_on(self.ring.right), self.pass_on(self.ring.left)]

    def wait_passed(self, near=True):
        if near:
            self.near.wait_recv()
        for one in self.passed:
            one.wait_recv()

    def next_pairs(self, near=True):
        self.ring.forward()
        self.wait_next()
        self.wait_passed(near)

    def far_pair(self):
        self.ring.wait_far()
        self.passed.append(self.pass_on(self.ring.far))
        self.passed[-1].wait_recv()

    def copies(self):
        return self.ring.near + [self.ring.far_right, self.ring.far_left, self.near] + self.passed


class Blend:
    def __init__(self, copy, terms, coefficients, delta, p, sums, firsts, to_previous):
        self.terms, self.coefficients, self.delta, self.p, self.sums, self.firsts = terms, coefficients, delta, p, sums, firsts
        self.edge = copy(firsts.at[0], firsts.at[4], to_previous)

    def pair(self, q):
        step = 512
        row = lax.broadcasted_iota(jnp.int32, (16, step), 0)
        for s in range(2):

            def columns(k, carry):
                lanes = pl.ds(pl.multiple_of(k * step, step), step)
                factors = [ref[n : n + 1, lanes] for ref, n in self.coefficients]
                added = [0.0] * len(factors)
                following = jnp.zeros((1, step), jnp.float32)
                for b in (1, 0):
                    for t in reversed(range(BLOCK_LEN // 16)):
                        at = s * BLOCK_LEN + t * 16
                        rows = slice(b * 2 * BLOCK_LEN + at, b * 2 * BLOCK_LEN + at + 16)
                        gap = self.delta[pl.ds(pl.multiple_of(q * 4 * BLOCK_LEN + b * 2 * BLOCK_LEN + at, 16), 16), lanes]
                        gap = gap.astype(jnp.float32)
                        here, whole = 0.0, 0.0
                        for n, factor in enumerate(factors):
                            term = self.terms[n, rows, lanes]
                            here = here + factor * term
                            whole = whole + term
                            product = gap * term
                            added[n] = added[n] + product[:8] + product[8:]
                        behind = whole - here
                        moved = jnp.where(row == 15, following, pltpu.roll(behind, 15, 0))
                        self.p[q * 2 + b, at : at + 16, lanes] = (here + moved).astype(low)
                        following = behind[0:1]
                for n, value in enumerate(added):
                    self.sums[n, :, lanes] += value
                self.firsts[q, s, 0:1, lanes] = following
                return carry

            lax.fori_loop(0, self.p.shape[2] // step, columns, 0)

        @pl.when(q == 0)
        def _():
            self.edge.start()

    def close(self, q):
        @pl.when(q == 3)
        def _():
            self.edge.wait_recv()

        row = lax.broadcasted_iota(jnp.int32, (16, self.p.shape[2]), 0)
        for s in range(2):
            following = self.firsts[q + 1, s, 0:1, :]
            following = jnp.where(jnp.logical_and(q == 3, lax.axis_index("x") == 3), 0.0, following)
            rows = slice(s * BLOCK_LEN + BLOCK_LEN - 16, (s + 1) * BLOCK_LEN)
            value = self.p[q * 2 + 1, rows].astype(jnp.float32)
            self.p[q * 2 + 1, rows] = (value + jnp.where(row == 15, following, 0.0)).astype(low)


def channel_kernel(
    own_hbm, hidden_hbm, cot_hbm, mask_ref, w_hbm, set_hbm,
    out_ref, up_ref, grad_ref, sums_ref, dw_ref,
    hidden_ref, cot_ref, set_ref, slots, w, ckey, cgate, delta, rect, hidden, gown, pre, gg, gg_own, gkey, terms, p, value, sums, firsts, dw,
    from_sibling, mid, from_left, from_right, end_left, end_right, send, recv, local,
):
    x, member, near, near_devices, to_next, to_previous = group_and_line()
    loads = [
        pltpu.make_async_copy(source, target, local.at[3 + n])
        for n, (source, target) in enumerate(
            ((own_hbm, slots.at[member]), (set_hbm, set_ref), (hidden_hbm, hidden_ref), (cot_hbm, cot_ref))
        )
    ]
    for one in loads:
        one.start()
    y, c, right, left, far = ring_places()
    firsts[0:4] = jnp.zeros_like(firsts[0:4])
    sums[...] = jnp.zeros_like(sums)
    greet(near_devices + [to_next, to_previous])
    copy = Copies(send, recv)
    load = pltpu.make_async_copy(w_hbm, w, local.at[0])
    load.start()
    for one in loads:
        one.wait()
    gathered = Tokens(copy, slots, member)
    wide = rect.shape[1]
    cols = gown.shape[2]
    step = 512
    row = lax.broadcasted_iota(jnp.int32, (16, step), 0)
    edges = [
        copy(slots.at[7, pl.ds(s * BLOCK_LEN + BLOCK_LEN - 16, 16)], slots.at[8, pl.ds(s * BLOCK_LEN + BLOCK_LEN - 16, 16)], to_next)
        for s in range(2)
    ]

    def compute(q):
        @pl.when(q == 0)
        def _():
            for one in edges:
                one.wait_recv()

        for b in range(2):
            j = q * 2 + b
            for s in range(2):
                before_slot = jnp.where(j == 0, 8, j - 1)
                last = slice(s * BLOCK_LEN + BLOCK_LEN - 16, (s + 1) * BLOCK_LEN)

                def columns(n, carry):
                    lanes = pl.ds(pl.multiple_of(n * step, step), step)
                    before = slots[before_slot, last, lanes].astype(jnp.float32)[15:16]
                    before = jnp.where(jnp.logical_and(j == 0, x == 0), 0.0, before)
                    for t in range(BLOCK_LEN // 16):
                        at = s * BLOCK_LEN + t * 16
                        values = slots[j, at : at + 16, lanes].astype(jnp.float32)
                        moved = jnp.where(row == 0, before, pltpu.roll(values, 1, 0))
                        before = values[15:16]
                        gap = values - moved
                        to = pl.ds(pl.multiple_of(j * 2 * BLOCK_LEN + at, 16), 16)
                        delta[to, lanes] = gap.astype(low)
                        ckey[to, lanes] = (moved + set_ref[11:12, lanes] * gap).astype(low)
                        cgate[to, lanes] = (moved + set_ref[12:13, lanes] * gap).astype(low)
                    return carry

                lax.fori_loop(0, w_hbm.shape[0] // step, columns, 0)
        rows = pl.ds(pl.multiple_of(q * 256, 256), 256)
        kept = jnp.maximum(nn(ckey[rows], w[:, :wide]), 0.0)
        rect[rows] = kept.astype(low)
        hidden[rows] = (kept * kept).astype(low)
        part = nt(hidden[rows], w[:, wide : 2 * wide]).astype(low)
        early = nn(cgate[rows], w[:, 2 * wide :]).astype(low)
        for b in range(2):
            p[q * 2 + b] = part[b * 128 : (b + 1) * 128]
            gown[q * 2 + b] = early[b * 128 : (b + 1) * 128]

    gates = []

    def give_gate(j):
        one = copy(gown.at[j], pre.at[member], {"y": j // 2, "core": lax.rem(j, 2)})
        one.start()
        gates.append(one)

    buffers = (from_sibling, mid, from_left, from_right, end_left, end_right)
    total = Scatter(copy, p, value, *buffers)
    gathered.next_pairs()

    @pl.when(y != 1)
    def _():
        for one in edges:
            one.start()

    load.wait()
    compute(right)
    total.share(1)
    compute(y)
    total.share(3)
    gathered.far_pair()

    @pl.when(y == 1)
    def _():
        for one in edges:
            one.start()

    copy.wait_sent(edges)
    for turn in range(2):
        give_gate(right * 2 + lax.rem(c + turn, 2))
    give_gate(y * 2 + 1 - c)
    compute(far)
    total.share(0)
    total.right_b()
    total.far_out()
    compute(left)
    copy.wait_sent(gathered.copies())
    total.share(2)
    total.left_b()
    for at in (left, far):
        for turn in range(2):
            give_gate(at * 2 + lax.rem(c + turn, 2))
    pre[member] = gown[member]
    total.right_a()
    total.left_a()
    total.finish()
    for one in gates:
        one.wait_recv()
    copy.wait_sent()

    def gate_block(n, carry):
        at = pl.ds(pl.multiple_of(n * cols, cols), cols)
        gate = jax.nn.sigmoid(pre[n].astype(jnp.float32))
        up = cot_ref[:, at].astype(jnp.float32) * mask_ref[...]
        up_ref[:, at] = up
        out_ref[:, at] = (hidden_ref[:, at] + gate * value[:, at]).astype(low)
        slots[member, :, at] = (up * gate).astype(low)
        gg_own[n] = (up * value[:, at] * gate * (1.0 - gate)).astype(low)
        return carry

    lax.fori_loop(0, 8, gate_block, 0)

    gates = [copy(gg_own.at[at], gg.at[member], d) for at, d in zip(near, near_devices)]
    for one in gates:
        one.start()
    gathered = Tokens(copy, slots, member)
    gg[member] = gg_own[member]
    blend = Blend(copy, terms, [(set_ref, 11), (set_ref, 12)], delta, p, sums, firsts, to_previous)

    def compute_back(q):
        rows = pl.ds(pl.multiple_of(q * 256, 256), 256)
        pair = pl.ds(q * 2, 2)
        grad_hidden = nn(slots[pair].reshape(256, slots.shape[2]), w[:, wide : 2 * wide])
        gkey[rows] = (2.0 * grad_hidden * rect[rows].astype(jnp.float32)).astype(low)
        terms[0] = nt(gkey[rows], w[:, :wide])
        terms[1] = nt(gg[pair].reshape(256, cols), w[:, 2 * wide :])
        blend.pair(q)

    total = Scatter(copy, p, grad_ref, *buffers)
    gathered.near.wait_recv()
    for one in gates:
        one.wait_recv()
    compute_back(y)
    gathered.next_pairs(False)
    compute_back(right)
    blend.close(y)
    total.share(3)
    compute_back(left)
    blend.close(left)
    total.share(2)
    gathered.far_pair()
    total.left_b()
    compute_back(far)
    blend.close(far)
    total.share(0)
    blend.close(right)
    total.share(1)
    total.far_out()
    total.right_b()

    def give(block, slot):
        at = pl.ds(pl.multiple_of(block * 256, 256), 256)
        return pltpu.make_async_copy(dw.at[slot], dw_ref.at[at], local.at[1 + slot])

    def weight_blocks(n, carry):
        for slot in range(2):
            block = n * 2 + slot
            at = pl.ds(pl.multiple_of(block * 256, 256), 256)

            @pl.when(n > 0)
            def _():
                give(block - 2, slot).wait()

            dw[slot, :, :wide] = tn(ckey[:, at], gkey[...]).astype(low)
            dw[slot, :, wide : 2 * wide] = tn(slots[0:8, :, at].reshape(8 * 128, 256), hidden[...]).astype(low)
            dw[slot, :, 2 * wide :] = tn(cgate[:, at], gg[...].reshape(8 * 128, cols)).astype(low)
            give(block, slot).start()
        return carry

    lax.fori_loop(0, 2, weight_blocks, 0)
    total.right_a()
    total.left_a()
    lax.fori_loop(2, 4, weight_blocks, 0)
    for n in range(2):
        sums_ref[n : n + 1, :] = jnp.sum(sums[n], axis=0, keepdims=True)
    sums_ref[2:8, :] = jnp.zeros((6, sums_ref.shape[1]), jnp.float32)
    total.finish()
    copy.wait_sent()
    for slot in range(2):
        give(6 + slot, slot).wait()


def channel(own, hidden_one, cotangent, mask, weights, settings, cid):
    rows, width = own.shape
    cols = width // 8
    wide = (weights.shape[1] - cols) // 2
    shape = jax.ShapeDtypeStruct
    big = pltpu.VMEM((8 * rows, width), low)
    mid = pltpu.VMEM((8 * rows, wide), low)
    small = pltpu.VMEM((8, rows, cols), low)
    return pl.pallas_call(
        channel_kernel,
        name="channel",
        cost_estimate=cost(120),
        out_shape=[
            shape((rows, width), low),
            shape((rows, width), jnp.float32),
            shape((rows, width), jnp.float32),
            shape((8, width), jnp.float32),
            shape(weights.shape, low),
        ],
        in_specs=[HBM] * 3 + [VMEM] + [HBM] * 2,
        out_specs=[VMEM] * 4 + [HBM],
        scratch_shapes=[
            pltpu.VMEM((rows, width), jnp.float32),
            pltpu.VMEM((rows, width), low),
            pltpu.VMEM(settings.shape, jnp.float32),
            pltpu.VMEM((9, rows, width), low),
            pltpu.VMEM(weights.shape, low),
            big,
            big,
            big,
            mid,
            mid,
            small,
            small,
            small,
            small,
            mid,
            pltpu.VMEM((2, 256, width), jnp.float32),
            pltpu.VMEM((8, rows, width), low),
            pltpu.VMEM((rows, width), jnp.float32),
            pltpu.VMEM((2, 8, width), jnp.float32),
            pltpu.VMEM((5, 2, 8, width), jnp.float32),
            pltpu.VMEM((2, 256, weights.shape[1]), low),
            *scatter_scratch(rows, width),
            pltpu.SemaphoreType.DMA((70,)),
            pltpu.SemaphoreType.DMA((70,)),
            pltpu.SemaphoreType.DMA((7,)),
        ],
        compiler_params=pltpu.CompilerParams(collective_id=cid, has_side_effects=True, vmem_limit_bytes=59 * 2**20),
    )(own, hidden_one, cotangent, mask, weights, settings)


def middle_kernel(
    second_ref, hidden_ref, up_ref, set_ref, column_ref, params_ref,
    g_ref, scaled_ref, inverse_ref, r_ref, k_ref, v_ref, w_ref, in_ref, time_hbm, prev_hbm, delta_hbm, gated_hbm,
    upper_ref, proj_ref, vec_ref, sums_ref, dw_ref,
    time, prev, delta, gated, out, out_all, p, gg, dw, norm_sums, part_k, part_v, suffix, total, slots, sums,
    from_sibling, mid, from_left, from_right, end_left, end_right, send, recv, local,
):
    x, member, near, near_devices, _, _ = group_and_line()
    y, c, right, left, far = ring_places()
    greet(near_devices + [{"x": lax.rem(x + n, 4)} for n in range(1, 4)])
    copy = Copies(send, recv)
    cols = g_ref.shape[1]
    loads = [
        pltpu.make_async_copy(src, dst, local.at[n])
        for n, (src, dst) in enumerate(
            ((time_hbm.at[3:5], time.at[1:3]), (time_hbm.at[0:1], time.at[0:1]), (gated_hbm, gated), (prev_hbm, prev), (delta_hbm, delta))
        )
    ]
    for one in loads:
        one.start()

    norm_sums[...] = jnp.zeros_like(norm_sums)

    def norm_rows(t, carry):
        rows = pl.ds(pl.multiple_of(t * 16, 16), 16)
        values = hidden_ref[rows]
        center = values - jnp.mean(values, axis=-1, keepdims=True)
        inverse = lax.rsqrt(jnp.mean(center * center, axis=-1, keepdims=True) + epsilon)
        unit = center * inverse
        grad = second_ref[rows]
        product = grad * unit
        norm_sums[0] += product[:8] + product[8:]
        norm_sums[1] += grad[:8] + grad[8:]
        inner = grad * set_ref[9:10, :]
        mean = jnp.mean(inner, axis=-1, keepdims=True)
        along = jnp.mean(inner * unit, axis=-1, keepdims=True)
        upper = up_ref[rows] + inverse * (inner - mean - unit * along)
        upper_ref[rows] = upper
        for n in range(8):
            out[n, rows] = upper[:, n * cols : (n + 1) * cols].astype(low)
        return carry

    lax.fori_loop(0, 8, norm_rows, 0)
    given = [copy(out.at[at], out_all.at[member], d) for at, d in zip(near, near_devices)]
    for one in given:
        one.start()
    out_all[member] = out[member]
    for n in range(2):
        vec_ref[n : n + 1, :] = jnp.sum(norm_sums[n], axis=0, keepdims=True)
    vec_ref[4:8, :] = jnp.zeros((4, vec_ref.shape[1]), jnp.float32)
    sums[...] = jnp.zeros_like(sums)
    for one in loads:
        one.wait()
    for one in given:
        one.wait_recv()

    def through(q):
        for b in range(2):
            m = q * 2 + b
            rows = pl.ds(pl.multiple_of(m * cols, cols), cols)
            p[m] = nt(out_all[...].reshape(8 * 128, cols), time[2, rows]).astype(low)

    def out_block(m, carry):
        rows = pl.ds(pl.multiple_of(m * cols, cols), cols)
        dw[rows, 2 * cols : 3 * cols] = tn(gated[m], out_all[...].reshape(8 * 128, cols)).astype(low)
        return carry

    total_gg = Scatter(copy, p, gg, from_sibling, mid, from_left, from_right, end_left, end_right)
    through(far)
    total_gg.share(0)
    through(right)
    total_gg.share(1)
    through(left)
    total_gg.share(2)
    total_gg.far_out()
    total_gg.right_b()
    total_gg.left_b()
    through(y)
    total_gg.share(3)
    lax.fori_loop(0, 4, out_block, 0)
    total_gg.right_a()
    total_gg.left_a()
    lax.fori_loop(4, 8, out_block, 0)
    total_gg.finish()

    log_row, bonus, gain, bias = [params_ref[n : n + 1, :] for n in range(4)]
    mask, eye, enter, leave, same = head_tables(log_row)
    block_decay = jnp.exp(BLOCK_LEN * log_row)
    ones = jnp.where(same, 1.0, 0.0).astype(low)

    def first(m, carry):
        for s in range(2):
            rows = block_rows(m, s)
            gate, grad, scaled = g_ref[rows], gg[rows], scaled_ref[rows]
            sigma = jax.nn.sigmoid(gate)
            grad_normed = grad * gate * sigma
            proj_ref[3, rows] = (grad * (scaled * gain + bias) * sigma * (1.0 + gate * (1.0 - sigma))).astype(low)
            inner = grad_normed * gain
            wide = inverse_ref[rows] * (inner - head_mean(inner, same) - scaled * head_mean(inner * scaled, same))
            grad_wkv = wide.astype(low)
            r, k, v = r_ref[rows], k_ref[rows], v_ref[rows]
            r_wide, k_wide = r.astype(jnp.float32), k.astype(jnp.float32)
            grad_weights = nt(grad_wkv, expand(v, same)).astype(low).astype(jnp.float32)
            masked = (grad_weights * mask).astype(low)
            own = nn(jnp.where(eye, grad_weights, 0.0).astype(low), ones)
            grad_r = nn(masked, expand(k, same)) + own * bonus * k_wide
            grad_r = grad_r + nt(grad_wkv, expand(in_ref[m * 2 + s], same)) * enter
            proj_ref[0, rows] = grad_r.astype(low)
            part_k[rows] = compress(tn(masked, r), same) + own * bonus * r_wide
            part_v[rows] = compress(tn(w_ref[rows], grad_wkv), same)
            suffix[m * 2 + s] = compress(tn((r_wide * enter).astype(low), grad_wkv), same)
            sums[0] += own * r_wide * k_wide
            sums[1] += grad_normed * scaled
            sums[2] += grad_normed
        return carry

    lax.fori_loop(0, 8, first, 0)

    def chain(n, states):
        m = 7 - n
        after = []
        for s in range(2):
            here = suffix[m * 2 + s]
            suffix[m * 2 + s] = states[s]
            after.append(states[s] * block_decay + here)
        return tuple(after)

    zero = jnp.zeros(enter.shape, jnp.float32)
    states = lax.fori_loop(0, 8, chain, (zero, zero))
    for s in range(2):
        total[s] = states[s]
    line = start_line(total, slots, send.at[pl.ds(40, 3)], recv.at[pl.ds(40, 3)])

    def gate_block(n, carry):
        rows = pl.ds(pl.multiple_of(n * cols, cols), cols)
        prev_block, delta_block = prev[:, rows].T, delta[:, rows].T
        column = column_ref[rows]
        for n, source in enumerate((0, 3)):
            by_delta = nn(delta_block, proj_ref[source])
            grads = nn(prev_block, proj_ref[source]) + column[:, 2 + source : 3 + source] * by_delta
            dw[rows, n * cols : (n + 1) * cols] = grads.astype(low)
            product = (time[n, rows].astype(jnp.float32) * by_delta).astype(low)
            vec_ref[2 + n : 3 + n, rows] = nt(jnp.ones((8, cols), low), product)[0:1]
        return carry

    lax.fori_loop(0, 8, gate_block, 0)
    give = pltpu.make_async_copy(dw, dw_ref, local.at[5])
    give.start()
    for one in line:
        one.wait()
    x_place = lax.axis_index("x")
    leaving = [zero, zero]
    span_decay = jnp.exp(8.0 * BLOCK_LEN * log_row)
    for x in (3, 2, 1):
        for s in range(2):
            leaving[s] = jnp.where(x > x_place, leaving[s] * span_decay + slots[x, s], leaving[s])
    for s in range(2):
        total[s] = leaving[s]

    def second(m, carry):
        power = jnp.exp(((7 - m) * BLOCK_LEN).astype(jnp.float32) * log_row)
        for s in range(2):
            rows = block_rows(m, s)
            state = expand((suffix[m * 2 + s] + power * total[s]).astype(low), same)
            key_leave = (k_ref[rows].astype(jnp.float32) * leave).astype(low)
            proj_ref[1, rows] = (part_k[rows] + nt(v_ref[rows], state) * leave).astype(low)
            proj_ref[2, rows] = (part_v[rows] + nn(key_leave, state)).astype(low)
        return carry

    lax.fori_loop(0, 8, second, 0)


    for n in range(3):
        sums_ref[n : n + 1, :] = jnp.sum(sums[n], axis=0, keepdims=True)
    sums_ref[3:8, :] = jnp.zeros((5, cols), jnp.float32)
    copy.wait_sent()
    give.wait()


def middle(second, hidden, up, settings, columns, params, g, scaled, inverse, r, k, v, w, states, time, prev, delta, gated, cid):
    rows, width = second.shape
    cols = g.shape[1]
    tall = pltpu.VMEM((8 * rows, cols), jnp.float32)
    shape = jax.ShapeDtypeStruct
    return pl.pallas_call(
        middle_kernel,
        name="middle",
        out_shape=[
            shape((rows, width), jnp.float32),
            shape((4, 8 * rows, cols), low),
            shape((8, width), jnp.float32),
            shape((8, cols), jnp.float32),
            shape((width, 3 * cols), low),
        ],
        in_specs=[VMEM] * 14 + [HBM] * 4,
        out_specs=[VMEM] * 4 + [HBM],
        scratch_shapes=[
            pltpu.VMEM((3, width, cols), low),
            pltpu.VMEM(prev.shape, low),
            pltpu.VMEM(delta.shape, low),
            pltpu.VMEM(gated.shape, low),
            pltpu.VMEM((8, rows, cols), low),
            pltpu.VMEM((8, rows, cols), low),
            pltpu.VMEM((8, 8 * rows, cols), low),
            tall,
            pltpu.VMEM((width, 3 * cols), low),
            pltpu.VMEM((2, 8, width), jnp.float32),
            tall,
            tall,
            pltpu.VMEM((16, BLOCK_LEN, cols), jnp.float32),
            pltpu.VMEM((2, BLOCK_LEN, cols), jnp.float32),
            pltpu.VMEM((4, 2, BLOCK_LEN, cols), jnp.float32),
            pltpu.VMEM((3, BLOCK_LEN, cols), jnp.float32),
            *scatter_scratch(8 * rows, cols),
            pltpu.SemaphoreType.DMA((43,)),
            pltpu.SemaphoreType.DMA((43,)),
            pltpu.SemaphoreType.DMA((6,)),
        ],
        compiler_params=pltpu.CompilerParams(collective_id=cid, has_side_effects=True, vmem_limit_bytes=58 * 2**20),
    )(second, hidden, up, settings, columns, params, g, scaled, inverse, r, k, v, w, states, time, prev, delta, gated)


class RingScatter:
    def __init__(self, copy, axis, part, halves, bufs):
        me = lax.axis_index(axis)
        right, left, self.far = [lax.rem(me + k, 4) for k in (1, 3, 2)]
        self.me, self.right, self.left, self.part, self.halves, self.copy = me, right, left, part, halves, copy
        self.to_right, self.to_left = {axis: right}, {axis: left}
        self.from_left, self.from_right, self.end_left, self.end_right = bufs

    def send(self, src, dst, device):
        one = self.copy(src, dst, device)
        one.start()
        return one

    def far_out(self):
        first, last = self.halves
        self.far_right = self.send(self.part(self.far).at[first], self.from_left, self.to_right)
        self.far_left = self.send(self.part(self.far).at[last], self.from_right, self.to_left)

    def near_out(self):
        first, last = self.halves
        self.last_right = self.send(self.part(self.right).at[last], self.end_left.at[last], self.to_right)
        self.first_left = self.send(self.part(self.left).at[first], self.end_right.at[first], self.to_left)

    def pass_on(self):
        first, last = self.halves
        self.far_right.wait_recv()
        here = self.part(self.right).at[first]
        here[...] = (here[...].astype(jnp.float32) + self.from_left[...].astype(jnp.float32)).astype(low)
        self.first_right = self.send(here, self.end_left.at[first], self.to_right)
        self.far_left.wait_recv()
        here = self.part(self.left).at[last]
        here[...] = (here[...].astype(jnp.float32) + self.from_right[...].astype(jnp.float32)).astype(low)
        self.last_left = self.send(here, self.end_right.at[last], self.to_left)

    def finish(self, out):
        for one in (self.last_right, self.first_left, self.first_right, self.last_left):
            one.wait_recv()
        value = self.part(self.me)[...].astype(jnp.float32) + self.end_left[...].astype(jnp.float32)
        out[...] = (value + self.end_right[...].astype(jnp.float32)).astype(low)


def closing_kernel(
    grad_ref, early_hbm, time_hbm, prev_hbm, delta_hbm, unit_hbm, set_ref, column_ref, tok_hbm, upper_hbm, own_ref, middle_ref, channel_ref,
    token_ref, weight_ref, total_ref,
    time, scaled, prev, delta, unit, early, terms, p, firsts, one_dw, other_dw, one_sum, other_sum, stripe, gathered, parts,
    one_a, one_b, one_c, one_d, other_a, other_b, other_c, other_d,
    one_e, one_f, one_g, one_h, other_e, other_f, other_g, other_h,
    early_a, early_b, early_c, early_d, early_e, early_f, early_g, early_h,
    early_i, early_j, early_k, early_l, early_m, early_n, early_o, early_p, early_one, early_other, vec_far, vec_near, vec_stripe, norm_sums,
    from_sibling, mid, from_left, from_right, end_left, end_right, send, recv, local,
):
    place, member, far_places, near_members, far_devices, near_devices = cube_places()
    x = lax.axis_index("x")
    y, c, right, left, far = ring_places()
    to_previous = {"x": lax.rem(x + 3, 4)}
    firsts[0:4] = jnp.zeros_like(firsts[0:4])
    greet(far_devices + near_devices)
    copy = Copies(send, recv)
    cols = grad_ref.shape[2]
    loads = [
        pltpu.make_async_copy(src, dst, local.at[n])
        for n, (src, dst) in enumerate(
            ((time_hbm.at[0:4], time), (early_hbm, early), (unit_hbm, unit), (prev_hbm, prev), (delta_hbm, delta))
        )
    ]
    for one in loads:
        one.start()
    slots = (pl.ds(0, 2), pl.ds(2, 2))
    halves = (pl.ds(0, 64), pl.ds(64, 64))
    side = early.shape[3] // 2
    parts[...] = jnp.zeros_like(parts)
    parts[2:3, :] = middle_ref[2:3, :]
    parts[5:6, :] = middle_ref[3:4, :]
    parts[6:9, pl.ds(pl.multiple_of(member * cols, cols), cols)] = own_ref[0:3, :]
    parts[9:11, :] = middle_ref[0:2, :]
    parts[11:13, :] = channel_ref[0:2, :]
    norm_sums[...] = jnp.zeros_like(norm_sums)
    loads[0].wait()
    loads[1].wait()
    early_z = RingScatter(copy, "z", lambda at: early.at[at, :, :, 0:side], slots, (early_a, early_b, early_c, early_d))
    early_x = RingScatter(
        copy, "x", lambda at: early.at[:, at, :, side : 2 * side], slots, (early_e, early_f, early_g, early_h)
    )
    for ring in (early_z, early_x):
        ring.far_out()
        ring.near_out()

    def scale_block(n, carry):
        rows = pl.ds(pl.multiple_of(n * 256, 256), 256)
        column = column_ref[rows]
        for k in range(4):
            scaled[k, rows] = (column[:, 2 + k : 3 + k] * time[k, rows].astype(jnp.float32)).astype(low)
        return carry

    lax.fori_loop(0, 8, scale_block, 0)
    for one in loads[2:]:
        one.wait()

    ones = jnp.ones((8, cols), low)

    def weight_block(at):
        def part(h, carry):
            block = at * 2 + h
            rows = pl.ds(pl.multiple_of(block * 256, 256), 256)
            prev_block, delta_block = prev[:, rows].T, delta[:, rows].T
            column = column_ref[rows]
            grads = []
            for n in (1, 2):
                by_delta = nn(delta_block, grad_ref[n])
                factor = column[:, 2 + n : 3 + n]
                grads.append((nn(prev_block, grad_ref[n]) + factor * by_delta).astype(low))
                weight = time[n, rows].astype(jnp.float32)
                parts[2 + n : 3 + n, rows] = nt(ones, (weight * by_delta).astype(low))[0:1]
            whole = jnp.concatenate(grads, axis=1)
            half = whole.shape[1] // 2
            for k in range(2):
                one_dw[at, h * 2 + k] = whole[k * 128 : (k + 1) * 128, :half]
                other_dw[at, h * 2 + k] = whole[k * 128 : (k + 1) * 128, half:]
            return carry

        lax.fori_loop(0, 2, part, 0)

    z_first = RingScatter(copy, "z", lambda at: one_dw.at[at], slots, (one_a, one_b, one_c, one_d))
    x_first = RingScatter(copy, "x", lambda at: other_dw.at[:, at], slots, (other_a, other_b, other_c, other_d))

    step = 512
    edge = copy(firsts.at[0], firsts.at[4], to_previous)

    def compute(q):
        rows = pl.ds(pl.multiple_of(q * 256, 256), 256)
        whole, here = 0.0, 0.0
        for n in range(4):
            whole = whole + nt(grad_ref[n, rows], time[n])
            here = here + nt(grad_ref[n, rows], scaled[n])
        terms[0] = here
        terms[1] = whole - here
        row = lax.broadcasted_iota(jnp.int32, (16, step), 0)
        for s in range(2):

            def columns(k, carry):
                lanes = pl.ds(pl.multiple_of(k * step, step), step)
                following = jnp.zeros((1, step), jnp.float32)
                added = [0.0, 0.0]
                for b in (1, 0):
                    for t in reversed(range(BLOCK_LEN // 16)):
                        at = s * BLOCK_LEN + t * 16
                        rows = slice(b * 2 * BLOCK_LEN + at, b * 2 * BLOCK_LEN + at + 16)
                        behind = terms[1, rows, lanes]
                        value = terms[0, rows, lanes] + jnp.where(row == 15, following, pltpu.roll(behind, 15, 0))
                        following = behind[0:1]
                        p[q * 2 + b, at : at + 16, lanes] = value.astype(low)
                        product = value * unit[
                            pl.ds(pl.multiple_of(q * 4 * BLOCK_LEN + b * 2 * BLOCK_LEN + at, 16), 16), lanes
                        ].astype(jnp.float32)
                        added = [added[0] + product[:8] + product[8:], added[1] + value[:8] + value[8:]]
                for n in range(2):
                    norm_sums[n, :, lanes] += added[n]
                firsts[q, s, 0:1, lanes] = following
                return carry

            lax.fori_loop(0, p.shape[2] // step, columns, 0)

        @pl.when(q == 0)
        def _():
            edge.start()

    def close(q):
        @pl.when(q == 3)
        def _():
            edge.wait_recv()

        row = lax.broadcasted_iota(jnp.int32, (16, p.shape[2]), 0)
        for s in range(2):
            following = firsts[q + 1, s, 0:1, :]
            following = jnp.where(jnp.logical_and(q == 3, x == 3), 0.0, following)
            rows = slice(s * BLOCK_LEN + BLOCK_LEN - 16, (s + 1) * BLOCK_LEN)
            value = p[q * 2 + 1, rows].astype(jnp.float32)
            p[q * 2 + 1, rows] = (value + jnp.where(row == 15, following, 0.0)).astype(low)
            last = pl.ds(pl.multiple_of(q * 4 * BLOCK_LEN + 2 * BLOCK_LEN + s * BLOCK_LEN + BLOCK_LEN - 16, 16), 16)
            norm_sums[0, 0:1, :] += following * unit[last].astype(jnp.float32)[15:16]
            norm_sums[1, 0:1, :] += following

    total = Scatter(copy, p, terms.at[1, pl.ds(0, p.shape[1])], from_sibling, mid, from_left, from_right, end_left, end_right)
    compute(left)
    compute(far)
    close(far)
    total.share(0)
    early_z.pass_on()
    early_x.pass_on()
    weight_block(z_first.far)
    z_first.far_out()
    total.far_out()
    weight_block(z_first.right)
    weight_block(z_first.left)
    z_first.near_out()
    weight_block(z_first.me)
    x_first.far_out()
    x_first.near_out()
    early_z.finish(early_one)
    early_x.finish(early_other)
    early_last_x = RingScatter(copy, "x", lambda at: early_one.at[at], halves, (early_i, early_j, early_k, early_l))
    early_last_z = RingScatter(copy, "z", lambda at: early_other.at[at], halves, (early_m, early_n, early_o, early_p))
    for ring in (early_last_x, early_last_z):
        ring.far_out()
        ring.near_out()
    compute(right)
    close(right)
    total.share(1)
    z_first.pass_on()
    x_first.pass_on()
    total.right_b()
    compute(y)
    rest = [
        pltpu.make_async_copy(upper_hbm, terms.at[0, pl.ds(0, p.shape[1])], local.at[5]),
        pltpu.make_async_copy(tok_hbm, delta.at[pl.ds(0, p.shape[1])], local.at[6]),
    ]
    for one in rest:
        one.start()
    close(left)
    total.share(2)
    close(y)
    total.share(3)
    total.left_b()
    total.right_a()
    total.left_a()
    early_last_x.pass_on()
    early_last_z.pass_on()
    for n in range(2):
        parts[n : n + 1, :] = jnp.sum(norm_sums[n], axis=0, keepdims=True)
    vec_first = [
        copy(parts.at[:, pl.ds(pl.multiple_of(at * 128, 128), 128)], vec_far.at[n], d)
        for n, (at, d) in enumerate(zip(far_places, far_devices))
    ]
    for one in vec_first:
        one.start()
    z_first.finish(one_sum)
    x_last = RingScatter(copy, "x", lambda at: one_sum.at[at], halves, (one_e, one_f, one_g, one_h))
    x_last.far_out()
    x_last.near_out()
    x_first.finish(other_sum)
    z_last = RingScatter(copy, "z", lambda at: other_sum.at[at], halves, (other_e, other_f, other_g, other_h))
    z_last.far_out()
    z_last.near_out()
    early_last_x.finish(stripe.at[:, 2 * cols : 2 * cols + side])
    early_last_z.finish(stripe.at[:, 2 * cols + side : 2 * cols + 2 * side])
    x_last.pass_on()
    z_last.pass_on()
    half = one_sum.shape[2]
    x_last.finish(stripe.at[:, 0:half])
    z_last.finish(stripe.at[:, half : 2 * half])
    given = [
        copy(stripe.at[pl.ds(pl.multiple_of(at * 16, 16), 16)], gathered.at[member], d)
        for at, d in zip(near_members, near_devices)
    ]
    for one in given:
        one.start()
    gathered[member] = stripe[pl.ds(pl.multiple_of(member * 16, 16), 16)]
    sum_all = parts[:, pl.ds(pl.multiple_of(place * 128, 128), 128)]
    for n, one in enumerate(vec_first):
        one.wait_recv()
        sum_all = sum_all + vec_far[n]
    vec_stripe[...] = sum_all
    vec_last = [copy(vec_stripe, vec_near.at[n], d) for n, d in enumerate(near_devices)]
    for one in vec_last:
        one.start()
    total.finish()

    def norm_rows(t, carry):
        rows = pl.ds(pl.multiple_of(t * 16, 16), 16)
        values = delta[rows].astype(jnp.float32)
        center = values - jnp.mean(values, axis=-1, keepdims=True)
        inverse = lax.rsqrt(jnp.mean(center * center, axis=-1, keepdims=True) + epsilon)
        scaled_row = center * inverse
        inner = terms[1, rows] * set_ref[0:1, :]
        mean = jnp.mean(inner, axis=-1, keepdims=True)
        along = jnp.mean(inner * scaled_row, axis=-1, keepdims=True)
        token_ref[rows] = (terms[0, rows] + inverse * (inner - mean - scaled_row * along)).astype(low)
        return carry

    for one in rest:
        one.wait()
    lax.fori_loop(0, 8, norm_rows, 0)
    for one in given:
        one.wait_recv()
    for m in range(8):
        for n, source in enumerate((2, 0, 1, 3, 4)):
            block = gathered[m, :, source * cols : (source + 1) * cols]
            weight_ref[n, :, m * cols : (m + 1) * cols] = block.astype(jnp.float32)
    for n, one in enumerate(vec_last):
        one.wait_recv()
        sum_all = sum_all + vec_near[n]
    total_ref[...] = sum_all
    copy.wait_sent()


def closing(grads, early, time, prev, delta, unit, settings, columns, tokens, upper, own_sums, middle_sums, channel_sums, cid):
    _, width, cols = time.shape
    rows = delta.shape[0] // 8
    half, side = cols, 3 * cols // 2
    early = early.reshape(4, 4, 128, 3 * cols)
    shape = jax.ShapeDtypeStruct
    wide = [pltpu.VMEM((2, 128, half), low)] * 2 + [pltpu.VMEM((4, 128, half), low)] * 2
    thin = [pltpu.VMEM((64, half), low)] * 2 + [pltpu.VMEM((128, half), low)] * 2
    early_wide = [pltpu.VMEM((2, 128, side), low)] * 2 + [pltpu.VMEM((4, 128, side), low)] * 2
    early_thin = [pltpu.VMEM((64, side), low)] * 2 + [pltpu.VMEM((128, side), low)] * 2
    early_sum = pltpu.VMEM((4, 128, side), low)
    return pl.pallas_call(
        closing_kernel,
        name="closing",
        out_shape=[
            shape((rows, width), low),
            shape((5, 16, width), jnp.float32),
            shape((16, 128), jnp.float32),
        ],
        in_specs=[VMEM] + [HBM] * 5 + [VMEM] * 2 + [HBM] * 2 + [VMEM] * 3,
        out_specs=[VMEM] * 3,
        scratch_shapes=[
            pltpu.VMEM((4, width, cols), low),
            pltpu.VMEM((4, width, cols), low),
            pltpu.VMEM(delta.shape, low),
            pltpu.VMEM(delta.shape, low),
            pltpu.VMEM(delta.shape, low),
            pltpu.VMEM(early.shape, low),
            pltpu.VMEM((2, 256, width), jnp.float32),
            pltpu.VMEM((8, rows, width), low),
            pltpu.VMEM((5, 2, 8, width), jnp.float32),
            pltpu.VMEM((4, 4, 128, half), low),
            pltpu.VMEM((4, 4, 128, half), low),
            pltpu.VMEM((4, 128, half), low),
            pltpu.VMEM((4, 128, half), low),
            pltpu.VMEM((128, 5 * cols), low),
            pltpu.VMEM((8, 16, 5 * cols), low),
            pltpu.VMEM((16, width), jnp.float32),
            *wide,
            *wide,
            *thin,
            *thin,
            *early_wide,
            *early_wide,
            *early_thin,
            *early_thin,
            early_sum,
            early_sum,
            pltpu.VMEM((15, 16, 128), jnp.float32),
            pltpu.VMEM((7, 16, 128), jnp.float32),
            pltpu.VMEM((16, 128), jnp.float32),
            pltpu.VMEM((2, 8, width), jnp.float32),
            *scatter_scratch(rows, width),
            pltpu.SemaphoreType.DMA((104,)),
            pltpu.SemaphoreType.DMA((104,)),
            pltpu.SemaphoreType.DMA((7,)),
        ],
        compiler_params=pltpu.CompilerParams(collective_id=cid, has_side_effects=True, vmem_limit_bytes=60 * 2**20),
    )(grads, early, time, prev, delta, unit, settings, columns, tokens, upper, own_sums, middle_sums, channel_sums)


def ending_kernel(x_ref, key_ref, value_ref, gate_ref, blocks, send, recv):
    _, member, near, near_devices, _, _ = group_and_line()
    greet(near_devices)
    copy = Copies(send, recv)
    given = [
        copy(x_ref.at[pl.ds(pl.multiple_of(at * 16, 16), 16)], blocks.at[member], d) for at, d in zip(near, near_devices)
    ]
    for one in given:
        one.start()
    blocks[member] = x_ref[pl.ds(pl.multiple_of(member * 16, 16), 16)]
    for one in given:
        one.wait_recv()
    wide, cols = key_ref.shape[1] // 8, gate_ref.shape[1] // 8
    for m in range(8):
        key_ref[:, m * wide : (m + 1) * wide] = blocks[m, :, :wide].astype(jnp.float32)
        value_ref[:, m * wide : (m + 1) * wide] = blocks[m, :, wide : 2 * wide].astype(jnp.float32)
        gate_ref[:, m * cols : (m + 1) * cols] = blocks[m, :, 2 * wide :].astype(jnp.float32)
    copy.wait_sent()


def ending(stripe, features, width, cid):
    rows = stripe.shape[0] // 8
    shape = jax.ShapeDtypeStruct
    return pl.pallas_call(
        ending_kernel,
        name="ending",
        out_shape=[shape((rows, n), jnp.float32) for n in (features, features, width)],
        in_specs=[VMEM],
        out_specs=[VMEM] * 3,
        scratch_shapes=[
            pltpu.VMEM((8, rows, stripe.shape[1]), low),
            pltpu.SemaphoreType.DMA((7,)),
            pltpu.SemaphoreType.DMA((7,)),
        ],
        compiler_params=pltpu.CompilerParams(collective_id=cid, has_side_effects=True, vmem_limit_bytes=32 * 2**20),
    )(stripe)


def body(tokens, time_weights, channel_key, channel_value, channel_gate, vectors, head_decay, lengths, cotangent):
    groups, span, width = tokens.shape
    features = channel_key.shape[1]
    local_rows = channel_key.shape[0]
    members = lax.axis_size(GROUP)
    member = lax.axis_index(GROUP)
    x_size, x_place = lax.axis_size("x"), lax.axis_index("x")
    heads = head_decay.shape[0] // members
    head_width = width // head_decay.shape[0]
    own = width // members
    own_features = features // members
    row_count = groups * span
    all_rows = members * row_count
    stripe = members * local_rows

    vector_rows = vectors.shape[0]
    mine = jnp.arange(stripe, dtype=jnp.int32)[None, :] // local_rows == member
    vector_block = jnp.where(mine, jnp.tile(vectors, (1, members)), jnp.zeros((), low))
    vector_block = jnp.pad(vector_block, ((0, 16 - vector_rows), (0, 0)))
    recv, key, value, gate_pre, settings, time_full, first_prev, first_delta, first_unit, channel_part = opening(
        tokens.reshape(row_count, width), time_weights, channel_key, channel_value, channel_gate, vector_block, 1
    )
    time_full = time_full.reshape(5, width, own)
    own_settings = lax.dynamic_slice_in_dim(settings, member * own, own, axis=1)

    log_decay = jnp.log(lax.dynamic_slice_in_dim(head_decay, member * heads, heads))
    params = jnp.concatenate(
        [jnp.repeat(log_decay, head_width)[None], own_settings[6:9], jnp.zeros((4, own), jnp.float32)]
    )
    second, weights, wkv_scaled, wkv_inverse, incoming, hidden_one, gated_all, channel_full = recurrence(
        recv, key, value, gate_pre, params, tokens.reshape(row_count, width), settings, time_full, channel_part, 3
    )
    channel_full = channel_full.reshape(width, channel_part.shape[1])

    row = jnp.arange(row_count, dtype=jnp.int32)[:, None]
    used = jnp.where(row < span, lengths[0], lengths[1])
    mask = (lax.axis_index(SEQ) * span + row % span < used).astype(jnp.float32)
    layer_out, upstream, grad_second, channel_sums, channel_term = channel(
        second, hidden_one, cotangent.reshape(row_count, width), mask, channel_full, settings, 7
    )
    layer_out = layer_out.reshape(groups, span, width)
    channel_sum = lax.psum_scatter(channel_term, ROWS, scatter_dimension=0, tiled=True)
    upper, grad_proj, middle_sums, own_sums, early_term = middle(
        grad_second,
        hidden_one,
        upstream,
        settings,
        settings.T,
        params,
        gate_pre,
        wkv_scaled,
        wkv_inverse,
        recv,
        key,
        value,
        weights,
        incoming,
        time_full,
        first_prev,
        first_delta,
        gated_all,
        4,
    )
    token_grad, time_grads, vector_sum = closing(
        grad_proj,
        early_term,
        time_full,
        first_prev,
        first_delta,
        first_unit,
        settings,
        settings.T,
        tokens.reshape(row_count, width),
        upper,
        own_sums,
        middle_sums,
        channel_sums,
        9,
    )
    token_grad = token_grad.reshape(groups, span, width)
    channel_sum, vector_sum = lax.optimization_barrier((channel_sum, vector_sum))
    key_grad, value_grad, gate_grad = ending(channel_sum, features, width, 6)
    vector_sum = lax.dynamic_slice(vector_sum, (0, member * local_rows), (vector_rows, local_rows))
    return layer_out, token_grad, time_grads, key_grad, value_grad, gate_grad, vector_sum


def solution(mesh):
    batch, seq = mesh.devices.shape
    side = 4
    fine = Mesh(mesh.devices.reshape(batch, side, seq // (2 * side), 2), ALL)
    return jax.shard_map(
        body,
        mesh=fine,
        in_specs=(
            P("z", SEQ, None),
            P(None, ALL, None),
            P(ALL, None),
            P(ALL, None),
            P(ALL, None),
            P(None, ALL),
            P(),
            P("z"),
            P("z", SEQ, None),
        ),
        out_specs=(
            P("z", SEQ, None),
            P("z", SEQ, None),
            P(None, ALL, None),
            P(ALL, None),
            P(ALL, None),
            P(ALL, None),
            P(None, ALL),
        ),
        check_vma=False,
    )
```
